32 devices in a mesh: band: 8 (over z, y), lon: 4 (over x, core).
Axes of the slice: x: 2, y: 2, z: 4, core: 2. Of those that a mesh axis runs over, the one named last changes fastest.
Arguments:
- node_state: bfloat16 [65536, 64], P(('band', 'lon')), may hold values from -6 to 6
- latent: bfloat16 [65536, 64], P(('band', 'lon')), may hold values from -6 to 6
- edge_attr: bfloat16 [2, 65536, 8, 64], P(None, ('band', 'lon')), may hold values from -6 to 6
- neighbours: int32 [2, 65536, 8], P(None, ('band', 'lon')), may hold values from 0 to 2559
- halo_lists: int32 [128, 128], P(('band', 'lon')), may hold values from 0 to 1023
- valid_counts: int32 [32], P(('band', 'lon')), may hold values from 1024 to 2048
- channel_mask: int32 [2, 64], replicated, may hold values 0 or 1
- edge_w1: bfloat16 [2, 192, 64], replicated, may hold values from -0.4375 to 0.4375
- edge_b1: float32 [2, 64], replicated, may hold values from -3 to 3
- edge_w2: bfloat16 [2, 64, 64], replicated, may hold values from -0.75 to 0.75
- edge_gain: float32 [2, 64], replicated, may hold values from 0.25 to 1.75
- edge_shift: float32 [2, 64], replicated, may hold values from -2 to 2
- node_w1: bfloat16 [2, 128, 64], replicated, may hold values from -0.5 to 0.5
- node_b1: float32 [2, 64], replicated, may hold values from -3 to 3
- node_w2: bfloat16 [2, 64, 64], replicated, may hold values from -0.75 to 0.75
- node_gain: float32 [2, 64], replicated, may hold values from 0.25 to 1.75
- node_shift: float32 [2, 64], replicated, may hold values from -2 to 2
- out_grad: bfloat16 [65536, 64], P(('band', 'lon')), may hold values from -6 to 6
Outputs:
- mesh_out: bfloat16 [65536, 64], P(('band', 'lon'))
- grad_state: float32 [65536, 64], P(('band', 'lon'))
- grad_latent: float32 [65536, 64], P(('band', 'lon'))
- grad_edge_w1: float32 [2, 192, 64], replicated
- grad_edge_b1: float32 [2, 64], replicated
- grad_edge_w2: float32 [2, 64, 64], replicated
- grad_edge_gain: float32 [2, 64], replicated
- grad_edge_shift: float32 [2, 64], replicated
- grad_node_w1: float32 [2, 128, 64], replicated
- grad_node_b1: float32 [2, 64], replicated
- grad_node_w2: float32 [2, 64, 64], replicated
- grad_node_gain: float32 [2, 64], replicated
- grad_node_shift: float32 [2, 64], replicated
The draws below stay inside these ranges and needn't reach their ends.
Inputs may be any that keep to these rules, and one draw needn't show every extreme that they name: `neighbours`: values below 2048 name this device's own rows; the next four blocks of 128 name the rows from the band below, the band above, the sector west and the sector east, in order. `halo_lists`: rows of the device itself, always below its live count.
All inputs are finite; a program needn't handle non-finite values.
Results may differ from the reference program's by a relative error of at most 0.012.
Values may be sent and summed in bfloat16 or wider, within the bound.
A program may use at most 128 MiB of HBM per device.

```python
import jax
import jax.numpy as jnp
from jax import lax

D = 64
DEGREE = 8
NODE_DEV = 2048
HALO = 128
NODES = 65536
N_BAND = 8
N_LON = 4
DEVICES = 32


def set_ends(drawn, rng, least, high):
    dims = drawn.shape
    index_at = [jax.random.randint(jax.random.fold_in(rng, axis), (), 0, dims[axis]) for axis in range(len(dims))]
    drawn = drawn.at[tuple(index_at)].set(least)
    longest = dims.index(max(dims))
    index_at[longest] = (index_at[longest] + 1) % dims[longest]
    return drawn.at[tuple(index_at)].set(high)


def levels(rng, dims, shards, low, high):
    level, own = 1.0, jax.random.fold_in(rng, 6)
    for dim, blocks in shards:
        heights = jnp.exp(jax.random.uniform(jax.random.fold_in(own, dim), (blocks,), jnp.float32, low / len(shards), high / len(shards)))
        level = level * jnp.repeat(heights, dims[dim] // blocks).reshape([-1 if axis == dim else 1 for axis in range(len(dims))])
    return level


def centred(rng, extent, scale, limit, shards=(), kind=jnp.bfloat16):
    level = levels(rng, extent, shards, -0.22, 0.18) if shards else 1.0
    entries = jax.random.normal(rng, extent, jnp.float32) * scale * level
    return jnp.minimum(jnp.maximum(entries, -limit), limit).astype(kind)


def setup_inputs(seed: int = 0) -> dict:
    arg_keys = jax.random.split(jax.random.key(seed), 19)
    node_state = centred(arg_keys[0], (NODES, D), 1.0, 6.0, ((0, 32),))
    latent = centred(arg_keys[1], (NODES, D), 1.0, 6.0, ((0, 32),))
    edge_attr = centred(arg_keys[2], (2, NODES, DEGREE, D), 1.0, 6.0, ((1, 32),))
    neighbours = set_ends(jax.random.randint(arg_keys[3], (2, NODES, DEGREE), 0, NODE_DEV + 4 * HALO), jax.random.fold_in(arg_keys[3], 1), 0, (NODE_DEV + 4 * HALO) - 1).astype(jnp.int32)
    halo_lists = set_ends(jax.random.randint(arg_keys[4], (4 * DEVICES, HALO), 0, NODE_DEV // 2), jax.random.fold_in(arg_keys[4], 1), 0, (NODE_DEV // 2) - 1).astype(jnp.int32)
    valid_counts = set_ends(jax.random.randint(arg_keys[5], (DEVICES,), NODE_DEV // 2, NODE_DEV + 1), jax.random.fold_in(arg_keys[5], 1), NODE_DEV // 2, NODE_DEV).astype(jnp.int32)
    channel_mask = set_ends((jax.random.randint(arg_keys[6], (2, D), 0, 4) < 3).astype(jnp.int32), jax.random.fold_in(arg_keys[6], 1), 0, 1)
    edge_w1 = centred(arg_keys[7], (2, 3 * D, D), (3 * D) ** -0.5, 0.4375)
    edge_b1 = centred(arg_keys[8], (2, D), 0.5, 3.0, (), jnp.float32)
    edge_w2 = centred(arg_keys[9], (2, D, D), D ** -0.5, 0.75)
    edge_gain = jnp.clip(1.0 + 0.15 * jax.random.normal(arg_keys[10], (2, D), jnp.float32), 0.25, 1.75)
    edge_shift = centred(arg_keys[11], (2, D), 0.3, 2.0, (), jnp.float32)
    node_w1 = centred(arg_keys[12], (2, 2 * D, D), (2 * D) ** -0.5, 0.5)
    node_b1 = centred(arg_keys[13], (2, D), 0.5, 3.0, (), jnp.float32)
    node_w2 = centred(arg_keys[14], (2, D, D), D ** -0.5, 0.75)
    node_gain = jnp.clip(1.0 + 0.15 * jax.random.normal(arg_keys[15], (2, D), jnp.float32), 0.25, 1.75)
    node_shift = centred(arg_keys[16], (2, D), 0.3, 2.0, (), jnp.float32)
    out_grad = centred(arg_keys[17], (NODES, D), 1.0, 6.0, ((0, 32),))
    return dict(node_state=node_state, latent=latent, edge_attr=edge_attr, neighbours=neighbours, halo_lists=halo_lists, valid_counts=valid_counts, channel_mask=channel_mask, edge_w1=edge_w1, edge_b1=edge_b1, edge_w2=edge_w2, edge_gain=edge_gain, edge_shift=edge_shift, node_w1=node_w1, node_b1=node_b1, node_w2=node_w2, node_gain=node_gain, node_shift=node_shift, out_grad=out_grad)


@jax.custom_vjp
def low(v):
    return lax.optimization_barrier(v.astype(jnp.bfloat16)).astype(jnp.float32)

@jax.custom_vjp
def low_back(v):
    return v

def low_keep(v):
    return (low(v), None)

def low_pass(kept, grad):
    return (grad,)

def back_keep(v):
    return (v, None)

def back_low(kept, grad):
    return (low(grad),)
low.defvjp(low_keep, low_pass)
low_back.defvjp(back_keep, back_low)

def layer_norm(values, gain, shift):
    center = values - lax.optimization_barrier(jnp.mean(values, axis=-1, keepdims=True))
    spread = lax.optimization_barrier(jnp.mean(center * center, axis=-1, keepdims=True))
    return center * lax.rsqrt(spread + 1e-05) * gain + shift

def matmul(left, right):
    return jnp.einsum('...c,cd->...d', left, right, precision=lax.Precision.HIGHEST)

def pick_rows(source, index):
    return jax.vmap(jax.vmap(lambda table, rows: table[rows]))(source, index)

def reference(node_state, latent, edge_attr, neighbours, halo_lists, valid_counts, channel_mask, edge_w1, edge_b1, edge_w2, edge_gain, edge_shift, node_w1, node_b1, node_w2, node_gain, node_shift, out_grad):
    shape_nodes = (N_BAND, N_LON, NODE_DEV, D)
    start = node_state.astype(jnp.float32).reshape(shape_nodes)
    top_latent = latent.astype(jnp.float32).reshape(shape_nodes)
    attribute = edge_attr.astype(jnp.float32).reshape(2, N_BAND, N_LON, NODE_DEV, DEGREE, D)
    neighbour = neighbours.reshape(2, N_BAND, N_LON, NODE_DEV, DEGREE).astype(jnp.int32)
    lists = halo_lists.reshape(N_BAND, N_LON, 4 * HALO).astype(jnp.int32)
    counts = valid_counts.reshape(N_BAND, N_LON)
    live = jnp.arange(NODE_DEV, dtype=jnp.int32)[None, None, :] < counts[:, :, None]
    valid = live.astype(jnp.float32)
    band_id = jnp.arange(N_BAND, dtype=jnp.int32)[None, :, None, None, None]
    sender_ok = jnp.where(neighbour < NODE_DEV, neighbour < counts[None, :, :, None, None], jnp.where(neighbour < NODE_DEV + HALO, band_id > 0, jnp.where(neighbour < NODE_DEV + 2 * HALO, band_id < N_BAND - 1, True)))
    edge_ok = (sender_ok & live[None, :, :, :, None]).astype(jnp.float32)
    chan = channel_mask.astype(jnp.float32)

    def one_layer(state, params, layer_at):
        first, bias_one, second, gain_e, shift_e, node_first, bias_three, node_second, gain_n, shift_n = params
        node_low = low(state)
        picked = pick_rows(node_low, lists).reshape(N_BAND, N_LON, 4, HALO, D)
        empty = jnp.zeros((1, N_LON, HALO, D), jnp.float32)
        south = jnp.concatenate([empty, picked[:-1, :, 1]], axis=0)
        north = jnp.concatenate([picked[1:, :, 0], empty], axis=0)
        west = jnp.roll(picked[:, :, 3], 1, axis=1)
        east = jnp.roll(picked[:, :, 2], -1, axis=1)
        table = jnp.concatenate([node_low, south, north, west, east], axis=2)
        sender_part = pick_rows(matmul(table, first[:D]), neighbour[layer_at].reshape(N_BAND, N_LON, NODE_DEV * DEGREE))
        sender_part = sender_part.reshape(N_BAND, N_LON, NODE_DEV, DEGREE, D)
        pre_one = low_back(sender_part + matmul(node_low, first[D:2 * D])[:, :, :, None, :] + matmul(attribute[layer_at], first[2 * D:]) + bias_one)
        act_one = low(jax.nn.silu(pre_one))
        pre_two = low_back(matmul(act_one, second))
        message = layer_norm(pre_two, gain_e, shift_e) * edge_ok[layer_at][..., None] * chan[layer_at]
        summed = low(lax.optimization_barrier(jnp.sum(message, axis=3)))
        pre_three = low_back(matmul(node_low, node_first[:D]) + matmul(summed, node_first[D:]) + bias_three)
        act_three = low(jax.nn.silu(pre_three))
        pre_four = low_back(matmul(act_three, node_second))
        return state + valid[..., None] * layer_norm(pre_four, gain_n, shift_n)

    def forward(state, lat, weights):
        middle = one_layer(state, tuple((w[0] for w in weights)), 0) + lat
        return one_layer(middle, tuple((w[1] for w in weights)), 1)
    weights = tuple((w.astype(jnp.float32) for w in (edge_w1, edge_b1, edge_w2, edge_gain, edge_shift, node_w1, node_b1, node_w2, node_gain, node_shift)))
    top, pull = jax.vjp(forward, start, top_latent, weights)
    grad_start, grad_lat, grad_weights = pull(out_grad.astype(jnp.float32).reshape(shape_nodes))
    mesh_out = top.reshape(N_BAND * N_LON * NODE_DEV, D).astype(jnp.bfloat16)
    flat = N_BAND * N_LON * NODE_DEV
    return (mesh_out, grad_start.reshape(flat, D), grad_lat.reshape(flat, D), grad_weights[0], grad_weights[1], grad_weights[2], grad_weights[3], grad_weights[4], grad_weights[5], grad_weights[6], grad_weights[7], grad_weights[8], grad_weights[9])
```

```python
import functools
import types

import jax
import jax.numpy as jnp
from jax import lax
from jax.experimental import pallas as pl
from jax.experimental.pallas import tpu as pltpu
from jax.sharding import PartitionSpec as P

F32 = jnp.float32
BF16 = jnp.bfloat16
MESH = pl.DeviceIdType.MESH
LISTED = 1024
TILE = 256
GROUP = 4
EB1, EGAIN, ESHIFT, NB1, NGAIN, NSHIFT, CMASK = range(7)


def dot(left, right):
    return jnp.dot(left, right, preferred_element_type=F32)


def dot_nt(left, right):
    return lax.dot_general(left, right, (((1,), (1,)), ((), ())), preferred_element_type=F32)


def exact_dot(left, right, dims):
    return lax.dot_general(
        left, right, (dims, ((), ())), precision=lax.Precision.HIGHEST, preferred_element_type=F32
    )


def eye(size, kind):
    row = lax.broadcasted_iota(jnp.int32, (size, size), 0)
    col = lax.broadcasted_iota(jnp.int32, (size, size), 1)
    return (row == col).astype(F32).astype(kind)


def turned(matrix):
    return dot_nt(eye(matrix.shape[1], BF16), matrix).astype(BF16)


def one_hot(row, total):
    width = row.shape[1]
    index = lax.broadcasted_iota(jnp.int16, (total, width), 0)
    return jnp.where(
        index == jnp.broadcast_to(row.astype(jnp.int16), (total, width)), BF16(1), BF16(0)
    )


def join(parts):
    return parts[0] if len(parts) == 1 else jnp.concatenate(parts, axis=1)


def mean0(values):
    return jnp.mean(values, axis=0, keepdims=True)


def gate(half):
    bend = jnp.tanh(half)
    act = half + half * bend
    return act, (1.0 + bend) + act * (1.0 - bend)


def fold(values):
    total = values[:, :128]
    for at in range(128, values.shape[1], 128):
        total = total + values[:, at : at + 128]
    return total


def kernel(names, bands, lons, *refs):
    k = types.SimpleNamespace(**dict(zip(names, refs)))
    band, lon = lax.axis_index("band"), lax.axis_index("lon")
    wide, nodes = k.state.shape
    degree = k.nbr.shape[1]
    halo = k.lists.shape[1]
    high = 4 * halo
    locals_ = nodes // high
    parts = locals_ + 1
    count = k.count[0]
    west, east = lax.rem(lon + lons - 1, lons), lax.rem(lon + 1, lons)
    has_low, has_high = band > 0, band < bands - 1

    for use in range(2):
        for way in range(2):
            k.halos[use, way] = jnp.zeros((wide, halo), BF16)
            k.backs[use, way] = jnp.zeros((wide, halo), BF16)
    barrier = pltpu.get_barrier_semaphore()

    def greet_band(step, carry):
        other = lax.rem(band + step, bands)
        pl.semaphore_signal(barrier, inc=1, device_id=(other, lon), device_id_type=MESH)
        return carry

    def greet_lon(step, carry):
        other = lax.rem(lon + step, lons)
        pl.semaphore_signal(barrier, inc=1, device_id=(band, other), device_id_type=MESH)
        return carry

    lax.fori_loop(1, bands, greet_band, 0)
    lax.fori_loop(1, lons, greet_lon, 0)

    def exchange(source, target, sends, recvs, use):
        def copy(block, landing, device):
            return pltpu.make_async_remote_copy(
                src_ref=source.at[use, block],
                dst_ref=target.at[use, landing],
                send_sem=sends.at[use, block],
                recv_sem=recvs.at[use, landing],
                device_id=device,
                device_id_type=MESH,
            )

        return copy

    turn = (1, 0, 3, 2)

    def targets():
        return ((band - 1, lon), (band + 1, lon), (band, west), (band, east))

    def start_exchange(copy):
        peers = targets()
        for block in range(4):
            go = copy(block, turn[block], peers[block]).start
            if block == 0:
                pl.when(has_low)(go)
            elif block == 1:
                pl.when(has_high)(go)
            else:
                go()

    def finish_exchange(copy):
        peers = targets()
        for block in range(4):
            def end(block=block):
                copy(block, block, peers[block]).wait()

            if block == 0:
                pl.when(has_low)(end)
            elif block == 1:
                pl.when(has_high)(end)
            else:
                end()

    for at, rows in enumerate((k.eb1, k.egain, k.eshift, k.nb1, k.ngain, k.nshift)):
        k.vrows[2 * at : 2 * at + 2, :] = rows[...]
    k.vrows[12:14, :] = k.cmask[...].astype(F32)
    k.vrows[14:16, :] = jnp.zeros((2, wide), F32)
    k.cols[...] = exact_dot(eye(wide, F32), k.vrows[...], ((1,), (1,)))

    def col(layer, which):
        at = 2 * which + layer
        return k.cols[:, at : at + 1]

    for way in range(4):
        k.owner[:, way * halo : (way + 1) * halo] = one_hot(k.lists[way : way + 1, :], LISTED)

    weights = []
    for layer in range(2):
        w1t = k.ew1t[layer]
        n1t = k.nw1t[layer]
        w2 = k.ew2[layer]
        n2 = k.nw2[layer]
        half = BF16(0.5)
        weights.append(
            dict(
                sender=w1t[:, :wide] * half,
                receiver=w1t[:, wide : 2 * wide] * half,
                attr=w1t[:, 2 * wide :] * half,
                second=turned(w2),
                node_one=n1t * half,
                node_two=turned(n2),
                sender_back=turned(w1t[:, :wide]),
                receiver_back=turned(w1t[:, wide : 2 * wide]),
                second_back=w2 * half,
                node_one_back=turned(n1t),
                node_two_back=n2 * half,
            )
        )
    for layer in range(2):
        for at, name in enumerate(
            (
                "sender", "receiver", "attr", "second", "node_two",
                "sender_back", "receiver_back", "second_back", "node_two_back",
            )
        ):
            k.small[layer, at] = weights[layer][name]
        k.wide_w[layer] = weights[layer]["node_one"]
        k.tall_w[layer] = weights[layer]["node_one_back"]
    SENDER, RECEIVER, ATTR, SECOND, NODE_TWO, SENDER_B, RECEIVER_B, SECOND_B, NODE_TWO_B = range(9)

    band_low_ok = has_low
    band_high_ok = has_high

    def tile_index(layer, at):
        lanes = pl.ds(pl.multiple_of(at * TILE, TILE), TILE)
        index = k.nbr[layer, :, lanes]
        place = lax.broadcasted_iota(jnp.int32, (1, TILE), 1) + at * TILE
        live = place < count
        return lanes, index, live

    def forward(layer):
        low = k.xs[layer, :wide, :]
        picked = dot(low[:, :LISTED], k.owner[...]).astype(BF16)
        for way in range(4):
            k.sends[layer, way] = picked[:, way * halo : (way + 1) * halo]
        copy = exchange(k.sends, k.halos, k.halo_send, k.halo_recv, layer)
        if layer == 0:
            pl.semaphore_wait(barrier, bands + lons - 2)
        start_exchange(copy)
        k.base[...] = dot(k.small[layer, RECEIVER], low) + 0.5 * col(layer, EB1)
        projected = dot(k.small[layer, SENDER], low).astype(BF16)
        for part in range(locals_):
            k.table[part * wide : (part + 1) * wide, :] = projected[
                :, part * high : (part + 1) * high
            ]
        finish_exchange(copy)
        for way in range(4):
            k.table[locals_ * wide :, way * halo : (way + 1) * halo] = dot(
                k.small[layer, SENDER], k.halos[layer, way]
            ).astype(BF16)

        def body(at, carry):
            lanes, index, live = tile_index(layer, at)
            sub, hi = index // high, index % high
            sender_ok = jnp.where(
                index < nodes,
                (index < count).astype(F32),
                jnp.where(
                    index < nodes + halo,
                    band_low_ok.astype(F32),
                    jnp.where(index < nodes + 2 * halo, band_high_ok.astype(F32), 1.0),
                ),
            )
            valid = live.astype(F32)
            edge_ok = sender_ok * valid
            base = k.base[:, lanes].reshape(wide // 8, 8, TILE)
            total = jnp.zeros((wide, TILE), F32)
            for first in range(0, degree, GROUP):
                slots = range(first, first + GROUP)
                hot = join([one_hot(hi[j : j + 1], high) for j in slots])
                found = dot(k.table[...], hot)
                for place, j in enumerate(slots):
                    piece = found[:, place * TILE : (place + 1) * TILE]
                    piece = piece.reshape(parts, wide // 8, 8, TILE)
                    which = jnp.broadcast_to(sub[j : j + 1], (8, TILE))
                    chosen = piece[0]
                    for part in range(1, parts):
                        chosen = jnp.where((which == part)[None], piece[part], chosen)
                    own = dot(k.small[layer, ATTR], k.attr[layer, j, :, lanes])
                    half = (chosen + base).reshape(wide, TILE) + own
                    act, slope = gate(half)
                    act = act.astype(BF16)
                    k.act[layer, j, :, lanes] = act
                    k.slope[layer, j, :, lanes] = slope.astype(BF16)
                    second = dot(k.small[layer, SECOND], act)
                    center = second - mean0(second)
                    rate = lax.rsqrt(mean0(center * center) + 1e-05) * edge_ok[j : j + 1]
                    k.rate_e[layer, j : j + 1, lanes] = rate
                    unit = center * rate
                    k.unit[layer, j, :, lanes] = unit.astype(BF16)
                    total = total + unit
            kept = jnp.sum(edge_ok, axis=0, keepdims=True)
            k.total[layer, :, lanes] = total
            k.kept[layer, :, lanes] = kept
            mask = col(layer, CMASK)
            summed = (mask * col(layer, EGAIN)) * total + (mask * col(layer, ESHIFT)) * kept
            k.xs[layer, wide:, lanes] = summed.astype(BF16)
            half = dot(k.wide_w[layer], k.xs[layer, :, lanes]) + 0.5 * col(layer, NB1)
            act, slope = gate(half)
            act = act.astype(BF16)
            k.act_n[layer, :, lanes] = act
            k.slope_n[layer, :, lanes] = slope.astype(BF16)
            fourth = dot(k.small[layer, NODE_TWO], act)
            center = fourth - mean0(fourth)
            rate = lax.rsqrt(mean0(center * center) + 1e-05)
            unit = center * rate
            k.rate_n[layer, :, lanes] = rate
            k.unit_n[layer, :, lanes] = unit
            change = valid * (unit * col(layer, NGAIN) + col(layer, NSHIFT))
            if layer == 0:
                middle = k.state[:, lanes].astype(F32) + change + k.latent[:, lanes].astype(F32)
                k.middle[:, lanes] = middle
                k.xs[1, :wide, lanes] = middle.astype(BF16)
            else:
                k.mesh_out[:, lanes] = (k.middle[:, lanes] + change).astype(BF16)
            return carry

        lax.fori_loop(0, nodes // TILE, body, 0)

    def backward(layer):
        into = k.grad_latent if layer == 1 else k.grad_state
        k.scatter[...] = jnp.zeros_like(k.scatter)
        k.sums[...] = jnp.zeros_like(k.sums)
        k.acc_64[...] = jnp.zeros_like(k.acc_64)
        k.acc_128[...] = jnp.zeros_like(k.acc_128)

        def body(at, carry):
            lanes, index, live = tile_index(layer, at)
            sub, hi = index // high, index % high
            valid = live.astype(F32)
            if layer == 1:
                grad = k.out_grad[:, lanes].astype(F32)
            else:
                grad = k.grad_latent[:, lanes]
            unit = k.unit_n[layer, :, lanes]
            grad_ok = valid * grad
            k.sums[NGAIN] += fold(grad_ok * unit)
            k.sums[NSHIFT] += fold(grad_ok)
            scaled = grad_ok * col(layer, NGAIN)
            fourth = k.rate_n[layer, :, lanes] * (
                scaled - mean0(scaled) - unit * mean0(scaled * unit)
            )
            fourth = fourth.astype(BF16)
            node_two = dot_nt(k.act_n[layer, :, lanes], fourth)
            third = dot(k.small[layer, NODE_TWO_B], fourth) * k.slope_n[layer, :, lanes].astype(F32)
            k.sums[NB1] += fold(third)
            third = third.astype(BF16)
            k.acc_128[...] += dot_nt(third, k.xs[layer, :, lanes])
            both = dot(k.tall_w[layer], third)
            state = grad + both[:wide]
            masked = both[wide:] * col(layer, CMASK)
            k.sums[EGAIN] += fold(masked * k.total[layer, :, lanes])
            k.sums[ESHIFT] += fold(masked * k.kept[layer, :, lanes])
            scaled = masked * col(layer, EGAIN)
            middle = scaled - mean0(scaled)
            first_sum = jnp.zeros((wide, TILE), F32)
            grad_two = jnp.zeros((wide, wide), F32)
            grad_attr = jnp.zeros((wide, wide), F32)
            for first in range(0, degree, GROUP):
                slots = range(first, first + GROUP)
                hots, spreads, seconds, firsts = [], [], [], []
                for j in slots:
                    unit = k.unit[layer, j, :, lanes].astype(F32)
                    second = (middle - unit * mean0(scaled * unit)) * k.rate_e[
                        layer, j : j + 1, lanes
                    ]
                    second = second.astype(BF16)
                    grad_one = dot(k.small[layer, SECOND_B], second) * k.slope[
                        layer, j, :, lanes
                    ].astype(F32)
                    first_sum = first_sum + grad_one
                    grad_one = grad_one.astype(BF16)
                    which = jnp.broadcast_to(sub[j : j + 1].astype(jnp.int16), (16, TILE))
                    rows = grad_one.reshape(wide // 16, 16, TILE)
                    spreads.append(
                        jnp.concatenate(
                            [
                                jnp.where((which == part)[None], rows, BF16(0)).reshape(wide, TILE)
                                for part in range(parts)
                            ],
                            axis=0,
                        )
                    )
                    hots.append(one_hot(hi[j : j + 1], high))
                    seconds.append(second)
                    firsts.append(grad_one)
                k.scatter[...] += dot_nt(join(spreads), join(hots))
                grad_two = grad_two + dot_nt(
                    join([k.act[layer, j, :, lanes] for j in slots]), join(seconds)
                )
                grad_attr = grad_attr + dot_nt(
                    join(firsts), join([k.attr[layer, j, :, lanes] for j in slots])
                )
            k.sums[EB1] += fold(first_sum)
            first_sum = first_sum.astype(BF16)
            k.acc_64[0] += dot_nt(first_sum, k.xs[layer, :wide, lanes])
            k.acc_64[1] += grad_attr
            k.acc_64[2] += grad_two
            k.acc_64[3] += node_two
            into[:, lanes] = state + dot(k.small[layer, RECEIVER_B], first_sum)
            return carry

        lax.fori_loop(0, nodes // TILE, body, 0)

        summed = k.scatter[...]
        coarse = summed.astype(BF16)
        fine = (summed - coarse.astype(F32)).astype(BF16)
        back = k.small[layer, SENDER_B]
        last = slice(locals_ * wide, parts * wide)
        to_owner = (dot(back, coarse[last]) + dot(back, fine[last])).astype(BF16)
        for way in range(4):
            k.gives[layer, way] = to_owner[:, way * halo : (way + 1) * halo]
        copy = exchange(k.gives, k.backs, k.back_send, k.back_recv, layer)
        start_exchange(copy)

        halo_rows = join([k.halos[layer, way] for way in range(4)])
        sender = dot_nt(coarse[last], halo_rows) + dot_nt(fine[last], halo_rows)
        for part in range(locals_):
            span = slice(part * wide, (part + 1) * wide)
            place = slice(part * high, (part + 1) * high)
            rows = k.xs[layer, :wide, place]
            sender = sender + dot_nt(coarse[span], rows) + dot_nt(fine[span], rows)
            into[:, place] += dot(back, coarse[span]) + dot(back, fine[span])
        lane = lax.broadcasted_iota(jnp.int32, (wide, wide), 1)
        vectors = jnp.zeros((wide, wide), F32)
        for which in range(6):
            vectors = jnp.where(
                lane == which, jnp.sum(k.sums[which], axis=1, keepdims=True), vectors
            )
        blocks = (
            join([sender, k.acc_64[0]]),
            join([k.acc_64[1], k.acc_64[2]]),
            k.acc_128[...],
            join([k.acc_64[3], vectors]),
        )
        rows = k.share.shape[2]
        for at, block in enumerate(blocks):
            for piece in range(wide // rows):
                k.share[layer, at * (wide // rows) + piece] = block[
                    piece * rows : (piece + 1) * rows, :
                ]

        finish_exchange(copy)
        returned = join([k.backs[layer, way] for way in range(4)])
        into[:, :LISTED] += dot_nt(returned, k.owner[...])

    def reduce_layer(layer):
        def band_copy(source, landing, sends, recvs, piece, slot, other):
            return pltpu.make_async_remote_copy(
                src_ref=source.at[layer, piece],
                dst_ref=landing.at[layer, slot],
                send_sem=sends.at[layer, other],
                recv_sem=recvs.at[layer, slot],
                device_id=(other, lon),
                device_id_type=MESH,
            )

        def scatter_start(step, carry):
            other = lax.rem(band + step, bands)
            band_copy(k.share, k.spread, k.rs_send, k.rs_recv, other, band, other).start()
            return carry

        def scatter_end(step, carry):
            other = lax.rem(band + step, bands)
            band_copy(k.share, k.spread, k.rs_send, k.rs_recv, other, other, other).wait()
            return carry

        lax.fori_loop(1, bands, scatter_start, 0)
        k.spread[layer, band] = k.share[layer, band]
        lax.fori_loop(1, bands, scatter_end, 0)
        k.swap[layer, lon] = jnp.sum(k.spread[layer], axis=0)

        def lon_copy(slot, other):
            return pltpu.make_async_remote_copy(
                src_ref=k.swap.at[layer, lon],
                dst_ref=k.swap.at[layer, slot],
                send_sem=k.sw_send.at[layer, other],
                recv_sem=k.sw_recv.at[layer, slot],
                device_id=(band, other),
                device_id_type=MESH,
            )

        def swap_start(step, carry):
            lon_copy(lon, lax.rem(lon + step, lons)).start()
            return carry

        def swap_end(step, carry):
            other = lax.rem(lon + step, lons)
            lon_copy(other, other).wait()
            return carry

        lax.fori_loop(1, lons, swap_start, 0)
        lax.fori_loop(1, lons, swap_end, 0)
        k.whole[layer, band] = jnp.sum(k.swap[layer], axis=0)

        def gather_start(step, carry):
            other = lax.rem(band + step, bands)
            band_copy(k.whole, k.whole, k.ag_send, k.ag_recv, band, band, other).start()
            return carry

        def gather_end(step, carry):
            other = lax.rem(band + step, bands)
            band_copy(k.whole, k.whole, k.ag_send, k.ag_recv, band, other, other).wait()
            return carry

        lax.fori_loop(1, bands, gather_start, 0)
        lax.fori_loop(1, bands, gather_end, 0)

        rows = k.share.shape[2]
        pieces = wide // rows
        blocks = []
        for at in range(4):
            block = [k.whole[layer, at * pieces + piece] for piece in range(pieces)]
            blocks.append(block[0] if pieces == 1 else jnp.concatenate(block, axis=0))
        k.g_ew1t[layer, :, : 2 * wide] = blocks[0]
        k.g_ew1t[layer, :, 2 * wide :] = blocks[1][:, :wide]
        k.g_ew2[layer] = blocks[1][:, wide:]
        k.g_nw1t[layer] = blocks[2]
        k.g_nw2[layer] = blocks[3][:, :wide]
        lines = exact_dot(blocks[3][:, wide:], eye(wide, F32), ((0,), (0,)))
        for which, out in enumerate(
            (k.g_eb1, k.g_egain, k.g_eshift, k.g_nb1, k.g_ngain, k.g_nshift)
        ):
            out[layer : layer + 1, :] = lines[which : which + 1, :]

    k.xs[0, :wide, :] = k.state[...]
    forward(0)
    forward(1)
    backward(1)
    backward(0)
    reduce_layer(1)
    reduce_layer(0)


INPUTS = (
    "state", "latent", "attr", "nbr", "lists", "count", "cmask", "ew1t", "eb1", "ew2",
    "egain", "eshift", "nw1t", "nb1", "nw2", "ngain", "nshift", "out_grad",
)
OUTPUTS = (
    "mesh_out", "grad_state", "grad_latent", "g_ew1t", "g_eb1", "g_ew2", "g_egain",
    "g_eshift", "g_nw1t", "g_nb1", "g_nw2", "g_ngain", "g_nshift",
)


def shards(bands, lons, *args):
    (
        node_state, latent, edge_attr, neighbours, halo_lists, valid_counts, channel_mask,
        edge_w1, edge_b1, edge_w2, edge_gain, edge_shift,
        node_w1, node_b1, node_w2, node_gain, node_shift, out_grad,
    ) = args
    nodes, wide = node_state.shape
    degree = neighbours.shape[2]
    halo = halo_lists.shape[1]
    high = 4 * halo
    parts = nodes // high + 1
    rows = max(8, 4 * wide // bands)
    while wide % rows:
        rows //= 2
    pieces = max(bands, 4 * wide // rows)
    shape = jax.ShapeDtypeStruct
    outs = (
        shape((wide, nodes), BF16),
        shape((wide, nodes), F32),
        shape((wide, nodes), F32),
        shape((2, wide, 3 * wide), F32),
        shape((2, wide), F32),
        shape((2, wide, wide), F32),
        shape((2, wide), F32),
        shape((2, wide), F32),
        shape((2, wide, 2 * wide), F32),
        shape((2, wide), F32),
        shape((2, wide, wide), F32),
        shape((2, wide), F32),
        shape((2, wide), F32),
    )
    sem = pltpu.SemaphoreType.DMA
    scratch = dict(
        halos=pltpu.VMEM((2, 4, wide, halo), BF16),
        backs=pltpu.VMEM((2, 4, wide, halo), BF16),
        sends=pltpu.VMEM((2, 4, wide, halo), BF16),
        gives=pltpu.VMEM((2, 4, wide, halo), BF16),
        share=pltpu.VMEM((2, pieces, rows, 128), F32),
        spread=pltpu.VMEM((2, bands, rows, 128), F32),
        swap=pltpu.VMEM((2, lons, rows, 128), F32),
        whole=pltpu.VMEM((2, pieces, rows, 128), F32),
        vrows=pltpu.VMEM((16, wide), F32),
        cols=pltpu.VMEM((wide, 16), F32),
        owner=pltpu.VMEM((LISTED, high), BF16),
        small=pltpu.VMEM((2, 9, wide, wide), BF16),
        wide_w=pltpu.VMEM((2, wide, 2 * wide), BF16),
        tall_w=pltpu.VMEM((2, 2 * wide, wide), BF16),
        xs=pltpu.VMEM((2, 2 * wide, nodes), BF16),
        base=pltpu.VMEM((wide, nodes), F32),
        table=pltpu.VMEM((parts * wide, high), BF16),
        act=pltpu.VMEM((2, degree, wide, nodes), BF16),
        slope=pltpu.VMEM((2, degree, wide, nodes), BF16),
        unit=pltpu.VMEM((2, degree, wide, nodes), BF16),
        rate_e=pltpu.VMEM((2, degree, nodes), F32),
        total=pltpu.VMEM((2, wide, nodes), F32),
        kept=pltpu.VMEM((2, 1, nodes), F32),
        act_n=pltpu.VMEM((2, wide, nodes), BF16),
        slope_n=pltpu.VMEM((2, wide, nodes), BF16),
        rate_n=pltpu.VMEM((2, 1, nodes), F32),
        unit_n=pltpu.VMEM((2, wide, nodes), F32),
        middle=pltpu.VMEM((wide, nodes), F32),
        scatter=pltpu.VMEM((parts * wide, high), F32),
        sums=pltpu.VMEM((6, wide, 128), F32),
        acc_64=pltpu.VMEM((4, wide, wide), F32),
        acc_128=pltpu.VMEM((wide, 2 * wide), F32),
        halo_send=sem((2, 4)),
        halo_recv=sem((2, 4)),
        back_send=sem((2, 4)),
        back_recv=sem((2, 4)),
        rs_send=sem((2, bands)),
        rs_recv=sem((2, bands)),
        sw_send=sem((2, lons)),
        sw_recv=sem((2, lons)),
        ag_send=sem((2, bands)),
        ag_recv=sem((2, bands)),
    )
    vmem = pl.BlockSpec(memory_space=pltpu.VMEM)
    specs = [vmem] * len(INPUTS)
    specs[INPUTS.index("count")] = pl.BlockSpec(memory_space=pltpu.SMEM)
    names = INPUTS + OUTPUTS + tuple(scratch)
    result = pl.pallas_call(
        functools.partial(kernel, names, bands, lons),
        out_shape=outs,
        in_specs=specs,
        out_specs=(vmem,) * len(OUTPUTS),
        scratch_shapes=list(scratch.values()),
        compiler_params=pltpu.CompilerParams(
            collective_id=0, has_side_effects=True, vmem_limit_bytes=60 * 2**20
        ),
        name="layers",
    )(
        node_state.T,
        latent.T,
        edge_attr.transpose(0, 2, 3, 1),
        neighbours.transpose(0, 2, 1),
        halo_lists,
        valid_counts,
        channel_mask,
        edge_w1.transpose(0, 2, 1),
        edge_b1,
        edge_w2,
        edge_gain,
        edge_shift,
        node_w1.transpose(0, 2, 1),
        node_b1,
        node_w2,
        node_gain,
        node_shift,
        out_grad.T,
    )
    result = list(result)
    for at in range(3):
        result[at] = result[at].T
    for at in (3, 8):
        result[at] = result[at].transpose(0, 2, 1)
    return tuple(result)


def solution(mesh):
    nodes = P(("band", "lon"), None)
    whole = P()
    in_specs = (
        nodes,
        nodes,
        P(None, ("band", "lon"), None, None),
        P(None, ("band", "lon"), None),
        nodes,
        P(("band", "lon")),
    ) + (whole,) * 11 + (nodes,)
    return jax.shard_map(
        functools.partial(shards, mesh.shape["band"], mesh.shape["lon"]),
        mesh=mesh,
        in_specs=in_specs,
        out_specs=(nodes,) * 3 + (whole,) * 10,
        check_vma=False,
    )
```

```python
import functools
import types

import jax
import jax.numpy as jnp
from jax import lax
from jax.experimental import pallas as pl
from jax.experimental.pallas import tpu as pltpu
from jax.sharding import PartitionSpec as P

F32 = jnp.float32
BF16 = jnp.bfloat16
MESH = pl.DeviceIdType.MESH
LISTED = 1024
TILE = 256
GROUP = 4
CHUNK = 256
EB1, EGAIN, ESHIFT, NB1, NGAIN, NSHIFT, CMASK = range(7)


def dot(left, right):
    return jnp.dot(left, right, preferred_element_type=F32)


def dot_nt(left, right):
    return lax.dot_general(left, right, (((1,), (1,)), ((), ())), preferred_element_type=F32)


def exact_dot(left, right, dims):
    return lax.dot_general(
        left, right, (dims, ((), ())), precision=lax.Precision.HIGHEST, preferred_element_type=F32
    )


def eye(size, kind):
    row = lax.broadcasted_iota(jnp.int32, (size, size), 0)
    col = lax.broadcasted_iota(jnp.int32, (size, size), 1)
    return (row == col).astype(F32).astype(kind)


def turned(matrix):
    return dot_nt(eye(matrix.shape[1], BF16), matrix).astype(BF16)


def one_hot(row, total):
    width = row.shape[1]
    index = lax.broadcasted_iota(jnp.int16, (total, width), 0)
    return jnp.where(
        index == jnp.broadcast_to(row.astype(jnp.int16), (total, width)), BF16(1), BF16(0)
    )


def join(parts):
    return parts[0] if len(parts) == 1 else jnp.concatenate(parts, axis=1)


def mean0(values):
    return jnp.mean(values, axis=0, keepdims=True)


def gate(half):
    bend = jnp.tanh(half)
    act = half + half * bend
    return act, (1.0 + bend) + act * (1.0 - bend)


def fold(values):
    total = values[:, :128]
    for at in range(128, values.shape[1], 128):
        total = total + values[:, at : at + 128]
    return total


def kernel(names, bands, lons, *refs):
    k = types.SimpleNamespace(**dict(zip(names, refs)))
    band, lon = lax.axis_index("band"), lax.axis_index("lon")
    wide, nodes = k.state.shape
    degree = k.nbr.shape[1]
    halo = k.lists.shape[1]
    high = 4 * halo
    shift = high.bit_length() - 1
    locals_ = nodes // high
    parts = locals_ + 1
    count = k.count[0]
    west, east = lax.rem(lon + lons - 1, lons), lax.rem(lon + 1, lons)
    has_low, has_high = band > 0, band < bands - 1

    for use in range(2):
        for way in range(2):
            k.halos[use, way] = jnp.zeros((wide, halo), BF16)
            k.backs[use, way] = jnp.zeros((wide, halo), BF16)
    barrier = pltpu.get_barrier_semaphore()

    def greet_band(step, carry):
        other = lax.rem(band + step, bands)
        pl.semaphore_signal(barrier, inc=1, device_id=(other, lon), device_id_type=MESH)
        return carry

    def greet_lon(step, carry):
        other = lax.rem(lon + step, lons)
        pl.semaphore_signal(barrier, inc=1, device_id=(band, other), device_id_type=MESH)
        return carry

    lax.fori_loop(1, bands, greet_band, 0)
    lax.fori_loop(1, lons, greet_lon, 0)

    def exchange(source, target, sends, recvs, use):
        def copy(block, landing, device):
            return pltpu.make_async_remote_copy(
                src_ref=source.at[use, block],
                dst_ref=target.at[use, landing],
                send_sem=sends.at[use, block],
                recv_sem=recvs.at[use, landing],
                device_id=device,
                device_id_type=MESH,
            )

        return copy

    turn = (1, 0, 3, 2)

    def targets():
        return ((band - 1, lon), (band + 1, lon), (band, west), (band, east))

    def start_exchange(copy):
        peers = targets()
        for block in range(4):
            go = copy(block, turn[block], peers[block]).start
            if block == 0:
                pl.when(has_low)(go)
            elif block == 1:
                pl.when(has_high)(go)
            else:
                go()

    def finish_exchange(copy):
        peers = targets()
        for block in range(4):
            def end(block=block):
                copy(block, block, peers[block]).wait()

            if block == 0:
                pl.when(has_low)(end)
            elif block == 1:
                pl.when(has_high)(end)
            else:
                end()

    for at, rows in enumerate((k.eb1, k.egain, k.eshift, k.nb1, k.ngain, k.nshift)):
        k.vrows[2 * at : 2 * at + 2, :] = rows[...]
    k.vrows[12:14, :] = k.cmask[...].astype(F32)
    k.vrows[14:16, :] = jnp.zeros((2, wide), F32)
    k.cols[...] = exact_dot(eye(wide, F32), k.vrows[...], ((1,), (1,)))

    def col(layer, which):
        at = 2 * which + layer
        return k.cols[:, at : at + 1]

    for way in range(4):
        k.owner[:, way * halo : (way + 1) * halo] = one_hot(k.lists[way : way + 1, :], LISTED)

    weights = []
    for layer in range(2):
        w1t = k.ew1t[layer]
        n1t = k.nw1t[layer]
        w2 = k.ew2[layer]
        n2 = k.nw2[layer]
        half = BF16(0.5)
        weights.append(
            dict(
                sender=w1t[:, :wide] * half,
                receiver=w1t[:, wide : 2 * wide] * half,
                attr=w1t[:, 2 * wide :] * half,
                second=turned(w2),
                node_one=n1t * half,
                node_two=turned(n2),
                sender_back=turned(w1t[:, :wide]),
                receiver_back=turned(w1t[:, wide : 2 * wide]),
                second_back=w2 * half,
                node_one_back=turned(n1t),
                node_two_back=n2 * half,
            )
        )
    for layer in range(2):
        for at, name in enumerate(
            (
                "sender", "receiver", "attr", "second", "node_two",
                "sender_back", "receiver_back", "second_back", "node_two_back",
            )
        ):
            k.small[layer, at] = weights[layer][name]
        k.wide_w[layer] = weights[layer]["node_one"]
        k.tall_w[layer] = weights[layer]["node_one_back"]
    SENDER, RECEIVER, ATTR, SECOND, NODE_TWO, SENDER_B, RECEIVER_B, SECOND_B, NODE_TWO_B = range(9)

    def split_index(layer, lanes):
        index = k.nbr[layer, :, lanes]
        return index, index >> shift, index & (high - 1)

    def live_lanes(start, width):
        return lax.broadcasted_iota(jnp.int32, (1, width), 1) + start < count

    def node_lanes(first, last):
        return [pl.ds(at, CHUNK) for at in range(first, last, CHUNK)]

    def send_halos(layer):
        picked = dot(k.xs[layer, :wide, :LISTED], k.owner[...]).astype(BF16)
        for way in range(4):
            k.sends[layer, way] = picked[:, way * halo : (way + 1) * halo]
        start_exchange(exchange(k.sends, k.halos, k.halo_send, k.halo_recv, layer))

    def project(layer):
        low = k.xs[layer, :wide, :]
        k.base[...] = dot(k.small[layer, RECEIVER], low) + 0.5 * col(layer, EB1)
        projected = dot(k.small[layer, SENDER], low).astype(BF16)
        for part in range(locals_):
            k.table[part * wide : (part + 1) * wide, :] = projected[
                :, part * high : (part + 1) * high
            ]

    def project_halos(layer):
        finish_exchange(exchange(k.sends, k.halos, k.halo_send, k.halo_recv, layer))
        for way in range(4):
            k.table[locals_ * wide :, way * halo : (way + 1) * halo] = dot(
                k.small[layer, SENDER], k.halos[layer, way]
            ).astype(BF16)

    def edges_forward(layer):
        def body(at, carry):
            start = pl.multiple_of(at * TILE, TILE)
            lanes = pl.ds(start, TILE)
            index, sub, hi = split_index(layer, lanes)
            sender_ok = jnp.where(
                index < nodes,
                (index < count).astype(F32),
                jnp.where(
                    index < nodes + halo,
                    has_low.astype(F32),
                    jnp.where(index < nodes + 2 * halo, has_high.astype(F32), 1.0),
                ),
            )
            edge_ok = sender_ok * live_lanes(start, TILE).astype(F32)
            base = k.base[:, lanes]
            total = jnp.zeros((wide, TILE), F32)
            for first in range(0, degree, GROUP):
                slots = range(first, first + GROUP)
                hot = join([one_hot(hi[j : j + 1], high) for j in slots])
                found = dot(k.table[...], hot)
                for place, j in enumerate(slots):
                    piece = found[:, place * TILE : (place + 1) * TILE]
                    piece = piece.reshape(parts, wide // 8, 8, TILE)
                    which = jnp.broadcast_to(sub[j : j + 1], (8, TILE))
                    chosen = piece[0]
                    for part in range(1, parts):
                        chosen = jnp.where((which == part)[None], piece[part], chosen)
                    own = dot(k.small[layer, ATTR], k.attr[layer, j, :, lanes])
                    act, slope = gate(chosen.reshape(wide, TILE) + base + own)
                    act = act.astype(BF16)
                    k.act[layer, j, :, lanes] = act
                    k.slope[layer, j, :, lanes] = slope.astype(BF16)
                    second = dot(k.small[layer, SECOND], act)
                    center = second - mean0(second)
                    rate = lax.rsqrt(mean0(center * center) + 1e-05) * edge_ok[j : j + 1]
                    k.rate_e[layer, j : j + 1, lanes] = rate
                    unit = center * rate
                    k.unit[layer, j, :, lanes] = unit.astype(BF16)
                    total = total + unit
            k.total[layer, :, lanes] = total
            k.kept[layer, :, lanes] = jnp.sum(edge_ok, axis=0, keepdims=True)
            return carry

        lax.fori_loop(0, nodes // TILE, body, 0)

    def nodes_forward(layer, first, last):
        for lanes in node_lanes(first, last):
            mask = col(layer, CMASK)
            summed = (mask * col(layer, EGAIN)) * k.total[layer, :, lanes] + (
                mask * col(layer, ESHIFT)
            ) * k.kept[layer, :, lanes]
            k.xs[layer, wide:, lanes] = summed.astype(BF16)
            half = dot(k.wide_w[layer], k.xs[layer, :, lanes]) + 0.5 * col(layer, NB1)
            act, slope = gate(half)
            act = act.astype(BF16)
            k.act_n[layer, :, lanes] = act
            k.slope_n[layer, :, lanes] = slope.astype(BF16)
            fourth = dot(k.small[layer, NODE_TWO], act)
            center = fourth - mean0(fourth)
            rate = lax.rsqrt(mean0(center * center) + 1e-05)
            unit = center * rate
            k.rate_n[layer, :, lanes] = rate
            k.unit_n[layer, :, lanes] = unit
            valid = live_lanes(lanes.start, CHUNK).astype(F32)
            change = valid * (unit * col(layer, NGAIN) + col(layer, NSHIFT))
            if layer == 0:
                middle = k.state[:, lanes].astype(F32) + change + k.latent[:, lanes].astype(F32)
                k.middle[:, lanes] = middle
                k.xs[1, :wide, lanes] = middle.astype(BF16)
            else:
                k.mesh_out[:, lanes] = (k.middle[:, lanes] + change).astype(BF16)

    def into(layer):
        return k.grad_latent if layer == 1 else k.grad_state

    def nodes_backward(layer, first, last):
        for lanes in node_lanes(first, last):
            valid = live_lanes(lanes.start, CHUNK).astype(F32)
            if layer == 1:
                grad = k.out_grad[:, lanes].astype(F32)
            else:
                grad = k.grad_latent[:, lanes]
            unit = k.unit_n[layer, :, lanes]
            grad_ok = valid * grad
            k.sums[layer, NGAIN] += fold(grad_ok * unit)
            k.sums[layer, NSHIFT] += fold(grad_ok)
            scaled = grad_ok * col(layer, NGAIN)
            fourth = k.rate_n[layer, :, lanes] * (
                scaled - mean0(scaled) - unit * mean0(scaled * unit)
            )
            fourth = fourth.astype(BF16)
            k.acc_64[layer, 3] += dot_nt(k.act_n[layer, :, lanes], fourth)
            third = dot(k.small[layer, NODE_TWO_B], fourth) * k.slope_n[layer, :, lanes].astype(F32)
            k.sums[layer, NB1] += fold(third)
            third = third.astype(BF16)
            k.acc_128[layer] += dot_nt(third, k.xs[layer, :, lanes])
            both = dot(k.tall_w[layer], third)
            into(layer)[:, lanes] = grad + both[:wide]
            masked = both[wide:] * col(layer, CMASK)
            k.sums[layer, EGAIN] += fold(masked * k.total[layer, :, lanes])
            k.sums[layer, ESHIFT] += fold(masked * k.kept[layer, :, lanes])
            scaled = masked * col(layer, EGAIN)
            k.scaled[:, lanes] = scaled
            k.center[:, lanes] = scaled - mean0(scaled)

    def edges_backward(layer):
        k.scatter[...] = jnp.zeros_like(k.scatter)

        def body(at, carry):
            lanes = pl.ds(pl.multiple_of(at * TILE, TILE), TILE)
            index, sub, hi = split_index(layer, lanes)
            scaled, center = k.scaled[:, lanes], k.center[:, lanes]
            first_sum = jnp.zeros((wide, TILE), F32)
            grad_two = jnp.zeros((wide, wide), F32)
            grad_attr = jnp.zeros((wide, wide), F32)
            for first in range(0, degree, GROUP):
                slots = range(first, first + GROUP)
                hots, spreads, seconds, firsts = [], [], [], []
                for j in slots:
                    unit = k.unit[layer, j, :, lanes].astype(F32)
                    second = (center - unit * mean0(scaled * unit)) * k.rate_e[
                        layer, j : j + 1, lanes
                    ]
                    second = second.astype(BF16)
                    grad_one = dot(k.small[layer, SECOND_B], second) * k.slope[
                        layer, j, :, lanes
                    ].astype(F32)
                    first_sum = first_sum + grad_one
                    grad_one = grad_one.astype(BF16)
                    which = jnp.broadcast_to(sub[j : j + 1].astype(jnp.int16), (16, TILE))
                    rows = grad_one.reshape(wide // 16, 16, TILE)
                    spreads.append(
                        jnp.concatenate(
                            [
                                jnp.where((which == part)[None], rows, BF16(0)).reshape(wide, TILE)
                                for part in range(parts)
                            ],
                            axis=0,
                        )
                    )
                    hots.append(one_hot(hi[j : j + 1], high))
                    seconds.append(second)
                    firsts.append(grad_one)
                k.scatter[...] += dot_nt(join(spreads), join(hots))
                grad_two = grad_two + dot_nt(
                    join([k.act[layer, j, :, lanes] for j in slots]), join(seconds)
                )
                grad_attr = grad_attr + dot_nt(
                    join(firsts), join([k.attr[layer, j, :, lanes] for j in slots])
                )
            k.first_sum[:, lanes] = first_sum
            k.acc_64[layer, 1] += grad_attr
            k.acc_64[layer, 2] += grad_two
            return carry

        lax.fori_loop(0, nodes // TILE, body, 0)

    def give_back(layer):
        summed = k.scatter[...]
        coarse = summed.astype(BF16)
        fine = (summed - coarse.astype(F32)).astype(BF16)
        back = k.small[layer, SENDER_B]
        last = slice(locals_ * wide, parts * wide)
        to_owner = (dot(back, coarse[last]) + dot(back, fine[last])).astype(BF16)
        for way in range(4):
            k.gives[layer, way] = to_owner[:, way * halo : (way + 1) * halo]
        start_exchange(exchange(k.gives, k.backs, k.back_send, k.back_recv, layer))
        k.sums[layer, EB1] = fold(k.first_sum[...])
        first_sum = k.first_sum[...].astype(BF16)
        receiver = dot_nt(first_sum, k.xs[layer, :wide, :])
        halo_rows = join([k.halos[layer, way] for way in range(4)])
        sender = dot_nt(coarse[last], halo_rows) + dot_nt(fine[last], halo_rows)
        for part in range(locals_):
            span = slice(part * wide, (part + 1) * wide)
            rows = k.xs[layer, :wide, part * high : (part + 1) * high]
            sender = sender + dot_nt(coarse[span], rows) + dot_nt(fine[span], rows)
        lane = lax.broadcasted_iota(jnp.int32, (wide, wide), 1)
        vectors = jnp.zeros((wide, wide), F32)
        for which in range(6):
            vectors = jnp.where(
                lane == which, jnp.sum(k.sums[layer, which], axis=1, keepdims=True), vectors
            )
        blocks = (
            join([sender, receiver]),
            join([k.acc_64[layer, 1], k.acc_64[layer, 2]]),
            k.acc_128[layer],
            join([k.acc_64[layer, 3], vectors]),
        )
        rows = k.share.shape[2]
        for at, block in enumerate(blocks):
            for piece in range(wide // rows):
                k.share[layer, at * (wide // rows) + piece] = block[
                    piece * rows : (piece + 1) * rows, :
                ]

    def own_rows(layer):
        summed = k.scatter[...]
        coarse = summed.astype(BF16)
        fine = (summed - coarse.astype(F32)).astype(BF16)
        back = k.small[layer, SENDER_B]
        first_sum = k.first_sum[...].astype(BF16)
        for part in range(locals_):
            span = slice(part * wide, (part + 1) * wide)
            place = slice(part * high, (part + 1) * high)
            into(layer)[:, place] += (
                dot(back, coarse[span])
                + dot(back, fine[span])
                + dot(k.small[layer, RECEIVER_B], first_sum[:, place])
            )

    def take_back(layer):
        finish_exchange(exchange(k.gives, k.backs, k.back_send, k.back_recv, layer))
        returned = join([k.backs[layer, way] for way in range(4)])
        into(layer)[:, :LISTED] += dot_nt(returned, k.owner[...])

    def band_copy(layer, source, landing, sends, recvs, piece, slot, other):
        return pltpu.make_async_remote_copy(
            src_ref=source.at[layer, piece],
            dst_ref=landing.at[layer, slot],
            send_sem=sends.at[layer, other],
            recv_sem=recvs.at[layer, slot],
            device_id=(other, lon),
            device_id_type=MESH,
        )

    def lon_copy(layer, slot, other):
        return pltpu.make_async_remote_copy(
            src_ref=k.swap.at[layer, lon],
            dst_ref=k.swap.at[layer, slot],
            send_sem=k.sw_send.at[layer, other],
            recv_sem=k.sw_recv.at[layer, slot],
            device_id=(band, other),
            device_id_type=MESH,
        )

    def over(count_, here, act):
        def step(at, carry):
            act(lax.rem(here + at, count_))
            return carry

        lax.fori_loop(1, count_, step, 0)

    def spread_start(layer):
        over(
            bands,
            band,
            lambda other: band_copy(
                layer, k.share, k.spread, k.rs_send, k.rs_recv, other, band, other
            ).start(),
        )
        k.spread[layer, band] = k.share[layer, band]

    def swap_start(layer):
        over(
            bands,
            band,
            lambda other: band_copy(
                layer, k.share, k.spread, k.rs_send, k.rs_recv, other, other, other
            ).wait(),
        )
        k.swap[layer, lon] = jnp.sum(k.spread[layer], axis=0)
        over(lons, lon, lambda other: lon_copy(layer, lon, other).start())

    def gather_start(layer):
        over(lons, lon, lambda other: lon_copy(layer, other, other).wait())
        k.whole[layer, band] = jnp.sum(k.swap[layer], axis=0)
        over(
            bands,
            band,
            lambda other: band_copy(
                layer, k.whole, k.whole, k.ag_send, k.ag_recv, band, band, other
            ).start(),
        )

    def gather_end(layer):
        over(
            bands,
            band,
            lambda other: band_copy(
                layer, k.whole, k.whole, k.ag_send, k.ag_recv, band, other, other
            ).wait(),
        )
        for piece in range(k.reduced.shape[1]):
            k.reduced[layer, piece] = k.whole[layer, piece]

    middle_row = nodes // 2
    k.xs[0, :wide, :] = k.state[...]
    k.sums[...] = jnp.zeros_like(k.sums)
    k.acc_64[...] = jnp.zeros_like(k.acc_64)
    k.acc_128[...] = jnp.zeros_like(k.acc_128)
    pl.semaphore_wait(barrier, bands + lons - 2)
    send_halos(0)
    project(0)
    project_halos(0)
    edges_forward(0)
    nodes_forward(0, 0, LISTED)
    send_halos(1)
    nodes_forward(0, LISTED, nodes)
    project(1)
    project_halos(1)
    edges_forward(1)
    nodes_forward(1, 0, nodes)
    nodes_backward(1, 0, nodes)
    edges_backward(1)
    give_back(1)
    spread_start(1)
    own_rows(1)
    nodes_backward(0, LISTED, nodes)
    take_back(1)
    nodes_backward(0, 0, LISTED)
    swap_start(1)
    edges_backward(0)
    give_back(0)
    spread_start(0)
    gather_start(1)
    own_rows(0)
    take_back(0)
    swap_start(0)
    gather_start(0)
    gather_end(1)
    gather_end(0)


def finish(names, *refs):
    k = types.SimpleNamespace(**dict(zip(names, refs)))
    wide = k.g_ew2.shape[1]
    k.mesh_out[...] = k.mesh_in[...]
    k.grad_state[...] = k.state_in[...]
    k.grad_latent[...] = k.latent_in[...]
    for layer in range(2):
        rows = k.reduced.shape[2]
        pieces = wide // rows
        blocks = []
        for at in range(4):
            block = [k.reduced[layer, at * pieces + piece] for piece in range(pieces)]
            blocks.append(block[0] if pieces == 1 else jnp.concatenate(block, axis=0))
        k.g_ew1t[layer, :, : 2 * wide] = blocks[0]
        k.g_ew1t[layer, :, 2 * wide :] = blocks[1][:, :wide]
        k.g_ew2[layer] = blocks[1][:, wide:]
        k.g_nw1t[layer] = blocks[2]
        k.g_nw2[layer] = blocks[3][:, :wide]
        lines = exact_dot(blocks[3][:, wide:], eye(wide, F32), ((0,), (0,)))
        for which, out in enumerate(
            (k.g_eb1, k.g_egain, k.g_eshift, k.g_nb1, k.g_ngain, k.g_nshift)
        ):
            out[layer : layer + 1, :] = lines[which : which + 1, :]


INPUTS = (
    "state", "latent", "attr", "nbr", "lists", "count", "cmask", "ew1t", "eb1", "ew2",
    "egain", "eshift", "nw1t", "nb1", "nw2", "ngain", "nshift", "out_grad",
)
OUTPUTS = (
    "mesh_out", "grad_state", "grad_latent", "g_ew1t", "g_eb1", "g_ew2", "g_egain",
    "g_eshift", "g_nw1t", "g_nb1", "g_nw2", "g_ngain", "g_nshift",
)


FIRST_OUTPUTS = ("mesh_out", "grad_state", "grad_latent", "reduced")
FINISH_INPUTS = ("mesh_in", "state_in", "latent_in", "reduced")
VMEM_BYTES = 60 * 2**20


def shards(bands, lons, *args):
    (
        node_state, latent, edge_attr, neighbours, halo_lists, valid_counts, channel_mask,
        edge_w1, edge_b1, edge_w2, edge_gain, edge_shift,
        node_w1, node_b1, node_w2, node_gain, node_shift, out_grad,
    ) = args
    nodes, wide = node_state.shape
    degree = neighbours.shape[2]
    halo = halo_lists.shape[1]
    high = 4 * halo
    parts = nodes // high + 1
    rows = max(8, 4 * wide // bands)
    while wide % rows:
        rows //= 2
    pieces = max(bands, 4 * wide // rows)
    shape = jax.ShapeDtypeStruct
    outs = (
        shape((wide, nodes), BF16),
        shape((wide, nodes), F32),
        shape((wide, nodes), F32),
        shape((2, wide, 3 * wide), F32),
        shape((2, wide), F32),
        shape((2, wide, wide), F32),
        shape((2, wide), F32),
        shape((2, wide), F32),
        shape((2, wide, 2 * wide), F32),
        shape((2, wide), F32),
        shape((2, wide, wide), F32),
        shape((2, wide), F32),
        shape((2, wide), F32),
    )
    sem = pltpu.SemaphoreType.DMA
    scratch = dict(
        halos=pltpu.VMEM((2, 4, wide, halo), BF16),
        backs=pltpu.VMEM((2, 4, wide, halo), BF16),
        sends=pltpu.VMEM((2, 4, wide, halo), BF16),
        gives=pltpu.VMEM((2, 4, wide, halo), BF16),
        share=pltpu.VMEM((2, pieces, rows, 128), F32),
        spread=pltpu.VMEM((2, bands, rows, 128), F32),
        swap=pltpu.VMEM((2, lons, rows, 128), F32),
        whole=pltpu.VMEM((2, pieces, rows, 128), F32),
        vrows=pltpu.VMEM((16, wide), F32),
        cols=pltpu.VMEM((wide, 16), F32),
        owner=pltpu.VMEM((LISTED, high), BF16),
        small=pltpu.VMEM((2, 9, wide, wide), BF16),
        wide_w=pltpu.VMEM((2, wide, 2 * wide), BF16),
        tall_w=pltpu.VMEM((2, 2 * wide, wide), BF16),
        xs=pltpu.VMEM((2, 2 * wide, nodes), BF16),
        base=pltpu.VMEM((wide, nodes), F32),
        table=pltpu.VMEM((parts * wide, high), BF16),
        act=pltpu.VMEM((2, degree, wide, nodes), BF16),
        slope=pltpu.VMEM((2, degree, wide, nodes), BF16),
        unit=pltpu.VMEM((2, degree, wide, nodes), BF16),
        rate_e=pltpu.VMEM((2, degree, nodes), F32),
        total=pltpu.VMEM((2, wide, nodes), F32),
        kept=pltpu.VMEM((2, 1, nodes), F32),
        act_n=pltpu.VMEM((2, wide, nodes), BF16),
        slope_n=pltpu.VMEM((2, wide, nodes), BF16),
        rate_n=pltpu.VMEM((2, 1, nodes), F32),
        unit_n=pltpu.VMEM((2, wide, nodes), F32),
        middle=pltpu.VMEM((wide, nodes), F32),
        scaled=pltpu.VMEM((wide, nodes), F32),
        center=pltpu.VMEM((wide, nodes), F32),
        first_sum=pltpu.VMEM((wide, nodes), F32),
        scatter=pltpu.VMEM((parts * wide, high), F32),
        sums=pltpu.VMEM((2, 6, wide, 128), F32),
        acc_64=pltpu.VMEM((2, 4, wide, wide), F32),
        acc_128=pltpu.VMEM((2, wide, 2 * wide), F32),
        halo_send=sem((2, 4)),
        halo_recv=sem((2, 4)),
        back_send=sem((2, 4)),
        back_recv=sem((2, 4)),
        rs_send=sem((2, bands)),
        rs_recv=sem((2, bands)),
        sw_send=sem((2, lons)),
        sw_recv=sem((2, lons)),
        ag_send=sem((2, bands)),
        ag_recv=sem((2, bands)),
    )
    vmem = pl.BlockSpec(memory_space=pltpu.VMEM)
    specs = [vmem] * len(INPUTS)
    specs[INPUTS.index("count")] = pl.BlockSpec(memory_space=pltpu.SMEM)
    first_outs = outs[:3] + (shape((2, pieces, rows, 128), F32),)
    mids = pl.pallas_call(
        functools.partial(kernel, INPUTS + FIRST_OUTPUTS + tuple(scratch), bands, lons),
        out_shape=first_outs,
        in_specs=specs,
        out_specs=(vmem,) * 4,
        scratch_shapes=list(scratch.values()),
        compiler_params=pltpu.CompilerParams(
            collective_id=0, has_side_effects=True, vmem_limit_bytes=VMEM_BYTES
        ),
        name="layers",
    )(
        node_state.T,
        latent.T,
        edge_attr.transpose(0, 2, 3, 1),
        neighbours.transpose(0, 2, 1),
        halo_lists,
        valid_counts,
        channel_mask,
        edge_w1.transpose(0, 2, 1),
        edge_b1,
        edge_w2,
        edge_gain,
        edge_shift,
        node_w1.transpose(0, 2, 1),
        node_b1,
        node_w2,
        node_gain,
        node_shift,
        out_grad.T,
    )
    result = pl.pallas_call(
        functools.partial(finish, FINISH_INPUTS + OUTPUTS),
        out_shape=outs,
        in_specs=(vmem,) * 4,
        out_specs=(vmem,) * 13,
        name="finish",
    )(*mids)
    result = list(result)
    for at in range(3):
        result[at] = result[at].T
    for at in (3, 8):
        result[at] = result[at].transpose(0, 2, 1)
    return tuple(result)


def solution(mesh):
    nodes = P(("band", "lon"), None)
    whole = P()
    in_specs = (
        nodes,
        nodes,
        P(None, ("band", "lon"), None, None),
        P(None, ("band", "lon"), None),
        nodes,
        P(("band", "lon")),
    ) + (whole,) * 11 + (nodes,)
    return jax.shard_map(
        functools.partial(shards, mesh.shape["band"], mesh.shape["lon"]),
        mesh=mesh,
        in_specs=in_specs,
        out_specs=(nodes,) * 3 + (whole,) * 10,
        check_vma=False,
    )
```

```python
import functools
import types

import jax
import jax.numpy as jnp
from jax import lax
from jax.experimental import pallas as pl
from jax.experimental.pallas import tpu as pltpu
from jax.sharding import PartitionSpec as P

F32 = jnp.float32
BF16 = jnp.bfloat16
MESH = pl.DeviceIdType.MESH
LISTED = 1024
TILE_F, TILE_B, TILE_S = 2048, 1024, 1024
GROUP_F, GROUP_B, GROUP_S = 1, 2, 2
WAYS = 4
CHUNK = 256
EB1, EGAIN, ESHIFT, NB1, NGAIN, NSHIFT, CMASK = range(7)


def dot(left, right):
    return jnp.dot(left, right, preferred_element_type=F32)


def dot_nt(left, right):
    return lax.dot_general(left, right, (((1,), (1,)), ((), ())), preferred_element_type=F32)


def exact_dot(left, right, dims):
    return lax.dot_general(
        left, right, (dims, ((), ())), precision=lax.Precision.HIGHEST, preferred_element_type=F32
    )


def eye(size, kind):
    row = lax.broadcasted_iota(jnp.int32, (size, size), 0)
    col = lax.broadcasted_iota(jnp.int32, (size, size), 1)
    return (row == col).astype(F32).astype(kind)


def turned(matrix):
    return dot_nt(eye(matrix.shape[1], BF16), matrix).astype(BF16)


def one_hot(row, total):
    width = row.shape[1]
    index = lax.broadcasted_iota(jnp.int16, (total, width), 0)
    return jnp.where(
        index == jnp.broadcast_to(row.astype(jnp.int16), (total, width)), BF16(1), BF16(0)
    )


def join(parts):
    return parts[0] if len(parts) == 1 else jnp.concatenate(parts, axis=1)


def mean0(values):
    return jnp.mean(values, axis=0, keepdims=True)


def gate(half):
    bend = jnp.tanh(half)
    act = half + half * bend
    return act, (1.0 + bend) + act * (1.0 - bend)


def fold(values):
    total = values[:, :128]
    for at in range(128, values.shape[1], 128):
        total = total + values[:, at : at + 128]
    return total


def kernel(names, bands, lons, *refs):
    k = types.SimpleNamespace(**dict(zip(names, refs)))
    band, lon = lax.axis_index("band"), lax.axis_index("lon")
    wide, nodes = k.state.shape
    degree = k.nbr.shape[1]
    halo = k.lists.shape[1]
    high = WAYS * halo
    shift = high.bit_length() - 1
    locals_ = nodes // high
    parts = locals_ + 4 // WAYS
    count = k.count[0]
    loads = [
        pltpu.make_async_copy(source, target, k.load_sem.at[at])
        for at, (source, target) in enumerate(
            (
                (k.attr_in.at[0], k.attr.at[0]),
                (k.attr_in.at[1], k.attr.at[1]),
                (k.latent_in, k.latent),
                (k.out_grad_in, k.out_grad),
            )
        )
    ]
    stores = [
        pltpu.make_async_copy(source, target, k.store_sem.at[at])
        for at, (source, target) in enumerate(
            (
                (k.mesh_out, k.mesh_to),
                (k.grad_latent, k.latent_to),
                (k.grad_state, k.state_to),
                (k.whole, k.reduced),
            )
        )
    ]
    for load in loads:
        load.start()
    west, east = lax.rem(lon + lons - 1, lons), lax.rem(lon + 1, lons)
    has_low, has_high = band > 0, band < bands - 1

    for use in range(2):
        for way in range(2):
            k.halos[use, way] = jnp.zeros((wide, halo), BF16)
            k.backs[use, way] = jnp.zeros((wide, halo), BF16)
    barrier = pltpu.get_barrier_semaphore()

    def greet_band(step, carry):
        other = lax.rem(band + step, bands)
        pl.semaphore_signal(barrier, inc=1, device_id=(other, lon), device_id_type=MESH)
        return carry

    def greet_lon(step, carry):
        other = lax.rem(lon + step, lons)
        pl.semaphore_signal(barrier, inc=1, device_id=(band, other), device_id_type=MESH)
        return carry

    lax.fori_loop(1, bands, greet_band, 0)
    lax.fori_loop(1, lons, greet_lon, 0)

    def exchange(source, target, sends, recvs, use):
        def copy(block, landing, device):
            return pltpu.make_async_remote_copy(
                src_ref=source.at[use, block],
                dst_ref=target.at[use, landing],
                send_sem=sends.at[use, block],
                recv_sem=recvs.at[use, landing],
                device_id=device,
                device_id_type=MESH,
            )

        return copy

    turn = (1, 0, 3, 2)

    def targets():
        return ((band - 1, lon), (band + 1, lon), (band, west), (band, east))

    def start_exchange(copy):
        peers = targets()
        for block in range(4):
            go = copy(block, turn[block], peers[block]).start
            if block == 0:
                pl.when(has_low)(go)
            elif block == 1:
                pl.when(has_high)(go)
            else:
                go()

    def finish_exchange(copy):
        peers = targets()
        for block in range(4):
            def end(block=block):
                copy(block, block, peers[block]).wait()

            if block == 0:
                pl.when(has_low)(end)
            elif block == 1:
                pl.when(has_high)(end)
            else:
                end()

    SENDER, RECEIVER, ATTR, SECOND, NODE_TWO, SENDER_B, RECEIVER_B, SECOND_B, NODE_TWO_B = range(9)

    def col(layer, which):
        at = 2 * which + layer
        return k.cols[:, at : at + 1]

    def tables():
        for at, rows in enumerate((k.eb1, k.egain, k.eshift, k.nb1, k.ngain, k.nshift)):
            k.vrows[2 * at : 2 * at + 2, :] = rows[...]
        k.vrows[12:14, :] = k.cmask[...].astype(F32)
        k.vrows[14:16, :] = jnp.zeros((2, wide), F32)
        k.cols[...] = exact_dot(eye(wide, F32), k.vrows[...], ((1,), (1,)))

        weights = []
        for layer in range(2):
            w1t = k.ew1t[layer]
            n1t = k.nw1t[layer]
            w2 = k.ew2[layer]
            n2 = k.nw2[layer]
            half = BF16(0.5)
            weights.append(
                dict(
                    sender=w1t[:, :wide] * half,
                    receiver=w1t[:, wide : 2 * wide] * half,
                    attr=w1t[:, 2 * wide :] * half,
                    second=turned(w2),
                    node_one=n1t * half,
                    node_two=turned(n2),
                    sender_back=turned(w1t[:, :wide]),
                    receiver_back=turned(w1t[:, wide : 2 * wide]),
                    second_back=w2 * half,
                    node_one_back=turned(n1t),
                    node_two_back=n2 * half,
                )
            )
        for layer in range(2):
            for at, name in enumerate(
                (
                    "sender", "receiver", "attr", "second", "node_two",
                    "sender_back", "receiver_back", "second_back", "node_two_back",
                )
            ):
                k.small[layer, at] = weights[layer][name]
            k.wide_w[layer] = weights[layer]["node_one"]
            k.tall_w[layer] = weights[layer]["node_one_back"]

    def owners():
        for way in range(4):
            k.owner[:, way * halo : (way + 1) * halo] = one_hot(k.lists[way : way + 1, :], LISTED)

    def split_index(layer, lanes):
        index = k.nbr[layer, :, lanes]
        return index, index >> shift, index & (high - 1)

    def live_lanes(start, width):
        return lax.broadcasted_iota(jnp.int32, (1, width), 1) + start < count

    def node_lanes(first, last):
        return [pl.ds(at, CHUNK) for at in range(first, last, CHUNK)]

    def send_halos(layer):
        picked = dot(k.xs[layer, :wide, :LISTED], k.owner[...]).astype(BF16)
        for way in range(4):
            k.sends[layer, way] = picked[:, way * halo : (way + 1) * halo]
        start_exchange(exchange(k.sends, k.halos, k.halo_send, k.halo_recv, layer))

    def as_sent(layer, rows):
        return rows if layer == 0 else dot(k.small[layer, SENDER], rows).astype(BF16)

    def project(layer):
        low = k.xs[layer, :wide, :]
        own = as_sent(layer, low)
        for part in range(locals_):
            k.table[part * wide : (part + 1) * wide, :] = own[:, part * high : (part + 1) * high]
        base = dot(k.small[layer, RECEIVER], low) + 0.5 * col(layer, EB1)
        loads[layer].wait()
        for j in range(degree):
            k.pre[j] = dot(k.small[layer, ATTR], k.attr[layer, j]) + base

    def project_halos(layer):
        finish_exchange(exchange(k.sends, k.halos, k.halo_send, k.halo_recv, layer))
        for way in range(4):
            top, left = (locals_ + way // WAYS) * wide, way % WAYS * halo
            k.table[top : top + wide, left : left + halo] = as_sent(layer, k.halos[layer, way])

    def edges_forward(layer):
        def body(at, carry):
            start = pl.multiple_of(at * TILE_F, TILE_F)
            lanes = pl.ds(start, TILE_F)
            index, sub, hi = split_index(layer, lanes)
            sender_ok = jnp.where(
                index < nodes,
                (index < count).astype(F32),
                jnp.where(
                    index < nodes + halo,
                    has_low.astype(F32),
                    jnp.where(index < nodes + 2 * halo, has_high.astype(F32), 1.0),
                ),
            )
            edge_ok = sender_ok * live_lanes(start, TILE_F).astype(F32)
            total = jnp.zeros((wide, TILE_F), F32)
            for first in range(0, degree, GROUP_F):
                slots = range(first, first + GROUP_F)
                hot = join([one_hot(hi[j : j + 1], high) for j in slots])
                found = dot(k.table[...], hot)
                for place, j in enumerate(slots):
                    piece = found[:, place * TILE_F : (place + 1) * TILE_F]
                    piece = piece.reshape(parts, wide // 8, 8, TILE_F)
                    which = jnp.broadcast_to(sub[j : j + 1], (8, TILE_F))
                    chosen = piece[0]
                    for part in range(1, parts):
                        chosen = jnp.where((which == part)[None], piece[part], chosen)
                    chosen = chosen.reshape(wide, TILE_F)
                    if layer == 0:
                        chosen = chosen.astype(BF16)
                        k.senders[j, :, lanes] = chosen
                        chosen = dot(k.small[layer, SENDER], chosen)
                    act, slope = gate(chosen + k.pre[j, :, lanes])
                    act = act.astype(BF16)
                    k.act[layer, j, :, lanes] = act
                    k.slope[layer, j, :, lanes] = slope.astype(BF16)
                    second = dot(k.small[layer, SECOND], act)
                    center = second - mean0(second)
                    rate = lax.rsqrt(mean0(center * center) + 1e-05) * edge_ok[j : j + 1]
                    k.rate_e[layer, j : j + 1, lanes] = rate
                    unit = center * rate
                    k.unit[layer, j, :, lanes] = unit.astype(BF16)
                    total = total + unit
            k.total[layer, :, lanes] = total
            k.kept[layer, :, lanes] = jnp.sum(edge_ok, axis=0, keepdims=True)
            return carry

        lax.fori_loop(0, nodes // TILE_F, body, 0)

    def nodes_forward(layer, first, last):
        for lanes in node_lanes(first, last):
            mask = col(layer, CMASK)
            summed = (mask * col(layer, EGAIN)) * k.total[layer, :, lanes] + (
                mask * col(layer, ESHIFT)
            ) * k.kept[layer, :, lanes]
            k.xs[layer, wide:, lanes] = summed.astype(BF16)
            half = dot(k.wide_w[layer], k.xs[layer, :, lanes]) + 0.5 * col(layer, NB1)
            act, slope = gate(half)
            act = act.astype(BF16)
            k.act_n[layer, :, lanes] = act
            k.slope_n[layer, :, lanes] = slope.astype(BF16)
            fourth = dot(k.small[layer, NODE_TWO], act)
            center = fourth - mean0(fourth)
            rate = lax.rsqrt(mean0(center * center) + 1e-05)
            unit = center * rate
            k.rate_n[layer, :, lanes] = rate
            k.unit_n[layer, :, lanes] = unit
            valid = live_lanes(lanes.start, CHUNK).astype(F32)
            change = valid * (unit * col(layer, NGAIN) + col(layer, NSHIFT))
            if layer == 0:
                middle = k.state[:, lanes].astype(F32) + change + k.latent[:, lanes].astype(F32)
                k.middle[:, lanes] = middle
                k.xs[1, :wide, lanes] = middle.astype(BF16)
            else:
                k.mesh_out[:, lanes] = (k.middle[:, lanes] + change).astype(BF16)

    def into(layer):
        return k.grad_latent if layer == 1 else k.grad_state

    def nodes_backward(layer, first, last):
        for lanes in node_lanes(first, last):
            valid = live_lanes(lanes.start, CHUNK).astype(F32)
            if layer == 1:
                grad = k.out_grad[:, lanes].astype(F32)
            else:
                grad = k.grad_latent[:, lanes]
            unit = k.unit_n[layer, :, lanes]
            grad_ok = valid * grad
            k.sums[layer, NGAIN] += fold(grad_ok * unit)
            k.sums[layer, NSHIFT] += fold(grad_ok)
            scaled = grad_ok * col(layer, NGAIN)
            fourth = k.rate_n[layer, :, lanes] * (
                scaled - mean0(scaled) - unit * mean0(scaled * unit)
            )
            fourth = fourth.astype(BF16)
            k.acc_64[layer, 3] += dot_nt(k.act_n[layer, :, lanes], fourth)
            third = dot(k.small[layer, NODE_TWO_B], fourth) * k.slope_n[layer, :, lanes].astype(F32)
            k.sums[layer, NB1] += fold(third)
            third = third.astype(BF16)
            k.acc_128[layer] += dot_nt(third, k.xs[layer, :, lanes])
            both = dot(k.tall_w[layer], third)
            into(layer)[:, lanes] = grad + both[:wide]
            masked = both[wide:] * col(layer, CMASK)
            k.sums[layer, EGAIN] += fold(masked * k.total[layer, :, lanes])
            k.sums[layer, ESHIFT] += fold(masked * k.kept[layer, :, lanes])
            scaled = masked * col(layer, EGAIN)
            k.scaled[:, lanes] = scaled
            k.center[:, lanes] = scaled - mean0(scaled)

    def scatter_slots(lanes, sub, hi, firsts, slots):
        spreads, hots = [], []
        for j, grad in zip(slots, firsts):
            width = grad.shape[1]
            which = jnp.broadcast_to(sub[j : j + 1].astype(jnp.int16), (16, width))
            rows = grad.reshape(wide // 16, 16, width)
            spreads.append(
                jnp.concatenate(
                    [
                        jnp.where((which == part)[None], rows, BF16(0)).reshape(wide, width)
                        for part in range(parts)
                    ],
                    axis=0,
                )
            )
            hots.append(one_hot(hi[j : j + 1], high))
        k.scatter[...] += dot_nt(join(spreads), join(hots))

    def scatter_pass(layer, first, last):
        def body(at, carry):
            lanes = pl.ds(pl.multiple_of(at * TILE_S, TILE_S), TILE_S)
            index, sub, hi = split_index(layer, lanes)
            for start in range(0, degree, GROUP_S):
                slots = range(start, start + GROUP_S)
                scatter_slots(lanes, sub, hi, [k.first[j, :, lanes] for j in slots], slots)
            return carry

        lax.fori_loop(first, last, body, 0)

    def edges_backward(layer):
        def body(at, carry):
            lanes = pl.ds(pl.multiple_of(at * TILE_B, TILE_B), TILE_B)
            index, sub, hi = split_index(layer, lanes)
            scaled, center = k.scaled[:, lanes], k.center[:, lanes]
            first_sum = jnp.zeros((wide, TILE_B), F32)
            for start in range(0, degree, GROUP_B):
                slots = range(start, start + GROUP_B)
                firsts = []
                for j in slots:
                    unit = k.unit[layer, j, :, lanes].astype(F32)
                    second = (center - unit * mean0(scaled * unit)) * k.rate_e[
                        layer, j : j + 1, lanes
                    ]
                    second = second.astype(BF16)
                    grad_one = dot(k.small[layer, SECOND_B], second) * k.slope[
                        layer, j, :, lanes
                    ].astype(F32)
                    first_sum = first_sum + grad_one
                    grad_one = grad_one.astype(BF16)
                    k.first[j, :, lanes] = grad_one
                    k.second[j, :, lanes] = second
                    firsts.append(grad_one)
                if layer == 1:
                    scatter_slots(lanes, sub, hi, firsts, slots)
            k.first_sum[:, lanes] = first_sum
            return carry

        lax.fori_loop(0, nodes // TILE_B, body, 0)

    def edge_weights(layer):
        grad_two = jnp.zeros((wide, wide), F32)
        grad_attr = jnp.zeros((wide, wide), F32)
        grad_both = jnp.zeros((wide, 2 * wide), F32)
        for j in range(degree):
            grad_two = grad_two + dot_nt(k.act[layer, j], k.second[j])
            if layer == 0:
                both = jnp.concatenate([k.senders[j], k.attr[layer, j]], axis=0)
                grad_both = grad_both + dot_nt(k.first[j], both)
            else:
                grad_attr = grad_attr + dot_nt(k.first[j], k.attr[layer, j])
        k.acc_64[layer, 2] = grad_two
        if layer == 0:
            k.acc_64[layer, 0] = grad_both[:, :wide]
            k.acc_64[layer, 1] = grad_both[:, wide:]
        else:
            k.acc_64[layer, 1] = grad_attr

    def two_terms(values):
        coarse = values.astype(BF16)
        return coarse, (values - coarse.astype(F32)).astype(BF16)

    def give_back(layer):
        back = k.small[layer, SENDER_B]
        halo_sums = [
            two_terms(k.scatter[part * wide : (part + 1) * wide, :])
            for part in range(locals_, parts)
        ]
        to_owner = join([dot(back, coarse) + dot(back, fine) for coarse, fine in halo_sums])
        to_owner = to_owner.astype(BF16)
        for way in range(4):
            k.gives[layer, way] = to_owner[:, way * halo : (way + 1) * halo]
        start_exchange(exchange(k.gives, k.backs, k.back_send, k.back_recv, layer))

    def sender_weights(layer):
        sender = jnp.zeros((wide, wide), F32)
        for part in range(parts):
            if part < locals_:
                rows = k.xs[layer, :wide, part * high : (part + 1) * high]
            else:
                first = (part - locals_) * WAYS
                rows = join([k.halos[layer, first + way] for way in range(WAYS)])
            coarse, fine = two_terms(k.scatter[part * wide : (part + 1) * wide, :])
            sender = sender + dot_nt(coarse, rows) + dot_nt(fine, rows)
        k.acc_64[layer, 0] = sender

    def share_weights(layer):
        k.sums[layer, EB1] = fold(k.first_sum[...])
        first_sum = k.first_sum[...].astype(BF16)
        receiver = dot_nt(first_sum, k.xs[layer, :wide, :])
        sender = k.acc_64[layer, 0]
        lane = lax.broadcasted_iota(jnp.int32, (wide, wide), 1)
        vectors = jnp.zeros((wide, wide), F32)
        for which in range(6):
            vectors = jnp.where(
                lane == which, jnp.sum(k.sums[layer, which], axis=1, keepdims=True), vectors
            )
        blocks = (
            join([sender, receiver]),
            join([k.acc_64[layer, 1], k.acc_64[layer, 2]]),
            k.acc_128[layer],
            join([k.acc_64[layer, 3], vectors]),
        )
        rows = k.share.shape[2]
        for at, block in enumerate(blocks):
            for piece in range(wide // rows):
                k.share[layer, at * (wide // rows) + piece] = block[
                    piece * rows : (piece + 1) * rows, :
                ]

    def own_rows(layer):
        back = k.small[layer, SENDER_B]
        first_sum = k.first_sum[...].astype(BF16)
        for part in range(locals_):
            place = slice(part * high, (part + 1) * high)
            coarse, fine = two_terms(k.scatter[part * wide : (part + 1) * wide, :])
            into(layer)[:, place] += (
                dot(back, coarse)
                + dot(back, fine)
                + dot(k.small[layer, RECEIVER_B], first_sum[:, place])
            )

    def take_back(layer):
        finish_exchange(exchange(k.gives, k.backs, k.back_send, k.back_recv, layer))
        returned = join([k.backs[layer, way] for way in range(4)])
        into(layer)[:, :LISTED] += dot_nt(returned, k.owner[...])

    def band_copy(layer, source, landing, sends, recvs, piece, slot, other):
        return pltpu.make_async_remote_copy(
            src_ref=source.at[layer, piece],
            dst_ref=landing.at[layer, slot],
            send_sem=sends.at[layer, other],
            recv_sem=recvs.at[layer, slot],
            device_id=(other, lon),
            device_id_type=MESH,
        )

    def lon_copy(layer, slot, other):
        return pltpu.make_async_remote_copy(
            src_ref=k.swap.at[layer, lon],
            dst_ref=k.swap.at[layer, slot],
            send_sem=k.sw_send.at[layer, other],
            recv_sem=k.sw_recv.at[layer, slot],
            device_id=(band, other),
            device_id_type=MESH,
        )

    def over(count_, here, act):
        def step(at, carry):
            act(lax.rem(here + at, count_))
            return carry

        lax.fori_loop(1, count_, step, 0)

    def spread_start(layer):
        over(
            bands,
            band,
            lambda other: band_copy(
                layer, k.share, k.spread, k.rs_send, k.rs_recv, other, band, other
            ).start(),
        )
        k.spread[layer, band] = k.share[layer, band]

    def swap_start(layer):
        over(
            bands,
            band,
            lambda other: band_copy(
                layer, k.share, k.spread, k.rs_send, k.rs_recv, other, other, other
            ).wait(),
        )
        k.swap[layer, lon] = jnp.sum(k.spread[layer], axis=0)
        over(lons, lon, lambda other: lon_copy(layer, lon, other).start())

    def gather_start(layer):
        over(lons, lon, lambda other: lon_copy(layer, other, other).wait())
        k.whole[layer, band] = jnp.sum(k.swap[layer], axis=0)
        over(
            bands,
            band,
            lambda other: band_copy(
                layer, k.whole, k.whole, k.ag_send, k.ag_recv, band, band, other
            ).start(),
        )

    def gather_end(layer):
        over(
            bands,
            band,
            lambda other: band_copy(
                layer, k.whole, k.whole, k.ag_send, k.ag_recv, band, other, other
            ).wait(),
        )

    k.xs[0, :wide, :] = k.state[...]
    owners()
    pl.semaphore_wait(barrier, bands + lons - 2)
    send_halos(0)
    tables()
    k.sums[...] = jnp.zeros_like(k.sums)
    k.acc_64[...] = jnp.zeros_like(k.acc_64)
    k.acc_128[...] = jnp.zeros_like(k.acc_128)
    k.scatter[...] = jnp.zeros_like(k.scatter)
    project(0)
    project_halos(0)
    edges_forward(0)
    loads[2].wait()
    nodes_forward(0, 0, LISTED)
    send_halos(1)
    nodes_forward(0, LISTED, nodes)
    project(1)
    project_halos(1)
    edges_forward(1)
    loads[3].wait()
    nodes_forward(1, 0, nodes)
    stores[0].start()
    nodes_backward(1, 0, nodes)
    edges_backward(1)
    give_back(1)
    edge_weights(1)
    sender_weights(1)
    share_weights(1)
    spread_start(1)
    own_rows(1)
    nodes_backward(0, LISTED, nodes)
    take_back(1)
    stores[1].start()
    nodes_backward(0, 0, LISTED)
    swap_start(1)
    edges_backward(0)
    edge_weights(0)
    share_weights(0)
    spread_start(0)
    gather_start(1)
    k.scatter[...] = jnp.zeros_like(k.scatter)
    steps = nodes // TILE_S
    scatter_pass(0, 0, steps // 2)
    swap_start(0)
    scatter_pass(0, steps // 2, steps)
    give_back(0)
    gather_start(0)
    own_rows(0)
    take_back(0)
    stores[2].start()
    gather_end(1)
    gather_end(0)
    stores[3].start()
    for store in stores:
        store.wait()


def finish(names, *refs):
    k = types.SimpleNamespace(**dict(zip(names, refs)))
    wide = k.g_ew2.shape[1]
    k.mesh_out[...] = k.mesh_in[...]
    k.grad_state[...] = k.state_in[...]
    k.grad_latent[...] = k.latent_in[...]
    for layer in range(2):
        rows = k.reduced.shape[2]
        pieces = wide // rows
        blocks = []
        for at in range(4):
            block = [k.reduced[layer, at * pieces + piece] for piece in range(pieces)]
            blocks.append(block[0] if pieces == 1 else jnp.concatenate(block, axis=0))
        k.g_ew1t[layer, :, : 2 * wide] = blocks[0]
        k.g_ew1t[layer, :, 2 * wide :] = blocks[1][:, :wide]
        k.g_ew2[layer] = blocks[1][:, wide:]
        k.g_nw1t[layer] = blocks[2]
        k.g_nw2[layer] = blocks[3][:, :wide]
        lines = exact_dot(blocks[3][:, wide:], eye(wide, F32), ((0,), (0,)))
        for which, out in enumerate(
            (k.g_eb1, k.g_egain, k.g_eshift, k.g_nb1, k.g_ngain, k.g_nshift)
        ):
            out[layer : layer + 1, :] = lines[which : which + 1, :]


INPUTS = (
    "state", "latent_in", "attr_in", "nbr", "lists", "count", "cmask", "ew1t", "eb1", "ew2",
    "egain", "eshift", "nw1t", "nb1", "nw2", "ngain", "nshift", "out_grad_in",
)
OUTPUTS = (
    "mesh_out", "grad_state", "grad_latent", "g_ew1t", "g_eb1", "g_ew2", "g_egain",
    "g_eshift", "g_nw1t", "g_nb1", "g_nw2", "g_ngain", "g_nshift",
)


FIRST_OUTPUTS = ("mesh_to", "state_to", "latent_to", "reduced")
FINISH_INPUTS = ("mesh_in", "state_in", "latent_in", "reduced")
VMEM_BYTES = 60 * 2**20


def shards(bands, lons, *args):
    (
        node_state, latent, edge_attr, neighbours, halo_lists, valid_counts, channel_mask,
        edge_w1, edge_b1, edge_w2, edge_gain, edge_shift,
        node_w1, node_b1, node_w2, node_gain, node_shift, out_grad,
    ) = args
    nodes, wide = node_state.shape
    degree = neighbours.shape[2]
    halo = halo_lists.shape[1]
    high = WAYS * halo
    parts = nodes // high + 4 // WAYS
    rows = max(8, 4 * wide // bands)
    while wide % rows:
        rows //= 2
    pieces = max(bands, 4 * wide // rows)
    shape = jax.ShapeDtypeStruct
    outs = (
        shape((wide, nodes), BF16),
        shape((wide, nodes), F32),
        shape((wide, nodes), F32),
        shape((2, wide, 3 * wide), F32),
        shape((2, wide), F32),
        shape((2, wide, wide), F32),
        shape((2, wide), F32),
        shape((2, wide), F32),
        shape((2, wide, 2 * wide), F32),
        shape((2, wide), F32),
        shape((2, wide, wide), F32),
        shape((2, wide), F32),
        shape((2, wide), F32),
    )
    sem = pltpu.SemaphoreType.DMA
    scratch = dict(
        halos=pltpu.VMEM((2, 4, wide, halo), BF16),
        backs=pltpu.VMEM((2, 4, wide, halo), BF16),
        sends=pltpu.VMEM((2, 4, wide, halo), BF16),
        gives=pltpu.VMEM((2, 4, wide, halo), BF16),
        share=pltpu.VMEM((2, pieces, rows, 128), F32),
        spread=pltpu.VMEM((2, bands, rows, 128), F32),
        swap=pltpu.VMEM((2, lons, rows, 128), F32),
        whole=pltpu.VMEM((2, pieces, rows, 128), F32),
        vrows=pltpu.VMEM((16, wide), F32),
        cols=pltpu.VMEM((wide, 16), F32),
        owner=pltpu.VMEM((LISTED, 4 * halo), BF16),
        small=pltpu.VMEM((2, 9, wide, wide), BF16),
        wide_w=pltpu.VMEM((2, wide, 2 * wide), BF16),
        tall_w=pltpu.VMEM((2, 2 * wide, wide), BF16),
        xs=pltpu.VMEM((2, 2 * wide, nodes), BF16),
        attr=pltpu.VMEM((2, degree, wide, nodes), BF16),
        latent=pltpu.VMEM((wide, nodes), BF16),
        out_grad=pltpu.VMEM((wide, nodes), BF16),
        mesh_out=pltpu.VMEM((wide, nodes), BF16),
        grad_latent=pltpu.VMEM((wide, nodes), F32),
        grad_state=pltpu.VMEM((wide, nodes), F32),
        load_sem=sem((4,)),
        store_sem=sem((4,)),
        pre=pltpu.VMEM((degree, wide, nodes), F32),
        senders=pltpu.VMEM((degree, wide, nodes), BF16),
        first=pltpu.VMEM((degree, wide, nodes), BF16),
        second=pltpu.VMEM((degree, wide, nodes), BF16),
        table=pltpu.VMEM((parts * wide, high), BF16),
        act=pltpu.VMEM((2, degree, wide, nodes), BF16),
        slope=pltpu.VMEM((2, degree, wide, nodes), BF16),
        unit=pltpu.VMEM((2, degree, wide, nodes), BF16),
        rate_e=pltpu.VMEM((2, degree, nodes), F32),
        total=pltpu.VMEM((2, wide, nodes), F32),
        kept=pltpu.VMEM((2, 1, nodes), F32),
        act_n=pltpu.VMEM((2, wide, nodes), BF16),
        slope_n=pltpu.VMEM((2, wide, nodes), BF16),
        rate_n=pltpu.VMEM((2, 1, nodes), F32),
        unit_n=pltpu.VMEM((2, wide, nodes), F32),
        middle=pltpu.VMEM((wide, nodes), F32),
        scaled=pltpu.VMEM((wide, nodes), F32),
        center=pltpu.VMEM((wide, nodes), F32),
        first_sum=pltpu.VMEM((wide, nodes), F32),
        scatter=pltpu.VMEM((parts * wide, high), F32),
        sums=pltpu.VMEM((2, 6, wide, 128), F32),
        acc_64=pltpu.VMEM((2, 4, wide, wide), F32),
        acc_128=pltpu.VMEM((2, wide, 2 * wide), F32),
        halo_send=sem((2, 4)),
        halo_recv=sem((2, 4)),
        back_send=sem((2, 4)),
        back_recv=sem((2, 4)),
        rs_send=sem((2, bands)),
        rs_recv=sem((2, bands)),
        sw_send=sem((2, lons)),
        sw_recv=sem((2, lons)),
        ag_send=sem((2, bands)),
        ag_recv=sem((2, bands)),
    )
    vmem = pl.BlockSpec(memory_space=pltpu.VMEM)
    specs = [vmem] * len(INPUTS)
    anywhere = pl.BlockSpec(memory_space=pl.ANY)
    specs[INPUTS.index("count")] = pl.BlockSpec(memory_space=pltpu.SMEM)
    for name in ("latent_in", "attr_in", "out_grad_in"):
        specs[INPUTS.index(name)] = anywhere
    first_outs = outs[:3] + (shape((2, pieces, rows, 128), F32),)
    mids = pl.pallas_call(
        functools.partial(kernel, INPUTS + FIRST_OUTPUTS + tuple(scratch), bands, lons),
        out_shape=first_outs,
        in_specs=specs,
        out_specs=(anywhere,) * 4,
        scratch_shapes=list(scratch.values()),
        compiler_params=pltpu.CompilerParams(
            collective_id=0, has_side_effects=True, vmem_limit_bytes=VMEM_BYTES
        ),
        name="layers",
    )(
        node_state.T,
        latent.T,
        edge_attr.transpose(0, 2, 3, 1),
        neighbours.transpose(0, 2, 1),
        halo_lists,
        valid_counts,
        channel_mask,
        edge_w1.transpose(0, 2, 1),
        edge_b1,
        edge_w2,
        edge_gain,
        edge_shift,
        node_w1.transpose(0, 2, 1),
        node_b1,
        node_w2,
        node_gain,
        node_shift,
        out_grad.T,
    )
    result = pl.pallas_call(
        functools.partial(finish, FINISH_INPUTS + OUTPUTS),
        out_shape=outs,
        in_specs=(vmem,) * 4,
        out_specs=(vmem,) * 13,
        name="finish",
    )(*mids)
    result = list(result)
    for at in range(3):
        result[at] = result[at].T
    for at in (3, 8):
        result[at] = result[at].transpose(0, 2, 1)
    return tuple(result)


def solution(mesh):
    nodes = P(("band", "lon"), None)
    whole = P()
    in_specs = (
        nodes,
        nodes,
        P(None, ("band", "lon"), None, None),
        P(None, ("band", "lon"), None),
        nodes,
        P(("band", "lon")),
    ) + (whole,) * 11 + (nodes,)
    return jax.shard_map(
        functools.partial(shards, mesh.shape["band"], mesh.shape["lon"]),
        mesh=mesh,
        in_specs=in_specs,
        out_specs=(nodes,) * 3 + (whole,) * 10,
        check_vma=False,
    )
```

```python
import functools
import types

import jax
import jax.numpy as jnp
from jax import lax
from jax.experimental import pallas as pl
from jax.experimental.pallas import tpu as pltpu
from jax.sharding import PartitionSpec as P

F32 = jnp.float32
BF16 = jnp.bfloat16
MESH = pl.DeviceIdType.MESH
LISTED = 1024
TILE_F, TILE_B, TILE_S = 2048, 2048, 1024
GROUP_F, GROUP_B, GROUP_S = 2, 2, 4
WAYS = 4
CHUNK = 256
EB1, EGAIN, ESHIFT, NB1, NGAIN, NSHIFT, CMASK = range(7)


def dot(left, right):
    return jnp.dot(left, right, preferred_element_type=F32)


def dot_nt(left, right):
    return lax.dot_general(left, right, (((1,), (1,)), ((), ())), preferred_element_type=F32)


def exact_dot(left, right, dims):
    return lax.dot_general(
        left, right, (dims, ((), ())), precision=lax.Precision.HIGHEST, preferred_element_type=F32
    )


def eye(size, kind):
    row = lax.broadcasted_iota(jnp.int32, (size, size), 0)
    col = lax.broadcasted_iota(jnp.int32, (size, size), 1)
    return (row == col).astype(F32).astype(kind)


def turned(matrix):
    return dot_nt(eye(matrix.shape[1], BF16), matrix).astype(BF16)


def one_hot(row, total):
    width = row.shape[1]
    index = lax.broadcasted_iota(jnp.int16, (total, width), 0)
    return jnp.where(
        index == jnp.broadcast_to(row.astype(jnp.int16), (total, width)), BF16(1), BF16(0)
    )


def join(parts):
    return parts[0] if len(parts) == 1 else jnp.concatenate(parts, axis=1)


def mean0(values):
    return jnp.mean(values, axis=0, keepdims=True)


def gate(half):
    bend = jnp.tanh(half)
    act = half + half * bend
    return act, (1.0 + bend) + act * (1.0 - bend)


def fold(values):
    total = values[:, :128]
    for at in range(128, values.shape[1], 128):
        total = total + values[:, at : at + 128]
    return total


def kernel(names, bands, lons, *refs):
    k = types.SimpleNamespace(**dict(zip(names, refs)))
    band, lon = lax.axis_index("band"), lax.axis_index("lon")
    wide, nodes = k.state.shape
    degree = k.nbr.shape[1]
    halo = k.lists.shape[1]
    high = WAYS * halo
    shift = high.bit_length() - 1
    locals_ = nodes // high
    parts = locals_ + 4 // WAYS
    count = k.count[0]
    fetch = {
        name: pltpu.make_async_copy(getattr(k, name + "_in"), getattr(k, name), k.load_sem.at[at])
        for at, name in enumerate(FETCHED)
    }
    for layer in range(2):
        fetch["attr", layer] = pltpu.make_async_copy(
            k.attr_in.at[layer], k.attr.at[layer], k.load_sem.at[len(FETCHED) + layer]
        )
    stores = [
        pltpu.make_async_copy(source, target, k.store_sem.at[at])
        for at, (source, target) in enumerate(
            (
                (k.mesh_out, k.mesh_to),
                (k.grad_latent, k.latent_to),
                (k.grad_state, k.state_to),
                (k.whole, k.reduced),
            )
        )
    ]
    west, east = lax.rem(lon + lons - 1, lons), lax.rem(lon + 1, lons)
    has_low, has_high = band > 0, band < bands - 1

    near = 2 if bands % 2 == 0 else 1
    size_a, size_b = near * lons, bands // near
    at_a = lax.rem(band, near) * lons + lon
    at_b = band // near

    def member_a(at):
        return (at_b * near + at // lons, lax.rem(at, lons))

    def member_b(at):
        return (at * near + lax.rem(band, near), lon)

    def over(size, here, act):
        def step(at, carry):
            act(lax.rem(here + at, size))
            return carry

        lax.fori_loop(1, size, step, 0)

    for use in range(2):
        for way in range(2):
            k.halos[use, way] = jnp.zeros((wide, halo), BF16)
            k.backs[use, way] = jnp.zeros((wide, halo), BF16)
    barrier = pltpu.get_barrier_semaphore()

    def greet(device):
        pl.semaphore_signal(barrier, inc=1, device_id=device, device_id_type=MESH)

    pl.when(has_low)(lambda: greet((band - 1, lon)))
    pl.when(has_high)(lambda: greet((band + 1, lon)))
    over(size_a, at_a, lambda at: greet(member_a(at)))
    over(size_b, at_b, lambda at: greet(member_b(at)))
    greeted = size_a + size_b - 2 + has_low.astype(jnp.int32) + has_high.astype(jnp.int32)
    for name in FETCHED[:2]:
        fetch[name].start()
    fetch["attr", 0].start()
    for name in FETCHED[2:]:
        fetch[name].start()
    fetch["attr", 1].start()

    def exchange(source, target, sends, recvs, use):
        def copy(block, landing, device):
            return pltpu.make_async_remote_copy(
                src_ref=source.at[use, block],
                dst_ref=target.at[use, landing],
                send_sem=sends.at[use, block],
                recv_sem=recvs.at[use, landing],
                device_id=device,
                device_id_type=MESH,
            )

        return copy

    turn = (1, 0, 3, 2)

    def targets():
        return ((band - 1, lon), (band + 1, lon), (band, west), (band, east))

    def start_exchange(copy):
        peers = targets()
        for block in range(4):
            go = copy(block, turn[block], peers[block]).start
            if block == 0:
                pl.when(has_low)(go)
            elif block == 1:
                pl.when(has_high)(go)
            else:
                go()

    def finish_exchange(copy):
        peers = targets()
        for block in range(4):
            def end(block=block):
                copy(block, block, peers[block]).wait()

            if block == 0:
                pl.when(has_low)(end)
            elif block == 1:
                pl.when(has_high)(end)
            else:
                end()

    SENDER, RECEIVER, ATTR, SECOND, NODE_TWO, SENDER_B, RECEIVER_B, SECOND_B, NODE_TWO_B = range(9)

    def col(layer, which):
        at = 2 * which + layer
        return k.cols[:, at : at + 1]

    def tables():
        for at, rows in enumerate((k.eb1, k.egain, k.eshift, k.nb1, k.ngain, k.nshift)):
            k.vrows[2 * at : 2 * at + 2, :] = rows[...]
        k.vrows[12:14, :] = k.cmask[...].astype(F32)
        k.vrows[14:16, :] = jnp.zeros((2, wide), F32)
        k.cols[...] = exact_dot(eye(wide, F32), k.vrows[...], ((1,), (1,)))

        weights = []
        for layer in range(2):
            w1t = k.ew1t[layer]
            n1t = k.nw1t[layer]
            w2 = k.ew2[layer]
            n2 = k.nw2[layer]
            half = BF16(0.5)
            weights.append(
                dict(
                    sender=w1t[:, :wide] * half,
                    receiver=w1t[:, wide : 2 * wide] * half,
                    attr=w1t[:, 2 * wide :] * half,
                    second=turned(w2),
                    node_one=n1t * half,
                    node_two=turned(n2),
                    sender_back=turned(w1t[:, :wide]),
                    receiver_back=turned(w1t[:, wide : 2 * wide]),
                    second_back=w2 * half,
                    node_one_back=turned(n1t),
                    node_two_back=n2 * half,
                )
            )
        for layer in range(2):
            for at, name in enumerate(
                (
                    "sender", "receiver", "attr", "second", "node_two",
                    "sender_back", "receiver_back", "second_back", "node_two_back",
                )
            ):
                k.small[layer, at] = weights[layer][name]
            k.wide_w[layer] = weights[layer]["node_one"]
            k.tall_w[layer] = weights[layer]["node_one_back"]

    def owners():
        for way in range(4):
            k.owner[:, way * halo : (way + 1) * halo] = one_hot(k.lists[way : way + 1, :], LISTED)

    def split_index(layer, lanes):
        index = k.nbr[layer, :, lanes]
        return index, index >> shift, index & (high - 1)

    def live_lanes(start, width):
        return lax.broadcasted_iota(jnp.int32, (1, width), 1) + start < count

    def node_lanes(first, last):
        return [pl.ds(at, CHUNK) for at in range(first, last, CHUNK)]

    def pick_halos(layer):
        picked = dot(k.xs[layer, :wide, :LISTED], k.owner[...]).astype(BF16)
        for way in range(4):
            k.sends[layer, way] = picked[:, way * halo : (way + 1) * halo]

    def send_halos(layer):
        start_exchange(exchange(k.sends, k.halos, k.halo_send, k.halo_recv, layer))

    def as_sent(layer, rows):
        return rows if layer == 0 else dot(k.small[layer, SENDER], rows).astype(BF16)

    def project(layer):
        low = k.xs[layer, :wide, :]
        own = as_sent(layer, low)
        for part in range(locals_):
            k.table[part * wide : (part + 1) * wide, :] = own[:, part * high : (part + 1) * high]
        base = dot(k.small[layer, RECEIVER], low) + 0.5 * col(layer, EB1)
        fetch["attr", layer].wait()
        for j in range(degree):
            k.pre[j] = dot(k.small[layer, ATTR], k.attr[layer, j]) + base

    def project_halos(layer):
        finish_exchange(exchange(k.sends, k.halos, k.halo_send, k.halo_recv, layer))
        for way in range(4):
            top, left = (locals_ + way // WAYS) * wide, way % WAYS * halo
            k.table[top : top + wide, left : left + halo] = as_sent(layer, k.halos[layer, way])

    def edges_forward(layer):
        def body(at, carry):
            start = pl.multiple_of(at * TILE_F, TILE_F)
            lanes = pl.ds(start, TILE_F)
            index, sub, hi = split_index(layer, lanes)
            sender_ok = jnp.where(
                index < nodes,
                (index < count).astype(F32),
                jnp.where(
                    index < nodes + halo,
                    has_low.astype(F32),
                    jnp.where(index < nodes + 2 * halo, has_high.astype(F32), 1.0),
                ),
            )
            edge_ok = sender_ok * live_lanes(start, TILE_F).astype(F32)
            total = jnp.zeros((wide, TILE_F), F32)
            for first in range(0, degree, GROUP_F):
                slots = range(first, first + GROUP_F)
                hot = join([one_hot(hi[j : j + 1], high) for j in slots])
                found = dot(k.table[...], hot)
                for place, j in enumerate(slots):
                    piece = found[:, place * TILE_F : (place + 1) * TILE_F]
                    piece = piece.reshape(parts, wide // 8, 8, TILE_F)
                    which = jnp.broadcast_to(sub[j : j + 1], (8, TILE_F))
                    chosen = piece[0]
                    for part in range(1, parts):
                        chosen = jnp.where((which == part)[None], piece[part], chosen)
                    chosen = chosen.reshape(wide, TILE_F)
                    if layer == 0:
                        chosen = chosen.astype(BF16)
                        k.senders[j, :, lanes] = chosen
                        chosen = dot(k.small[layer, SENDER], chosen)
                    act, slope = gate(chosen + k.pre[j, :, lanes])
                    act = act.astype(BF16)
                    k.act[layer, j, :, lanes] = act
                    k.slope[layer, j, :, lanes] = slope.astype(BF16)
                    second = dot(k.small[layer, SECOND], act)
                    center = second - mean0(second)
                    rate = lax.rsqrt(mean0(center * center) + 1e-05) * edge_ok[j : j + 1]
                    k.rate_e[layer, j : j + 1, lanes] = rate
                    unit = center * rate
                    k.unit[layer, j, :, lanes] = unit.astype(BF16)
                    total = total + unit
            k.total[layer, :, lanes] = total
            k.kept[layer, :, lanes] = jnp.sum(edge_ok, axis=0, keepdims=True)
            return carry

        lax.fori_loop(0, nodes // TILE_F, body, 0)

    def nodes_forward(layer, first, last):
        for lanes in node_lanes(first, last):
            mask = col(layer, CMASK)
            summed = (mask * col(layer, EGAIN)) * k.total[layer, :, lanes] + (
                mask * col(layer, ESHIFT)
            ) * k.kept[layer, :, lanes]
            k.xs[layer, wide:, lanes] = summed.astype(BF16)
            half = dot(k.wide_w[layer], k.xs[layer, :, lanes]) + 0.5 * col(layer, NB1)
            act, slope = gate(half)
            act = act.astype(BF16)
            k.act_n[layer, :, lanes] = act
            k.slope_n[layer, :, lanes] = slope.astype(BF16)
            fourth = dot(k.small[layer, NODE_TWO], act)
            center = fourth - mean0(fourth)
            rate = lax.rsqrt(mean0(center * center) + 1e-05)
            unit = center * rate
            k.rate_n[layer, :, lanes] = rate
            k.unit_n[layer, :, lanes] = unit
            valid = live_lanes(lanes.start, CHUNK).astype(F32)
            change = valid * (unit * col(layer, NGAIN) + col(layer, NSHIFT))
            if layer == 0:
                middle = k.state[:, lanes].astype(F32) + change + k.latent[:, lanes].astype(F32)
                k.middle[:, lanes] = middle
                k.xs[1, :wide, lanes] = middle.astype(BF16)
            else:
                k.mesh_out[:, lanes] = (k.middle[:, lanes] + change).astype(BF16)

    def into(layer):
        return k.grad_latent if layer == 1 else k.grad_state

    def nodes_backward(layer, first, last):
        for lanes in node_lanes(first, last):
            valid = live_lanes(lanes.start, CHUNK).astype(F32)
            if layer == 1:
                grad = k.out_grad[:, lanes].astype(F32)
            else:
                grad = k.grad_latent[:, lanes]
            unit = k.unit_n[layer, :, lanes]
            grad_ok = valid * grad
            k.sums[layer, NGAIN] += fold(grad_ok * unit)
            k.sums[layer, NSHIFT] += fold(grad_ok)
            scaled = grad_ok * col(layer, NGAIN)
            fourth = k.rate_n[layer, :, lanes] * (
                scaled - mean0(scaled) - unit * mean0(scaled * unit)
            )
            fourth = fourth.astype(BF16)
            k.acc_64[layer, 3] += dot_nt(k.act_n[layer, :, lanes], fourth)
            third = dot(k.small[layer, NODE_TWO_B], fourth) * k.slope_n[layer, :, lanes].astype(F32)
            k.sums[layer, NB1] += fold(third)
            third = third.astype(BF16)
            k.acc_128[layer] += dot_nt(third, k.xs[layer, :, lanes])
            both = dot(k.tall_w[layer], third)
            into(layer)[:, lanes] = grad + both[:wide]
            masked = both[wide:] * col(layer, CMASK)
            k.sums[layer, EGAIN] += fold(masked * k.total[layer, :, lanes])
            k.sums[layer, ESHIFT] += fold(masked * k.kept[layer, :, lanes])
            scaled = masked * col(layer, EGAIN)
            k.scaled[:, lanes] = scaled
            k.center[:, lanes] = scaled - mean0(scaled)

    def scatter_slots(lanes, sub, hi, firsts, slots):
        spreads, hots = [], []
        for j, grad in zip(slots, firsts):
            width = grad.shape[1]
            which = jnp.broadcast_to(sub[j : j + 1].astype(jnp.int16), (16, width))
            rows = grad.reshape(wide // 16, 16, width)
            spreads.append(
                jnp.concatenate(
                    [
                        jnp.where((which == part)[None], rows, BF16(0)).reshape(wide, width)
                        for part in range(parts)
                    ],
                    axis=0,
                )
            )
            hots.append(one_hot(hi[j : j + 1], high))
        k.scatter[...] += dot_nt(join(spreads), join(hots))

    def scatter_pass(layer, first, last):
        def body(at, carry):
            lanes = pl.ds(pl.multiple_of(at * TILE_S, TILE_S), TILE_S)
            index, sub, hi = split_index(layer, lanes)
            for start in range(0, degree, GROUP_S):
                slots = range(start, start + GROUP_S)
                scatter_slots(lanes, sub, hi, [k.first[j, :, lanes] for j in slots], slots)
            return carry

        lax.fori_loop(first, last, body, 0)

    def edges_backward(layer):
        def body(at, carry):
            lanes = pl.ds(pl.multiple_of(at * TILE_B, TILE_B), TILE_B)
            index, sub, hi = split_index(layer, lanes)
            scaled, center = k.scaled[:, lanes], k.center[:, lanes]
            first_sum = jnp.zeros((wide, TILE_B), F32)
            for start in range(0, degree, GROUP_B):
                slots = range(start, start + GROUP_B)
                firsts = []
                for j in slots:
                    unit = k.unit[layer, j, :, lanes].astype(F32)
                    second = (center - unit * mean0(scaled * unit)) * k.rate_e[
                        layer, j : j + 1, lanes
                    ]
                    second = second.astype(BF16)
                    grad_one = dot(k.small[layer, SECOND_B], second) * k.slope[
                        layer, j, :, lanes
                    ].astype(F32)
                    first_sum = first_sum + grad_one
                    grad_one = grad_one.astype(BF16)
                    k.first[j, :, lanes] = grad_one
                    k.second[j, :, lanes] = second
                    firsts.append(grad_one)
                if layer == 1:
                    scatter_slots(lanes, sub, hi, firsts, slots)
            k.first_sum[:, lanes] = first_sum
            return carry

        lax.fori_loop(0, nodes // TILE_B, body, 0)

    def edge_weights(layer):
        grad_two = jnp.zeros((wide, wide), F32)
        grad_attr = jnp.zeros((wide, wide), F32)
        grad_both = jnp.zeros((wide, 2 * wide), F32)
        for j in range(degree):
            grad_two = grad_two + dot_nt(k.act[layer, j], k.second[j])
            if layer == 0:
                both = jnp.concatenate([k.senders[j], k.attr[layer, j]], axis=0)
                grad_both = grad_both + dot_nt(k.first[j], both)
            else:
                grad_attr = grad_attr + dot_nt(k.first[j], k.attr[layer, j])
        k.acc_64[layer, 2] = grad_two
        if layer == 0:
            k.acc_64[layer, 0] = grad_both[:, :wide]
            k.acc_64[layer, 1] = grad_both[:, wide:]
        else:
            k.acc_64[layer, 1] = grad_attr

    def two_terms(values):
        coarse = values.astype(BF16)
        return coarse, (values - coarse.astype(F32)).astype(BF16)

    def give_back(layer):
        back = k.small[layer, SENDER_B]
        halo_sums = [
            two_terms(k.scatter[part * wide : (part + 1) * wide, :])
            for part in range(locals_, parts)
        ]
        to_owner = join([dot(back, coarse) + dot(back, fine) for coarse, fine in halo_sums])
        to_owner = to_owner.astype(BF16)
        for way in range(4):
            k.gives[layer, way] = to_owner[:, way * halo : (way + 1) * halo]
        start_exchange(exchange(k.gives, k.backs, k.back_send, k.back_recv, layer))

    def sender_weights(layer):
        sender = jnp.zeros((wide, wide), F32)
        for part in range(parts):
            if part < locals_:
                rows = k.xs[layer, :wide, part * high : (part + 1) * high]
            else:
                first = (part - locals_) * WAYS
                rows = join([k.halos[layer, first + way] for way in range(WAYS)])
            coarse, fine = two_terms(k.scatter[part * wide : (part + 1) * wide, :])
            sender = sender + dot_nt(coarse, rows) + dot_nt(fine, rows)
        k.acc_64[layer, 0] = sender

    def share_weights(layer):
        k.sums[layer, EB1] = fold(k.first_sum[...])
        first_sum = k.first_sum[...].astype(BF16)
        receiver = dot_nt(first_sum, k.xs[layer, :wide, :])
        sender = k.acc_64[layer, 0]
        lines = exact_dot(
            jnp.ones((8, 128), F32), k.sums[layer].reshape(6 * wide, 128), ((1,), (1,))
        )
        row = lax.broadcasted_iota(jnp.int32, (8, wide), 0)
        vectors = jnp.zeros((8, wide), F32)
        for which in range(6):
            vectors = jnp.where(
                row == which, lines[:, which * wide : (which + 1) * wide], vectors
            )
        vectors = jnp.concatenate([vectors, jnp.zeros((wide - 8, wide), F32)], axis=0)
        blocks = (
            join([sender, receiver]),
            join([k.acc_64[layer, 1], k.acc_64[layer, 2]]),
            k.acc_128[layer],
            join([k.acc_64[layer, 3], vectors]),
        )
        rows = k.share.shape[2]
        for at, block in enumerate(blocks):
            for piece in range(wide // rows):
                k.share[layer, at * (wide // rows) + piece] = block[
                    piece * rows : (piece + 1) * rows, :
                ].astype(WIRE)

    def own_rows(layer):
        back = k.small[layer, SENDER_B]
        first_sum = k.first_sum[...].astype(BF16)
        for part in range(locals_):
            place = slice(part * high, (part + 1) * high)
            coarse, fine = two_terms(k.scatter[part * wide : (part + 1) * wide, :])
            into(layer)[:, place] += (
                dot(back, coarse)
                + dot(back, fine)
                + dot(k.small[layer, RECEIVER_B], first_sum[:, place])
            )

    def take_back(layer):
        finish_exchange(exchange(k.gives, k.backs, k.back_send, k.back_recv, layer))
        returned = join([k.backs[layer, way] for way in range(4)])
        into(layer)[:, :LISTED] += dot_nt(returned, k.owner[...])

    def spread_copy(layer, slot, other):
        return pltpu.make_async_remote_copy(
            src_ref=k.share.at[layer, other],
            dst_ref=k.spread.at[layer, slot],
            send_sem=k.rs_send.at[layer, other],
            recv_sem=k.rs_recv.at[layer, slot],
            device_id=member_a(other),
            device_id_type=MESH,
        )

    def swap_copy(layer, slot, other):
        return pltpu.make_async_remote_copy(
            src_ref=k.swap.at[layer, at_b],
            dst_ref=k.swap.at[layer, slot],
            send_sem=k.sw_send.at[layer, other],
            recv_sem=k.sw_recv.at[layer, slot],
            device_id=member_b(other),
            device_id_type=MESH,
        )

    def gather_copy(layer, slot, other):
        return pltpu.make_async_remote_copy(
            src_ref=k.whole.at[layer, at_a],
            dst_ref=k.whole.at[layer, slot],
            send_sem=k.ag_send.at[layer, other],
            recv_sem=k.ag_recv.at[layer, slot],
            device_id=member_a(other),
            device_id_type=MESH,
        )

    def added(blocks):
        return jnp.sum(blocks.astype(F32), axis=0).astype(WIRE)

    def spread_start(layer):
        over(size_a, at_a, lambda other: spread_copy(layer, at_a, other).start())
        k.spread[layer, at_a] = k.share[layer, at_a]

    def swap_start(layer):
        over(size_a, at_a, lambda other: spread_copy(layer, other, other).wait())
        k.swap[layer, at_b] = added(k.spread[layer])
        over(size_b, at_b, lambda other: swap_copy(layer, at_b, other).start())

    def gather_start(layer):
        over(size_b, at_b, lambda other: swap_copy(layer, other, other).wait())
        k.whole[layer, at_a] = added(k.swap[layer])
        over(size_a, at_a, lambda other: gather_copy(layer, at_a, other).start())

    def gather_end(layer):
        over(size_a, at_a, lambda other: gather_copy(layer, other, other).wait())

    fetch["lists"].wait()
    owners()
    fetch["state"].wait()
    k.xs[0, :wide, :] = k.state[...]
    pick_halos(0)
    for name in FETCHED[2:-2]:
        fetch[name].wait()
    tables()
    pl.semaphore_wait(barrier, greeted)
    send_halos(0)
    k.sums[...] = jnp.zeros_like(k.sums)
    k.acc_64[...] = jnp.zeros_like(k.acc_64)
    k.acc_128[...] = jnp.zeros_like(k.acc_128)
    k.scatter[...] = jnp.zeros_like(k.scatter)
    project(0)
    project_halos(0)
    edges_forward(0)
    fetch["latent"].wait()
    nodes_forward(0, 0, LISTED)
    pick_halos(1)
    send_halos(1)
    nodes_forward(0, LISTED, nodes)
    project(1)
    project_halos(1)
    edges_forward(1)
    fetch["out_grad"].wait()
    nodes_forward(1, 0, nodes)
    stores[0].start()
    nodes_backward(1, 0, nodes)
    edges_backward(1)
    give_back(1)
    edge_weights(1)
    sender_weights(1)
    share_weights(1)
    spread_start(1)
    own_rows(1)
    nodes_backward(0, LISTED, nodes)
    take_back(1)
    stores[1].start()
    nodes_backward(0, 0, LISTED)
    edges_backward(0)
    swap_start(1)
    edge_weights(0)
    share_weights(0)
    spread_start(0)
    gather_start(1)
    k.scatter[...] = jnp.zeros_like(k.scatter)
    steps = nodes // TILE_S
    scatter_pass(0, 0, steps // 2)
    swap_start(0)
    scatter_pass(0, steps // 2, steps)
    give_back(0)
    gather_start(0)
    own_rows(0)
    take_back(0)
    stores[2].start()
    gather_end(1)
    gather_end(0)
    stores[3].start()
    for store in stores:
        store.wait()


def finish(names, *refs):
    k = types.SimpleNamespace(**dict(zip(names, refs)))
    wide = k.g_ew2.shape[1]

    def move(at, source, target):
        return pltpu.make_async_copy(source, target, k.sem.at[at])

    ins = [
        move(0, k.reduced, k.sums),
        move(1, k.mesh_in, k.mesh),
        move(2, k.latent_in, k.latent),
        move(3, k.state_in, k.state),
    ]
    outs = [
        move(4, k.mesh, k.mesh_out),
        move(5, k.latent, k.grad_latent),
        move(6, k.state, k.grad_state),
    ]
    for step in ins:
        step.start()
    for step, then in zip(ins[1:], outs):
        step.wait()
        then.start()
    ins[0].wait()
    for layer in range(2):
        rows = k.sums.shape[2]
        pieces = wide // rows
        blocks = []
        for at in range(4):
            block = [k.sums[layer, at * pieces + piece].astype(F32) for piece in range(pieces)]
            blocks.append(block[0] if pieces == 1 else jnp.concatenate(block, axis=0))
        k.g_ew1t[layer, :, : 2 * wide] = blocks[0]
        k.g_ew1t[layer, :, 2 * wide :] = blocks[1][:, :wide]
        k.g_ew2[layer] = blocks[1][:, wide:]
        k.g_nw1t[layer] = blocks[2]
        k.g_nw2[layer] = blocks[3][:, :wide]
        for which, out in enumerate(
            (k.g_eb1, k.g_egain, k.g_eshift, k.g_nb1, k.g_ngain, k.g_nshift)
        ):
            out[layer : layer + 1, :] = blocks[3][which : which + 1, wide:]
    for then in outs:
        then.wait()


FETCHED = (
    "lists", "state", "nbr", "cmask", "ew1t", "eb1", "ew2", "egain", "eshift", "nw1t", "nb1",
    "nw2", "ngain", "nshift", "latent", "out_grad",
)
INPUTS = tuple(
    name if name == "count" else name + "_in"
    for name in (
        "state", "latent", "attr", "nbr", "lists", "count", "cmask", "ew1t", "eb1", "ew2",
        "egain", "eshift", "nw1t", "nb1", "nw2", "ngain", "nshift", "out_grad",
    )
)
OUTPUTS = (
    "mesh_out", "grad_state", "grad_latent", "g_ew1t", "g_eb1", "g_ew2", "g_egain",
    "g_eshift", "g_nw1t", "g_nb1", "g_nw2", "g_ngain", "g_nshift",
)


FIRST_OUTPUTS = ("mesh_to", "state_to", "latent_to", "reduced")
FINISH_INPUTS = ("mesh_in", "state_in", "latent_in", "reduced")
FINISH_SCRATCH = ("sums", "mesh", "latent", "state", "sem")
VMEM_BYTES = 60 * 2**20
WIRE = F32


def shards(bands, lons, *args):
    (
        node_state, latent, edge_attr, neighbours, halo_lists, valid_counts, channel_mask,
        edge_w1, edge_b1, edge_w2, edge_gain, edge_shift,
        node_w1, node_b1, node_w2, node_gain, node_shift, out_grad,
    ) = args
    nodes, wide = node_state.shape
    degree = neighbours.shape[2]
    halo = halo_lists.shape[1]
    high = WAYS * halo
    parts = nodes // high + 4 // WAYS
    size_a = lons * (2 if bands % 2 == 0 else 1)
    size_b = bands * lons // size_a
    rows = 4 * wide // size_a
    arrays = (
        node_state.T,
        latent.T,
        edge_attr.transpose(0, 2, 3, 1),
        neighbours.transpose(0, 2, 1),
        halo_lists,
        valid_counts,
        channel_mask,
        edge_w1.transpose(0, 2, 1),
        edge_b1,
        edge_w2,
        edge_gain,
        edge_shift,
        node_w1.transpose(0, 2, 1),
        node_b1,
        node_w2,
        node_gain,
        node_shift,
        out_grad.T,
    )
    shape = jax.ShapeDtypeStruct
    outs = (
        shape((wide, nodes), BF16),
        shape((wide, nodes), F32),
        shape((wide, nodes), F32),
        shape((2, wide, 3 * wide), F32),
        shape((2, wide), F32),
        shape((2, wide, wide), F32),
        shape((2, wide), F32),
        shape((2, wide), F32),
        shape((2, wide, 2 * wide), F32),
        shape((2, wide), F32),
        shape((2, wide, wide), F32),
        shape((2, wide), F32),
        shape((2, wide), F32),
    )
    sem = pltpu.SemaphoreType.DMA
    scratch = dict(
        halos=pltpu.VMEM((2, 4, wide, halo), BF16),
        backs=pltpu.VMEM((2, 4, wide, halo), BF16),
        sends=pltpu.VMEM((2, 4, wide, halo), BF16),
        gives=pltpu.VMEM((2, 4, wide, halo), BF16),
        share=pltpu.VMEM((2, size_a, rows, 128), WIRE),
        spread=pltpu.VMEM((2, size_a, rows, 128), WIRE),
        swap=pltpu.VMEM((2, size_b, rows, 128), WIRE),
        whole=pltpu.VMEM((2, size_a, rows, 128), WIRE),
        vrows=pltpu.VMEM((16, wide), F32),
        cols=pltpu.VMEM((wide, 16), F32),
        owner=pltpu.VMEM((LISTED, 4 * halo), BF16),
        small=pltpu.VMEM((2, 9, wide, wide), BF16),
        wide_w=pltpu.VMEM((2, wide, 2 * wide), BF16),
        tall_w=pltpu.VMEM((2, 2 * wide, wide), BF16),
        xs=pltpu.VMEM((2, 2 * wide, nodes), BF16),
        attr=pltpu.VMEM((2, degree, wide, nodes), BF16),
        mesh_out=pltpu.VMEM((wide, nodes), BF16),
        grad_latent=pltpu.VMEM((wide, nodes), F32),
        grad_state=pltpu.VMEM((wide, nodes), F32),
        load_sem=sem((len(FETCHED) + 2,)),
        store_sem=sem((4,)),
        pre=pltpu.VMEM((degree, wide, nodes), F32),
        senders=pltpu.VMEM((degree, wide, nodes), BF16),
        first=pltpu.VMEM((degree, wide, nodes), BF16),
        second=pltpu.VMEM((degree, wide, nodes), BF16),
        table=pltpu.VMEM((parts * wide, high), BF16),
        act=pltpu.VMEM((2, degree, wide, nodes), BF16),
        slope=pltpu.VMEM((2, degree, wide, nodes), BF16),
        unit=pltpu.VMEM((2, degree, wide, nodes), BF16),
        rate_e=pltpu.VMEM((2, degree, nodes), F32),
        total=pltpu.VMEM((2, wide, nodes), F32),
        kept=pltpu.VMEM((2, 1, nodes), F32),
        act_n=pltpu.VMEM((2, wide, nodes), BF16),
        slope_n=pltpu.VMEM((2, wide, nodes), BF16),
        rate_n=pltpu.VMEM((2, 1, nodes), F32),
        unit_n=pltpu.VMEM((2, wide, nodes), F32),
        middle=pltpu.VMEM((wide, nodes), F32),
        scaled=pltpu.VMEM((wide, nodes), F32),
        center=pltpu.VMEM((wide, nodes), F32),
        first_sum=pltpu.VMEM((wide, nodes), F32),
        scatter=pltpu.VMEM((parts * wide, high), F32),
        sums=pltpu.VMEM((2, 6, wide, 128), F32),
        acc_64=pltpu.VMEM((2, 4, wide, wide), F32),
        acc_128=pltpu.VMEM((2, wide, 2 * wide), F32),
        halo_send=sem((2, 4)),
        halo_recv=sem((2, 4)),
        back_send=sem((2, 4)),
        back_recv=sem((2, 4)),
        rs_send=sem((2, size_a)),
        rs_recv=sem((2, size_a)),
        sw_send=sem((2, size_b)),
        sw_recv=sem((2, size_b)),
        ag_send=sem((2, size_a)),
        ag_recv=sem((2, size_a)),
    )
    fetched = dict(zip(INPUTS, arrays))
    for name in FETCHED:
        array = fetched[name + "_in"]
        scratch[name] = pltpu.VMEM(array.shape, array.dtype)
    vmem = pl.BlockSpec(memory_space=pltpu.VMEM)
    anywhere = pl.BlockSpec(memory_space=pl.ANY)
    specs = [anywhere] * len(INPUTS)
    specs[INPUTS.index("count")] = pl.BlockSpec(memory_space=pltpu.SMEM)
    first_outs = outs[:3] + (shape((2, size_a, rows, 128), WIRE),)
    mids = pl.pallas_call(
        functools.partial(kernel, INPUTS + FIRST_OUTPUTS + tuple(scratch), bands, lons),
        out_shape=first_outs,
        in_specs=specs,
        out_specs=(anywhere,) * 4,
        scratch_shapes=list(scratch.values()),
        compiler_params=pltpu.CompilerParams(
            collective_id=0, has_side_effects=True, vmem_limit_bytes=VMEM_BYTES
        ),
        name="layers",
    )(*arrays)
    result = pl.pallas_call(
        functools.partial(finish, FINISH_INPUTS + OUTPUTS + FINISH_SCRATCH),
        out_shape=outs,
        in_specs=(anywhere,) * 4,
        out_specs=(anywhere,) * 3 + (vmem,) * 10,
        scratch_shapes=[
            pltpu.VMEM((2, size_a, rows, 128), WIRE),
            pltpu.VMEM((wide, nodes), BF16),
            pltpu.VMEM((wide, nodes), F32),
            pltpu.VMEM((wide, nodes), F32),
            sem((7,)),
        ],
        compiler_params=pltpu.CompilerParams(vmem_limit_bytes=VMEM_BYTES),
        name="finish",
    )(*mids)
    result = list(result)
    for at in range(3):
        result[at] = result[at].T
    for at in (3, 8):
        result[at] = result[at].transpose(0, 2, 1)
    return tuple(result)


def solution(mesh):
    nodes = P(("band", "lon"), None)
    whole = P()
    in_specs = (
        nodes,
        nodes,
        P(None, ("band", "lon"), None, None),
        P(None, ("band", "lon"), None),
        nodes,
        P(("band", "lon")),
    ) + (whole,) * 11 + (nodes,)
    return jax.shard_map(
        functools.partial(shards, mesh.shape["band"], mesh.shape["lon"]),
        mesh=mesh,
        in_specs=in_specs,
        out_specs=(nodes,) * 3 + (whole,) * 10,
        check_vma=False,
    )
```

```python
import functools
import types

import jax
import jax.numpy as jnp
from jax import lax
from jax.experimental import pallas as pl
from jax.experimental.pallas import tpu as pltpu
from jax.sharding import PartitionSpec as P

F32 = jnp.float32
BF16 = jnp.bfloat16
MESH = pl.DeviceIdType.MESH
LISTED = 1024
TILE_F, TILE_B, TILE_S = 2048, 2048, 1024
GROUP_F, GROUP_B, GROUP_S = 2, 2, 4
WAYS = 4
CHUNK = 256
EB1, EGAIN, ESHIFT, NB1, NGAIN, NSHIFT, CMASK = range(7)


def dot(left, right):
    return jnp.dot(left, right, preferred_element_type=F32)


def dot_nt(left, right):
    return lax.dot_general(left, right, (((1,), (1,)), ((), ())), preferred_element_type=F32)


def exact_dot(left, right, dims):
    return lax.dot_general(
        left, right, (dims, ((), ())), precision=lax.Precision.HIGHEST, preferred_element_type=F32
    )


def eye(size, kind):
    row = lax.broadcasted_iota(jnp.int32, (size, size), 0)
    col = lax.broadcasted_iota(jnp.int32, (size, size), 1)
    return (row == col).astype(F32).astype(kind)


def turned(matrix):
    return dot_nt(eye(matrix.shape[1], BF16), matrix).astype(BF16)


def one_hot(row, total):
    width = row.shape[1]
    index = lax.broadcasted_iota(jnp.int16, (total, width), 0)
    return jnp.where(
        index == jnp.broadcast_to(row.astype(jnp.int16), (total, width)), BF16(1), BF16(0)
    )


def join(parts):
    return parts[0] if len(parts) == 1 else jnp.concatenate(parts, axis=1)


def mean0(values):
    return jnp.mean(values, axis=0, keepdims=True)


def gate(half):
    bend = jnp.tanh(half)
    act = half + half * bend
    return act, (1.0 + bend) + act * (1.0 - bend)


def fold(values):
    total = values[:, :128]
    for at in range(128, values.shape[1], 128):
        total = total + values[:, at : at + 128]
    return total


def kernel(names, bands, lons, *refs):
    k = types.SimpleNamespace(**dict(zip(names, refs)))
    band, lon = lax.axis_index("band"), lax.axis_index("lon")
    wide, nodes = k.state.shape
    degree = k.nbr.shape[1]
    halo = k.lists.shape[1]
    high = WAYS * halo
    shift = high.bit_length() - 1
    locals_ = nodes // high
    parts = locals_ + 4 // WAYS
    count = k.count[0]
    fetch = {
        name: pltpu.make_async_copy(getattr(k, name + "_in"), getattr(k, name), k.load_sem.at[at])
        for at, name in enumerate(FETCHED)
    }
    for layer in range(2):
        fetch["attr", layer] = pltpu.make_async_copy(
            k.attr_in.at[layer], k.attr.at[layer], k.load_sem.at[len(FETCHED) + layer]
        )
    stores = [
        pltpu.make_async_copy(source, target, k.store_sem.at[at])
        for at, (source, target) in enumerate(
            (
                (k.mesh_out, k.mesh_to),
                (k.grad_latent, k.latent_to),
                (k.grad_state, k.state_to),
                (k.whole, k.reduced),
            )
        )
    ]
    west, east = lax.rem(lon + lons - 1, lons), lax.rem(lon + 1, lons)
    has_low, has_high = band > 0, band < bands - 1

    near = 2 if bands % 2 == 0 else 1
    size_a, size_b = near * lons, bands // near
    at_a = lax.rem(band, near) * lons + lon
    at_b = band // near

    def member_a(at):
        return (at_b * near + at // lons, lax.rem(at, lons))

    def member_b(at):
        return (at * near + lax.rem(band, near), lon)

    def over(size, here, act):
        def step(at, carry):
            act(lax.rem(here + at, size))
            return carry

        lax.fori_loop(1, size, step, 0)

    for use in range(2):
        for way in range(2):
            k.halos[use, way] = jnp.zeros((wide, halo), BF16)
            k.backs[use, way] = jnp.zeros((wide, halo), BF16)
    barrier = pltpu.get_barrier_semaphore()

    def greet(device):
        pl.semaphore_signal(barrier, inc=1, device_id=device, device_id_type=MESH)

    pl.when(has_low)(lambda: greet((band - 1, lon)))
    pl.when(has_high)(lambda: greet((band + 1, lon)))
    over(size_a, at_a, lambda at: greet(member_a(at)))
    over(size_b, at_b, lambda at: greet(member_b(at)))
    greeted = size_a + size_b - 2 + has_low.astype(jnp.int32) + has_high.astype(jnp.int32)
    for name in FETCHED[:2]:
        fetch[name].start()
    fetch["attr", 0].start()
    for name in FETCHED[2:]:
        fetch[name].start()
    fetch["attr", 1].start()

    def exchange(source, target, sends, recvs, use):
        def copy(block, landing, device):
            return pltpu.make_async_remote_copy(
                src_ref=source.at[use, block],
                dst_ref=target.at[use, landing],
                send_sem=sends.at[use, block],
                recv_sem=recvs.at[use, landing],
                device_id=device,
                device_id_type=MESH,
            )

        return copy

    turn = (1, 0, 3, 2)

    def targets():
        return ((band - 1, lon), (band + 1, lon), (band, west), (band, east))

    def start_exchange(copy):
        peers = targets()
        for block in range(4):
            go = copy(block, turn[block], peers[block]).start
            if block == 0:
                pl.when(has_low)(go)
            elif block == 1:
                pl.when(has_high)(go)
            else:
                go()

    def finish_exchange(copy):
        peers = targets()
        for block in range(4):
            def end(block=block):
                copy(block, block, peers[block]).wait()

            if block == 0:
                pl.when(has_low)(end)
            elif block == 1:
                pl.when(has_high)(end)
            else:
                end()

    SENDER, RECEIVER, ATTR, SECOND, NODE_TWO, SENDER_B, RECEIVER_B, SECOND_B, NODE_TWO_B = range(9)

    def col(layer, which):
        at = 2 * which + layer
        return k.cols[:, at : at + 1]

    def tables():
        for at, rows in enumerate((k.eb1, k.egain, k.eshift, k.nb1, k.ngain, k.nshift)):
            k.vrows[2 * at : 2 * at + 2, :] = rows[...]
        k.vrows[12:14, :] = k.cmask[...].astype(F32)
        k.vrows[14:16, :] = jnp.zeros((2, wide), F32)
        k.cols[...] = exact_dot(eye(wide, F32), k.vrows[...], ((1,), (1,)))

        weights = []
        for layer in range(2):
            w1t = k.ew1t[layer]
            n1t = k.nw1t[layer]
            w2 = k.ew2[layer]
            n2 = k.nw2[layer]
            half = BF16(0.5)
            weights.append(
                dict(
                    sender=w1t[:, :wide] * half,
                    receiver=w1t[:, wide : 2 * wide] * half,
                    attr=w1t[:, 2 * wide :] * half,
                    second=turned(w2),
                    node_one=n1t * half,
                    node_two=turned(n2),
                    sender_back=turned(w1t[:, :wide]),
                    receiver_back=turned(w1t[:, wide : 2 * wide]),
                    second_back=w2 * half,
                    node_one_back=turned(n1t),
                    node_two_back=n2 * half,
                )
            )
        for layer in range(2):
            for at, name in enumerate(
                (
                    "sender", "receiver", "attr", "second", "node_two",
                    "sender_back", "receiver_back", "second_back", "node_two_back",
                )
            ):
                k.small[layer, at] = weights[layer][name]
            k.wide_w[layer] = weights[layer]["node_one"]
            k.tall_w[layer] = weights[layer]["node_one_back"]

    def owners():
        for way in range(4):
            k.owner[:, way * halo : (way + 1) * halo] = one_hot(k.lists[way : way + 1, :], LISTED)

    def split_index(layer, lanes):
        index = k.nbr[layer, :, lanes]
        return index, index >> shift, index & (high - 1)

    def live_lanes(start, width):
        return lax.broadcasted_iota(jnp.int32, (1, width), 1) + start < count

    def node_lanes(first, last):
        return [pl.ds(at, CHUNK) for at in range(first, last, CHUNK)]

    def pick_halos(layer):
        picked = dot(k.xs[layer, :wide, :LISTED], k.owner[...]).astype(BF16)
        for way in range(4):
            k.sends[layer, way] = picked[:, way * halo : (way + 1) * halo]

    def send_halos(layer):
        start_exchange(exchange(k.sends, k.halos, k.halo_send, k.halo_recv, layer))

    def as_sent(layer, rows):
        return rows if layer == 0 else dot(k.small[layer, SENDER], rows).astype(BF16)

    def project(layer):
        low = k.xs[layer, :wide, :]
        own = as_sent(layer, low)
        for part in range(locals_):
            k.table[part * wide : (part + 1) * wide, :] = own[:, part * high : (part + 1) * high]
        base = dot(k.small[layer, RECEIVER], low) + 0.5 * col(layer, EB1)
        fetch["attr", layer].wait()
        for j in range(degree):
            k.pre[j] = dot(k.small[layer, ATTR], k.attr[layer, j]) + base

    def project_halos(layer):
        finish_exchange(exchange(k.sends, k.halos, k.halo_send, k.halo_recv, layer))
        for way in range(4):
            top, left = (locals_ + way // WAYS) * wide, way % WAYS * halo
            k.table[top : top + wide, left : left + halo] = as_sent(layer, k.halos[layer, way])

    def edges_forward(layer):
        def body(at, carry):
            start = pl.multiple_of(at * TILE_F, TILE_F)
            lanes = pl.ds(start, TILE_F)
            index, sub, hi = split_index(layer, lanes)
            sender_ok = jnp.where(
                index < nodes,
                (index < count).astype(F32),
                jnp.where(
                    index < nodes + halo,
                    has_low.astype(F32),
                    jnp.where(index < nodes + 2 * halo, has_high.astype(F32), 1.0),
                ),
            )
            edge_ok = sender_ok * live_lanes(start, TILE_F).astype(F32)
            total = jnp.zeros((wide, TILE_F), F32)
            for first in range(0, degree, GROUP_F):
                slots = range(first, first + GROUP_F)
                hot = join([one_hot(hi[j : j + 1], high) for j in slots])
                found = dot(k.table[...], hot)
                for place, j in enumerate(slots):
                    piece = found[:, place * TILE_F : (place + 1) * TILE_F]
                    piece = piece.reshape(parts, wide // 8, 8, TILE_F)
                    which = jnp.broadcast_to(sub[j : j + 1], (8, TILE_F))
                    chosen = piece[0]
                    for part in range(1, parts):
                        chosen = jnp.where((which == part)[None], piece[part], chosen)
                    chosen = chosen.reshape(wide, TILE_F)
                    if layer == 0:
                        chosen = chosen.astype(BF16)
                        k.senders[j, :, lanes] = chosen
                        chosen = dot(k.small[layer, SENDER], chosen)
                    act, slope = gate(chosen + k.pre[j, :, lanes])
                    act = act.astype(BF16)
                    k.act[layer, j, :, lanes] = act
                    k.slope[layer, j, :, lanes] = slope.astype(BF16)
                    second = dot(k.small[layer, SECOND], act)
                    center = second - mean0(second)
                    rate = lax.rsqrt(mean0(center * center) + 1e-05) * edge_ok[j : j + 1]
                    k.rate_e[layer, j : j + 1, lanes] = rate
                    unit = center * rate
                    k.unit[layer, j, :, lanes] = unit.astype(BF16)
                    total = total + unit
            k.total[layer, :, lanes] = total
            k.kept[layer, :, lanes] = jnp.sum(edge_ok, axis=0, keepdims=True)
            return carry

        lax.fori_loop(0, nodes // TILE_F, body, 0)

    def nodes_forward(layer, first, last):
        for lanes in node_lanes(first, last):
            mask = col(layer, CMASK)
            summed = (mask * col(layer, EGAIN)) * k.total[layer, :, lanes] + (
                mask * col(layer, ESHIFT)
            ) * k.kept[layer, :, lanes]
            k.xs[layer, wide:, lanes] = summed.astype(BF16)
            half = dot(k.wide_w[layer], k.xs[layer, :, lanes]) + 0.5 * col(layer, NB1)
            act, slope = gate(half)
            act = act.astype(BF16)
            k.act_n[layer, :, lanes] = act
            k.slope_n[layer, :, lanes] = slope.astype(BF16)
            fourth = dot(k.small[layer, NODE_TWO], act)
            center = fourth - mean0(fourth)
            rate = lax.rsqrt(mean0(center * center) + 1e-05)
            unit = center * rate
            k.rate_n[layer, :, lanes] = rate
            k.unit_n[layer, :, lanes] = unit
            valid = live_lanes(lanes.start, CHUNK).astype(F32)
            change = valid * (unit * col(layer, NGAIN) + col(layer, NSHIFT))
            if layer == 0:
                middle = k.state[:, lanes].astype(F32) + change + k.latent[:, lanes].astype(F32)
                k.middle[:, lanes] = middle
                k.xs[1, :wide, lanes] = middle.astype(BF16)
            else:
                k.mesh_out[:, lanes] = (k.middle[:, lanes] + change).astype(BF16)

    def into(layer):
        return k.grad_latent if layer == 1 else k.grad_state

    def nodes_backward(layer, first, last):
        for lanes in node_lanes(first, last):
            valid = live_lanes(lanes.start, CHUNK).astype(F32)
            if layer == 1:
                grad = k.out_grad[:, lanes].astype(F32)
            else:
                grad = k.grad_latent[:, lanes]
            unit = k.unit_n[layer, :, lanes]
            grad_ok = valid * grad
            k.sums[layer, NGAIN] += fold(grad_ok * unit)
            k.sums[layer, NSHIFT] += fold(grad_ok)
            scaled = grad_ok * col(layer, NGAIN)
            fourth = k.rate_n[layer, :, lanes] * (
                scaled - mean0(scaled) - unit * mean0(scaled * unit)
            )
            fourth = fourth.astype(BF16)
            k.acc_64[layer, 3] += dot_nt(k.act_n[layer, :, lanes], fourth)
            third = dot(k.small[layer, NODE_TWO_B], fourth) * k.slope_n[layer, :, lanes].astype(F32)
            k.sums[layer, NB1] += fold(third)
            third = third.astype(BF16)
            k.acc_128[layer] += dot_nt(third, k.xs[layer, :, lanes])
            both = dot(k.tall_w[layer], third)
            into(layer)[:, lanes] = grad + both[:wide]
            masked = both[wide:] * col(layer, CMASK)
            k.sums[layer, EGAIN] += fold(masked * k.total[layer, :, lanes])
            k.sums[layer, ESHIFT] += fold(masked * k.kept[layer, :, lanes])
            scaled = masked * col(layer, EGAIN)
            k.scaled[:, lanes] = scaled
            k.center[:, lanes] = scaled - mean0(scaled)

    def scatter_slots(lanes, sub, hi, firsts, slots):
        spreads, hots = [], []
        for j, grad in zip(slots, firsts):
            width = grad.shape[1]
            which = jnp.broadcast_to(sub[j : j + 1].astype(jnp.int16), (16, width))
            rows = grad.reshape(wide // 16, 16, width)
            spreads.append(
                jnp.concatenate(
                    [
                        jnp.where((which == part)[None], rows, BF16(0)).reshape(wide, width)
                        for part in range(parts)
                    ],
                    axis=0,
                )
            )
            hots.append(one_hot(hi[j : j + 1], high))
        k.scatter[...] += dot_nt(join(spreads), join(hots))

    def scatter_pass(layer, between):
        def body(at, carry):
            lanes = pl.ds(pl.multiple_of(at * TILE_S, TILE_S), TILE_S)
            index, sub, hi = split_index(layer, lanes)
            for start in range(0, degree, GROUP_S):
                slots = range(start, start + GROUP_S)
                scatter_slots(lanes, sub, hi, [k.first[j, :, lanes] for j in slots], slots)
            pl.when(at == 0)(between)
            return carry

        lax.fori_loop(0, nodes // TILE_S, body, 0)

    def edges_backward(layer):
        def body(at, carry):
            lanes = pl.ds(pl.multiple_of(at * TILE_B, TILE_B), TILE_B)
            index, sub, hi = split_index(layer, lanes)
            scaled, center = k.scaled[:, lanes], k.center[:, lanes]
            first_sum = jnp.zeros((wide, TILE_B), F32)
            for start in range(0, degree, GROUP_B):
                slots = range(start, start + GROUP_B)
                firsts = []
                for j in slots:
                    unit = k.unit[layer, j, :, lanes].astype(F32)
                    second = (center - unit * mean0(scaled * unit)) * k.rate_e[
                        layer, j : j + 1, lanes
                    ]
                    second = second.astype(BF16)
                    grad_one = dot(k.small[layer, SECOND_B], second) * k.slope[
                        layer, j, :, lanes
                    ].astype(F32)
                    first_sum = first_sum + grad_one
                    grad_one = grad_one.astype(BF16)
                    k.first[j, :, lanes] = grad_one
                    k.second[j, :, lanes] = second
                    firsts.append(grad_one)
                if layer == 1:
                    scatter_slots(lanes, sub, hi, firsts, slots)
            k.first_sum[:, lanes] = first_sum
            return carry

        lax.fori_loop(0, nodes // TILE_B, body, 0)

    def edge_weights(layer):
        grad_two = jnp.zeros((wide, wide), F32)
        grad_attr = jnp.zeros((wide, wide), F32)
        grad_both = jnp.zeros((wide, 2 * wide), F32)
        for j in range(degree):
            grad_two = grad_two + dot_nt(k.act[layer, j], k.second[j])
            if layer == 0:
                both = jnp.concatenate([k.senders[j], k.attr[layer, j]], axis=0)
                grad_both = grad_both + dot_nt(k.first[j], both)
            else:
                grad_attr = grad_attr + dot_nt(k.first[j], k.attr[layer, j])
        k.acc_64[layer, 2] = grad_two
        if layer == 0:
            k.acc_64[layer, 0] = grad_both[:, :wide]
            k.acc_64[layer, 1] = grad_both[:, wide:]
        else:
            k.acc_64[layer, 1] = grad_attr

    def two_terms(values):
        coarse = values.astype(BF16)
        return coarse, (values - coarse.astype(F32)).astype(BF16)

    def give_back(layer):
        back = k.small[layer, SENDER_B]
        halo_sums = [
            two_terms(k.scatter[part * wide : (part + 1) * wide, :])
            for part in range(locals_, parts)
        ]
        to_owner = join([dot(back, coarse) + dot(back, fine) for coarse, fine in halo_sums])
        to_owner = to_owner.astype(BF16)
        for way in range(4):
            k.gives[layer, way] = to_owner[:, way * halo : (way + 1) * halo]
        start_exchange(exchange(k.gives, k.backs, k.back_send, k.back_recv, layer))

    def sender_weights(layer):
        sender = jnp.zeros((wide, wide), F32)
        for part in range(parts):
            if part < locals_:
                rows = k.xs[layer, :wide, part * high : (part + 1) * high]
            else:
                first = (part - locals_) * WAYS
                rows = join([k.halos[layer, first + way] for way in range(WAYS)])
            coarse, fine = two_terms(k.scatter[part * wide : (part + 1) * wide, :])
            sender = sender + dot_nt(coarse, rows) + dot_nt(fine, rows)
        k.acc_64[layer, 0] = sender

    def share_weights(layer):
        k.sums[layer, EB1] = fold(k.first_sum[...])
        first_sum = k.first_sum[...].astype(BF16)
        receiver = dot_nt(first_sum, k.xs[layer, :wide, :])
        sender = k.acc_64[layer, 0]
        lines = exact_dot(
            jnp.ones((8, 128), F32), k.sums[layer].reshape(6 * wide, 128), ((1,), (1,))
        )
        row = lax.broadcasted_iota(jnp.int32, (8, wide), 0)
        vectors = jnp.zeros((8, wide), F32)
        for which in range(6):
            vectors = jnp.where(
                row == which, lines[:, which * wide : (which + 1) * wide], vectors
            )
        vectors = jnp.concatenate([vectors, jnp.zeros((wide - 8, wide), F32)], axis=0)
        blocks = (
            join([sender, receiver]),
            join([k.acc_64[layer, 1], k.acc_64[layer, 2]]),
            k.acc_128[layer],
            join([k.acc_64[layer, 3], vectors]),
        )
        rows = k.share.shape[2]
        for at, block in enumerate(blocks):
            for piece in range(wide // rows):
                k.share[layer, at * (wide // rows) + piece] = block[
                    piece * rows : (piece + 1) * rows, :
                ].astype(WIRE)

    def own_rows(layer):
        back = k.small[layer, SENDER_B]
        first_sum = k.first_sum[...].astype(BF16)
        for part in range(locals_):
            place = slice(part * high, (part + 1) * high)
            coarse, fine = two_terms(k.scatter[part * wide : (part + 1) * wide, :])
            into(layer)[:, place] += (
                dot(back, coarse)
                + dot(back, fine)
                + dot(k.small[layer, RECEIVER_B], first_sum[:, place])
            )

    def take_back(layer):
        finish_exchange(exchange(k.gives, k.backs, k.back_send, k.back_recv, layer))
        returned = join([k.backs[layer, way] for way in range(4)])
        into(layer)[:, :LISTED] += dot_nt(returned, k.owner[...])

    def spread_copy(layer, slot, other):
        return pltpu.make_async_remote_copy(
            src_ref=k.share.at[layer, other],
            dst_ref=k.spread.at[layer, slot],
            send_sem=k.rs_send.at[layer, other],
            recv_sem=k.rs_recv.at[layer, slot],
            device_id=member_a(other),
            device_id_type=MESH,
        )

    def swap_copy(layer, slot, other):
        return pltpu.make_async_remote_copy(
            src_ref=k.swap.at[layer, at_b],
            dst_ref=k.swap.at[layer, slot],
            send_sem=k.sw_send.at[layer, other],
            recv_sem=k.sw_recv.at[layer, slot],
            device_id=member_b(other),
            device_id_type=MESH,
        )

    def gather_copy(layer, slot, other):
        return pltpu.make_async_remote_copy(
            src_ref=k.whole.at[layer, at_a],
            dst_ref=k.whole.at[layer, slot],
            send_sem=k.ag_send.at[layer, other],
            recv_sem=k.ag_recv.at[layer, slot],
            device_id=member_a(other),
            device_id_type=MESH,
        )

    def added(blocks):
        return jnp.sum(blocks.astype(F32), axis=0).astype(WIRE)

    def spread_start(layer):
        over(size_a, at_a, lambda other: spread_copy(layer, at_a, other).start())
        k.spread[layer, at_a] = k.share[layer, at_a]

    def swap_start(layer):
        over(size_a, at_a, lambda other: spread_copy(layer, other, other).wait())
        k.swap[layer, at_b] = added(k.spread[layer])
        over(size_b, at_b, lambda other: swap_copy(layer, at_b, other).start())

    def gather_start(layer):
        over(size_b, at_b, lambda other: swap_copy(layer, other, other).wait())
        k.whole[layer, at_a] = added(k.swap[layer])
        over(size_a, at_a, lambda other: gather_copy(layer, at_a, other).start())

    def gather_end(layer):
        over(size_a, at_a, lambda other: gather_copy(layer, other, other).wait())

    fetch["lists"].wait()
    owners()
    fetch["state"].wait()
    k.xs[0, :wide, :] = k.state[...]
    pick_halos(0)
    for name in FETCHED[2:-2]:
        fetch[name].wait()
    tables()
    pl.semaphore_wait(barrier, greeted)
    send_halos(0)
    k.sums[...] = jnp.zeros_like(k.sums)
    k.acc_64[...] = jnp.zeros_like(k.acc_64)
    k.acc_128[...] = jnp.zeros_like(k.acc_128)
    k.scatter[...] = jnp.zeros_like(k.scatter)
    project(0)
    project_halos(0)
    edges_forward(0)
    fetch["latent"].wait()
    nodes_forward(0, 0, LISTED)
    pick_halos(1)
    send_halos(1)
    nodes_forward(0, LISTED, nodes)
    project(1)
    project_halos(1)
    edges_forward(1)
    fetch["out_grad"].wait()
    nodes_forward(1, 0, nodes)
    stores[0].start()
    nodes_backward(1, 0, nodes)
    edges_backward(1)
    give_back(1)
    edge_weights(1)
    sender_weights(1)
    share_weights(1)
    spread_start(1)
    own_rows(1)
    nodes_backward(0, LISTED, nodes)
    take_back(1)
    stores[1].start()
    nodes_backward(0, 0, LISTED)
    edges_backward(0)
    edge_weights(0)
    share_weights(0)
    spread_start(0)
    swap_start(1)
    k.scatter[...] = jnp.zeros_like(k.scatter)
    scatter_pass(0, lambda: swap_start(0))
    give_back(0)
    gather_start(0)
    gather_start(1)
    own_rows(0)
    take_back(0)
    stores[2].start()
    gather_end(1)
    gather_end(0)
    stores[3].start()
    for store in stores:
        store.wait()


def finish(names, *refs):
    k = types.SimpleNamespace(**dict(zip(names, refs)))
    wide = k.g_ew2.shape[1]
    k.mesh_out[...] = k.mesh_in[...]
    k.grad_state[...] = k.state_in[...]
    k.grad_latent[...] = k.latent_in[...]
    for layer in range(2):
        rows = k.reduced.shape[2]
        pieces = wide // rows
        blocks = []
        for at in range(4):
            block = [k.reduced[layer, at * pieces + piece].astype(F32) for piece in range(pieces)]
            blocks.append(block[0] if pieces == 1 else jnp.concatenate(block, axis=0))
        k.g_ew1t[layer, :, : 2 * wide] = blocks[0]
        k.g_ew1t[layer, :, 2 * wide :] = blocks[1][:, :wide]
        k.g_ew2[layer] = blocks[1][:, wide:]
        k.g_nw1t[layer] = blocks[2]
        k.g_nw2[layer] = blocks[3][:, :wide]
        for which, out in enumerate(
            (k.g_eb1, k.g_egain, k.g_eshift, k.g_nb1, k.g_ngain, k.g_nshift)
        ):
            out[layer : layer + 1, :] = blocks[3][which : which + 1, wide:]


FETCHED = (
    "lists", "state", "nbr", "cmask", "ew1t", "eb1", "ew2", "egain", "eshift", "nw1t", "nb1",
    "nw2", "ngain", "nshift", "latent", "out_grad",
)
INPUTS = tuple(
    name if name == "count" else name + "_in"
    for name in (
        "state", "latent", "attr", "nbr", "lists", "count", "cmask", "ew1t", "eb1", "ew2",
        "egain", "eshift", "nw1t", "nb1", "nw2", "ngain", "nshift", "out_grad",
    )
)
OUTPUTS = (
    "mesh_out", "grad_state", "grad_latent", "g_ew1t", "g_eb1", "g_ew2", "g_egain",
    "g_eshift", "g_nw1t", "g_nb1", "g_nw2", "g_ngain", "g_nshift",
)


FIRST_OUTPUTS = ("mesh_to", "state_to", "latent_to", "reduced")
FINISH_INPUTS = ("mesh_in", "state_in", "latent_in", "reduced")
VMEM_BYTES = 60 * 2**20
WIRE = F32


def shards(bands, lons, *args):
    (
        node_state, latent, edge_attr, neighbours, halo_lists, valid_counts, channel_mask,
        edge_w1, edge_b1, edge_w2, edge_gain, edge_shift,
        node_w1, node_b1, node_w2, node_gain, node_shift, out_grad,
    ) = args
    nodes, wide = node_state.shape
    degree = neighbours.shape[2]
    halo = halo_lists.shape[1]
    high = WAYS * halo
    parts = nodes // high + 4 // WAYS
    size_a = lons * (2 if bands % 2 == 0 else 1)
    size_b = bands * lons // size_a
    rows = 4 * wide // size_a
    arrays = (
        node_state.T,
        latent.T,
        edge_attr.transpose(0, 2, 3, 1),
        neighbours.transpose(0, 2, 1),
        halo_lists,
        valid_counts,
        channel_mask,
        edge_w1.transpose(0, 2, 1),
        edge_b1,
        edge_w2,
        edge_gain,
        edge_shift,
        node_w1.transpose(0, 2, 1),
        node_b1,
        node_w2,
        node_gain,
        node_shift,
        out_grad.T,
    )
    shape = jax.ShapeDtypeStruct
    outs = (
        shape((wide, nodes), BF16),
        shape((wide, nodes), F32),
        shape((wide, nodes), F32),
        shape((2, wide, 3 * wide), F32),
        shape((2, wide), F32),
        shape((2, wide, wide), F32),
        shape((2, wide), F32),
        shape((2, wide), F32),
        shape((2, wide, 2 * wide), F32),
        shape((2, wide), F32),
        shape((2, wide, wide), F32),
        shape((2, wide), F32),
        shape((2, wide), F32),
    )
    sem = pltpu.SemaphoreType.DMA
    scratch = dict(
        halos=pltpu.VMEM((2, 4, wide, halo), BF16),
        backs=pltpu.VMEM((2, 4, wide, halo), BF16),
        sends=pltpu.VMEM((2, 4, wide, halo), BF16),
        gives=pltpu.VMEM((2, 4, wide, halo), BF16),
        share=pltpu.VMEM((2, size_a, rows, 128), WIRE),
        spread=pltpu.VMEM((2, size_a, rows, 128), WIRE),
        swap=pltpu.VMEM((2, size_b, rows, 128), WIRE),
        whole=pltpu.VMEM((2, size_a, rows, 128), WIRE),
        vrows=pltpu.VMEM((16, wide), F32),
        cols=pltpu.VMEM((wide, 16), F32),
        owner=pltpu.VMEM((LISTED, 4 * halo), BF16),
        small=pltpu.VMEM((2, 9, wide, wide), BF16),
        wide_w=pltpu.VMEM((2, wide, 2 * wide), BF16),
        tall_w=pltpu.VMEM((2, 2 * wide, wide), BF16),
        xs=pltpu.VMEM((2, 2 * wide, nodes), BF16),
        attr=pltpu.VMEM((2, degree, wide, nodes), BF16),
        mesh_out=pltpu.VMEM((wide, nodes), BF16),
        grad_latent=pltpu.VMEM((wide, nodes), F32),
        grad_state=pltpu.VMEM((wide, nodes), F32),
        load_sem=sem((len(FETCHED) + 2,)),
        store_sem=sem((4,)),
        pre=pltpu.VMEM((degree, wide, nodes), F32),
        senders=pltpu.VMEM((degree, wide, nodes), BF16),
        first=pltpu.VMEM((degree, wide, nodes), BF16),
        second=pltpu.VMEM((degree, wide, nodes), BF16),
        table=pltpu.VMEM((parts * wide, high), BF16),
        act=pltpu.VMEM((2, degree, wide, nodes), BF16),
        slope=pltpu.VMEM((2, degree, wide, nodes), BF16),
        unit=pltpu.VMEM((2, degree, wide, nodes), BF16),
        rate_e=pltpu.VMEM((2, degree, nodes), F32),
        total=pltpu.VMEM((2, wide, nodes), F32),
        kept=pltpu.VMEM((2, 1, nodes), F32),
        act_n=pltpu.VMEM((2, wide, nodes), BF16),
        slope_n=pltpu.VMEM((2, wide, nodes), BF16),
        rate_n=pltpu.VMEM((2, 1, nodes), F32),
        unit_n=pltpu.VMEM((2, wide, nodes), F32),
        middle=pltpu.VMEM((wide, nodes), F32),
        scaled=pltpu.VMEM((wide, nodes), F32),
        center=pltpu.VMEM((wide, nodes), F32),
        first_sum=pltpu.VMEM((wide, nodes), F32),
        scatter=pltpu.VMEM((parts * wide, high), F32),
        sums=pltpu.VMEM((2, 6, wide, 128), F32),
        acc_64=pltpu.VMEM((2, 4, wide, wide), F32),
        acc_128=pltpu.VMEM((2, wide, 2 * wide), F32),
        halo_send=sem((2, 4)),
        halo_recv=sem((2, 4)),
        back_send=sem((2, 4)),
        back_recv=sem((2, 4)),
        rs_send=sem((2, size_a)),
        rs_recv=sem((2, size_a)),
        sw_send=sem((2, size_b)),
        sw_recv=sem((2, size_b)),
        ag_send=sem((2, size_a)),
        ag_recv=sem((2, size_a)),
    )
    fetched = dict(zip(INPUTS, arrays))
    for name in FETCHED:
        array = fetched[name + "_in"]
        scratch[name] = pltpu.VMEM(array.shape, array.dtype)
    vmem = pl.BlockSpec(memory_space=pltpu.VMEM)
    anywhere = pl.BlockSpec(memory_space=pl.ANY)
    specs = [anywhere] * len(INPUTS)
    specs[INPUTS.index("count")] = pl.BlockSpec(memory_space=pltpu.SMEM)
    first_outs = outs[:3] + (shape((2, size_a, rows, 128), WIRE),)
    mids = pl.pallas_call(
        functools.partial(kernel, INPUTS + FIRST_OUTPUTS + tuple(scratch), bands, lons),
        out_shape=first_outs,
        in_specs=specs,
        out_specs=(anywhere,) * 4,
        scratch_shapes=list(scratch.values()),
        compiler_params=pltpu.CompilerParams(
            collective_id=0, has_side_effects=True, vmem_limit_bytes=VMEM_BYTES
        ),
        name="layers",
    )(*arrays)
    result = pl.pallas_call(
        functools.partial(finish, FINISH_INPUTS + OUTPUTS),
        out_shape=outs,
        in_specs=(vmem,) * 4,
        out_specs=(vmem,) * 13,
        compiler_params=pltpu.CompilerParams(vmem_limit_bytes=VMEM_BYTES),
        name="finish",
    )(*mids)
    result = list(result)
    for at in range(3):
        result[at] = result[at].T
    for at in (3, 8):
        result[at] = result[at].transpose(0, 2, 1)
    return tuple(result)


def solution(mesh):
    nodes = P(("band", "lon"), None)
    whole = P()
    in_specs = (
        nodes,
        nodes,
        P(None, ("band", "lon"), None, None),
        P(None, ("band", "lon"), None),
        nodes,
        P(("band", "lon")),
    ) + (whole,) * 11 + (nodes,)
    return jax.shard_map(
        functools.partial(shards, mesh.shape["band"], mesh.shape["lon"]),
        mesh=mesh,
        in_specs=in_specs,
        out_specs=(nodes,) * 3 + (whole,) * 10,
        check_vma=False,
    )
```

```python
import functools
import types

import jax
import jax.numpy as jnp
from jax import lax
from jax.experimental import pallas as pl
from jax.experimental.pallas import tpu as pltpu
from jax.sharding import PartitionSpec as P

F32 = jnp.float32
BF16 = jnp.bfloat16
MESH = pl.DeviceIdType.MESH
LISTED = 1024
TILE_B, TILE_S = 2048, 1024
GROUP_F, GROUP_B, GROUP_S = 2, 2, 4
LOOP_P, LOOP_W = 2, 2
EARLY = 2
WAYS = 4
CHUNK = 256
EB1, EGAIN, ESHIFT, NB1, NGAIN, NSHIFT, CMASK = range(7)


def dot(left, right):
    return jnp.dot(left, right, preferred_element_type=F32)


def dot_nt(left, right):
    return lax.dot_general(left, right, (((1,), (1,)), ((), ())), preferred_element_type=F32)


def exact_dot(left, right, dims):
    return lax.dot_general(
        left, right, (dims, ((), ())), precision=lax.Precision.HIGHEST, preferred_element_type=F32
    )


def eye(size, kind):
    row = lax.broadcasted_iota(jnp.int32, (size, size), 0)
    col = lax.broadcasted_iota(jnp.int32, (size, size), 1)
    return (row == col).astype(F32).astype(kind)


def turned(matrix):
    return dot_nt(eye(matrix.shape[1], BF16), matrix).astype(BF16)


def one_hot(row, total):
    width = row.shape[1]
    index = lax.broadcasted_iota(jnp.int16, (total, width), 0)
    return jnp.where(
        index == jnp.broadcast_to(row.astype(jnp.int16), (total, width)), BF16(1), BF16(0)
    )


def join(parts):
    return parts[0] if len(parts) == 1 else jnp.concatenate(parts, axis=1)


def mean0(values):
    return jnp.mean(values, axis=0, keepdims=True)


def gate(half):
    bend = jnp.tanh(half)
    act = half + half * bend
    return act, (1.0 + bend) + act * (1.0 - bend)


def fold(values):
    total = values[:, :128]
    for at in range(128, values.shape[1], 128):
        total = total + values[:, at : at + 128]
    return total


def kernel(names, bands, lons, *refs):
    k = types.SimpleNamespace(**dict(zip(names, refs)))
    band, lon = lax.axis_index("band"), lax.axis_index("lon")
    wide, nodes = k.state.shape
    degree = k.nbr.shape[1]
    halo = k.lists.shape[1]
    high = WAYS * halo
    shift = high.bit_length() - 1
    locals_ = nodes // high
    parts = locals_ + 4 // WAYS
    count = k.count[0]
    fetch = {
        name: pltpu.make_async_copy(getattr(k, name + "_in"), getattr(k, name), k.load_sem.at[at])
        for at, name in enumerate(FETCHED)
    }
    for layer in range(2):
        fetch["attr", layer] = pltpu.make_async_copy(
            k.attr_in.at[layer], k.attr.at[layer], k.load_sem.at[len(FETCHED) + layer]
        )
    stores = [
        pltpu.make_async_copy(source, target, k.store_sem.at[at])
        for at, (source, target) in enumerate(
            (
                (k.mesh_out, k.mesh_to),
                (k.grad_latent, k.latent_to),
                (k.grad_state, k.state_to),
                (k.whole, k.reduced),
            )
        )
    ]
    west, east = lax.rem(lon + lons - 1, lons), lax.rem(lon + 1, lons)
    has_low, has_high = band > 0, band < bands - 1

    near = 2 if bands % 2 == 0 else 1
    size_a, size_b = near * lons, bands // near
    at_a = lax.rem(band, near) * lons + lon
    at_b = band // near

    def member_a(at):
        return (at_b * near + at // lons, lax.rem(at, lons))

    def member_b(at):
        return (at * near + lax.rem(band, near), lon)

    def over(size, here, act):
        def step(at, carry):
            act(lax.rem(here + at, size))
            return carry

        lax.fori_loop(1, size, step, 0)

    for use in range(2):
        for way in range(2):
            k.halos[use, way] = jnp.zeros((wide, halo), BF16)
            k.backs[use, way] = jnp.zeros((wide, halo), BF16)
    barrier = pltpu.get_barrier_semaphore()

    def greet(device):
        pl.semaphore_signal(barrier, inc=1, device_id=device, device_id_type=MESH)

    pl.when(has_low)(lambda: greet((band - 1, lon)))
    pl.when(has_high)(lambda: greet((band + 1, lon)))
    over(size_a, at_a, lambda at: greet(member_a(at)))
    over(size_b, at_b, lambda at: greet(member_b(at)))
    greeted = size_a + size_b - 2 + has_low.astype(jnp.int32) + has_high.astype(jnp.int32)
    for name in FETCHED[:2]:
        fetch[name].start()
    fetch["attr", 0].start()
    for name in FETCHED[2:]:
        fetch[name].start()
    fetch["attr", 1].start()

    def exchange(source, target, sends, recvs, use):
        def copy(block, landing, device):
            return pltpu.make_async_remote_copy(
                src_ref=source.at[use, block],
                dst_ref=target.at[use, landing],
                send_sem=sends.at[use, block],
                recv_sem=recvs.at[use, landing],
                device_id=device,
                device_id_type=MESH,
            )

        return copy

    turn = (1, 0, 3, 2)

    def targets():
        return ((band - 1, lon), (band + 1, lon), (band, west), (band, east))

    def start_exchange(copy):
        peers = targets()
        for block in range(4):
            go = copy(block, turn[block], peers[block]).start
            if block == 0:
                pl.when(has_low)(go)
            elif block == 1:
                pl.when(has_high)(go)
            else:
                go()

    def finish_exchange(copy):
        peers = targets()
        for block in range(4):
            def end(block=block):
                copy(block, block, peers[block]).wait()

            if block == 0:
                pl.when(has_low)(end)
            elif block == 1:
                pl.when(has_high)(end)
            else:
                end()

    SENDER, RECEIVER, ATTR, SECOND, NODE_TWO, SENDER_B, RECEIVER_B, SECOND_B, NODE_TWO_B = range(9)

    def col(layer, which):
        at = 2 * which + layer
        return k.cols[:, at : at + 1]

    def tables():
        for at, rows in enumerate((k.eb1, k.egain, k.eshift, k.nb1, k.ngain, k.nshift)):
            k.vrows[2 * at : 2 * at + 2, :] = rows[...]
        k.vrows[12:14, :] = k.cmask[...].astype(F32)
        k.vrows[14:16, :] = jnp.zeros((2, wide), F32)
        k.cols[...] = exact_dot(eye(wide, F32), k.vrows[...], ((1,), (1,)))

        weights = []
        for layer in range(2):
            w1t = k.ew1t[layer]
            n1t = k.nw1t[layer]
            w2 = k.ew2[layer]
            n2 = k.nw2[layer]
            half = BF16(0.5)
            weights.append(
                dict(
                    sender=w1t[:, :wide] * half,
                    receiver=w1t[:, wide : 2 * wide] * half,
                    attr=w1t[:, 2 * wide :] * half,
                    second=turned(w2),
                    node_one=n1t * half,
                    node_two=turned(n2),
                    sender_back=turned(w1t[:, :wide]),
                    receiver_back=turned(w1t[:, wide : 2 * wide]),
                    second_back=w2 * half,
                    node_one_back=turned(n1t),
                    node_two_back=n2 * half,
                )
            )
        for layer in range(2):
            for at, name in enumerate(
                (
                    "sender", "receiver", "attr", "second", "node_two",
                    "sender_back", "receiver_back", "second_back", "node_two_back",
                )
            ):
                k.small[layer, at] = weights[layer][name]
            k.wide_w[layer] = weights[layer]["node_one"]
            k.tall_w[layer] = weights[layer]["node_one_back"]

    def owners():
        for way in range(4):
            k.owner[:, way * halo : (way + 1) * halo] = one_hot(k.lists[way : way + 1, :], LISTED)

    def split_index(layer, lanes):
        index = k.nbr[layer, :, lanes]
        return index, index >> shift, index & (high - 1)

    def live_lanes(start, width):
        return lax.broadcasted_iota(jnp.int32, (1, width), 1) + start < count

    def over_nodes(first, last, act):
        for start in range(first, last, CHUNK):
            act(pl.ds(start, CHUNK))

    def pick_halos(layer):
        picked = dot(k.xs[layer, :wide, :LISTED], k.owner[...]).astype(BF16)
        for way in range(4):
            k.sends[layer, way] = picked[:, way * halo : (way + 1) * halo]

    def send_halos(layer):
        start_exchange(exchange(k.sends, k.halos, k.halo_send, k.halo_recv, layer))

    def as_sent(layer, rows):
        return rows if layer == 0 else dot(k.small[layer, SENDER], rows).astype(BF16)

    def project(layer):
        low = k.xs[layer, :wide, :]
        own = as_sent(layer, low)
        for part in range(locals_):
            k.table[part * wide : (part + 1) * wide, :] = own[:, part * high : (part + 1) * high]
        base = dot(k.small[layer, RECEIVER], low) + 0.5 * col(layer, EB1)
        fetch["attr", layer].wait()
        k.base[...] = base

        def attributes(at, carry):
            for inner in range(degree // LOOP_P):
                j = at * (degree // LOOP_P) + inner
                k.pre[j] = dot(k.small[layer, ATTR], k.attr[layer, j]) + k.base[...]
            return carry

        lax.fori_loop(0, LOOP_P, attributes, 0)

    def project_halos(layer):
        finish_exchange(exchange(k.sends, k.halos, k.halo_send, k.halo_recv, layer))
        rows = join([k.halos[layer, way] for way in range(4)])
        k.far[...] = rows.astype(F32) if layer == 0 else dot(k.small[layer, SENDER], rows)

    def own_senders(layer, first):
        slots = range(first, first + GROUP_F)
        index, sub, hi = split_index(layer, slice(None))
        found = dot(k.table[...], join([one_hot(hi[j : j + 1], high) for j in slots]))
        rows = []
        for place, j in enumerate(slots):
            piece = found[:, place * nodes : (place + 1) * nodes]
            piece = piece.reshape(locals_, wide // 8, 8, nodes)
            which = jnp.broadcast_to(sub[j : j + 1], (8, nodes))
            chosen = piece[0]
            for part in range(1, locals_):
                chosen = jnp.where((which == part)[None], piece[part], chosen)
            rows.append(chosen.reshape(wide, nodes))
        return rows

    def with_halos(layer, j, own):
        blocks = []
        for start in range(0, nodes, 128):
            index = jnp.broadcast_to(k.nbr[layer, j : j + 1, start : start + 128], (8, 128))
            lane, way = index & (halo - 1), (index - nodes) >> (halo.bit_length() - 1)
            rows = []
            for top in range(0, wide, 8):
                picked = own[top : top + 8, start : start + 128]
                for at in range(4):
                    block = k.far[top : top + 8, at * halo : (at + 1) * halo]
                    block = jnp.take_along_axis(block, lane, axis=1, mode="promise_in_bounds")
                    picked = jnp.where(way == at, block, picked)
                rows.append(picked)
            blocks.append(jnp.concatenate(rows, axis=0))
        return join(blocks)

    def edges_early(layer):
        for first in range(0, EARLY, GROUP_F):
            for place, rows in enumerate(own_senders(layer, first)):
                k.early[first + place] = rows

    def edges_forward(layer):
        index = k.nbr[layer]
        sender_ok = jnp.where(
            index < nodes,
            (index < count).astype(F32),
            jnp.where(
                index < nodes + halo,
                has_low.astype(F32),
                jnp.where(index < nodes + 2 * halo, has_high.astype(F32), 1.0),
            ),
        )
        edge_ok = sender_ok * live_lanes(0, nodes).astype(F32)
        total = jnp.zeros((wide, nodes), F32)
        for first in range(0, degree, GROUP_F):
            slots = range(first, first + GROUP_F)
            own = [k.early[j] for j in slots] if first < EARLY else own_senders(layer, first)
            for j, rows in zip(slots, own):
                chosen = with_halos(layer, j, rows)
                if layer == 0:
                    chosen = chosen.astype(BF16)
                    k.senders[j] = chosen
                    chosen = dot(k.small[layer, SENDER], chosen)
                act, slope = gate(chosen + k.pre[j])
                act = act.astype(BF16)
                k.act[layer, j] = act
                k.slope[layer, j] = slope.astype(BF16)
                second = dot(k.small[layer, SECOND], act)
                center = second - mean0(second)
                rate = lax.rsqrt(mean0(center * center) + 1e-05) * edge_ok[j : j + 1]
                k.rate_e[layer, j : j + 1, :] = rate
                unit = center * rate
                k.unit[layer, j] = unit.astype(BF16)
                total = total + unit
        k.total[layer] = total
        k.kept[layer] = jnp.sum(edge_ok, axis=0, keepdims=True)

    def nodes_forward(layer, first, last):
        def act_on(lanes):
            mask = col(layer, CMASK)
            summed = (mask * col(layer, EGAIN)) * k.total[layer, :, lanes] + (
                mask * col(layer, ESHIFT)
            ) * k.kept[layer, :, lanes]
            k.xs[layer, wide:, lanes] = summed.astype(BF16)
            half = dot(k.wide_w[layer], k.xs[layer, :, lanes]) + 0.5 * col(layer, NB1)
            act, slope = gate(half)
            act = act.astype(BF16)
            k.act_n[layer, :, lanes] = act
            k.slope_n[layer, :, lanes] = slope.astype(BF16)
            fourth = dot(k.small[layer, NODE_TWO], act)
            center = fourth - mean0(fourth)
            rate = lax.rsqrt(mean0(center * center) + 1e-05)
            unit = center * rate
            k.rate_n[layer, :, lanes] = rate
            k.unit_n[layer, :, lanes] = unit
            valid = live_lanes(lanes.start, CHUNK).astype(F32)
            change = valid * (unit * col(layer, NGAIN) + col(layer, NSHIFT))
            if layer == 0:
                middle = k.state[:, lanes].astype(F32) + change + k.latent[:, lanes].astype(F32)
                k.middle[:, lanes] = middle
                k.xs[1, :wide, lanes] = middle.astype(BF16)
            else:
                k.mesh_out[:, lanes] = (k.middle[:, lanes] + change).astype(BF16)

        over_nodes(first, last, act_on)

    def into(layer):
        return k.grad_latent if layer == 1 else k.grad_state

    def nodes_backward(layer, first, last):
        def act_on(lanes):
            valid = live_lanes(lanes.start, CHUNK).astype(F32)
            if layer == 1:
                grad = k.out_grad[:, lanes].astype(F32)
            else:
                grad = k.grad_latent[:, lanes]
            unit = k.unit_n[layer, :, lanes]
            grad_ok = valid * grad
            k.sums[layer, NGAIN] += fold(grad_ok * unit)
            k.sums[layer, NSHIFT] += fold(grad_ok)
            scaled = grad_ok * col(layer, NGAIN)
            fourth = k.rate_n[layer, :, lanes] * (
                scaled - mean0(scaled) - unit * mean0(scaled * unit)
            )
            fourth = fourth.astype(BF16)
            k.acc_64[layer, 3] += dot_nt(k.act_n[layer, :, lanes], fourth)
            third = dot(k.small[layer, NODE_TWO_B], fourth) * k.slope_n[layer, :, lanes].astype(F32)
            k.sums[layer, NB1] += fold(third)
            third = third.astype(BF16)
            k.acc_128[layer] += dot_nt(third, k.xs[layer, :, lanes])
            both = dot(k.tall_w[layer], third)
            into(layer)[:, lanes] = grad + both[:wide]
            masked = both[wide:] * col(layer, CMASK)
            k.sums[layer, EGAIN] += fold(masked * k.total[layer, :, lanes])
            k.sums[layer, ESHIFT] += fold(masked * k.kept[layer, :, lanes])
            scaled = masked * col(layer, EGAIN)
            k.scaled[:, lanes] = scaled
            k.center[:, lanes] = scaled - mean0(scaled)

        over_nodes(first, last, act_on)

    def scatter_slots(lanes, sub, hi, firsts, slots):
        spreads, hots = [], []
        for j, grad in zip(slots, firsts):
            width = grad.shape[1]
            which = jnp.broadcast_to(sub[j : j + 1].astype(jnp.int16), (16, width))
            rows = grad.reshape(wide // 16, 16, width)
            spreads.append(
                jnp.concatenate(
                    [
                        jnp.where((which == part)[None], rows, BF16(0)).reshape(wide, width)
                        for part in range(parts)
                    ],
                    axis=0,
                )
            )
            hots.append(one_hot(hi[j : j + 1], high))
        k.scatter[...] += dot_nt(join(spreads), join(hots))

    def scatter_pass(layer, between):
        def body(at, carry):
            lanes = pl.ds(pl.multiple_of(at * TILE_S, TILE_S), TILE_S)
            index, sub, hi = split_index(layer, lanes)
            for start in range(0, degree, GROUP_S):
                slots = range(start, start + GROUP_S)
                scatter_slots(lanes, sub, hi, [k.first[j, :, lanes] for j in slots], slots)
            pl.when(at == 0)(between)
            return carry

        lax.fori_loop(0, nodes // TILE_S, body, 0)

    def edges_backward(layer):
        def body(at, carry):
            lanes = pl.ds(pl.multiple_of(at * TILE_B, TILE_B), TILE_B)
            index, sub, hi = split_index(layer, lanes)
            scaled, center = k.scaled[:, lanes], k.center[:, lanes]
            first_sum = jnp.zeros((wide, TILE_B), F32)
            for start in range(0, degree, GROUP_B):
                slots = range(start, start + GROUP_B)
                firsts = []
                for j in slots:
                    unit = k.unit[layer, j, :, lanes].astype(F32)
                    second = (center - unit * mean0(scaled * unit)) * k.rate_e[
                        layer, j : j + 1, lanes
                    ]
                    second = second.astype(BF16)
                    grad_one = dot(k.small[layer, SECOND_B], second) * k.slope[
                        layer, j, :, lanes
                    ].astype(F32)
                    first_sum = first_sum + grad_one
                    grad_one = grad_one.astype(BF16)
                    k.first[j, :, lanes] = grad_one
                    k.second[j, :, lanes] = second
                    firsts.append(grad_one)
                if layer == 1:
                    scatter_slots(lanes, sub, hi, firsts, slots)
            k.first_sum[:, lanes] = first_sum
            return carry

        lax.fori_loop(0, nodes // TILE_B, body, 0)

    def edge_weights(layer):
        loops = LOOP_W if layer == 1 else 1

        def body(at, carry):
            grad_two = jnp.zeros((wide, wide), F32)
            grad_attr = jnp.zeros((wide, wide), F32)
            grad_both = jnp.zeros((wide, 2 * wide), F32)
            for inner in range(degree // loops):
                j = at * (degree // loops) + inner
                grad_two = grad_two + dot_nt(k.act[layer, j], k.second[j])
                if layer == 0:
                    both = jnp.concatenate([k.senders[j], k.attr[layer, j]], axis=0)
                    grad_both = grad_both + dot_nt(k.first[j], both)
                else:
                    grad_attr = grad_attr + dot_nt(k.first[j], k.attr[layer, j])
            k.acc_64[layer, 2] += grad_two
            if layer == 0:
                k.acc_64[layer, 0] += grad_both[:, :wide]
                k.acc_64[layer, 1] += grad_both[:, wide:]
            else:
                k.acc_64[layer, 1] += grad_attr
            return carry

        lax.fori_loop(0, loops, body, 0)

    def two_terms(values):
        coarse = values.astype(BF16)
        return coarse, (values - coarse.astype(F32)).astype(BF16)

    def give_back(layer):
        back = k.small[layer, SENDER_B]
        halo_sums = [
            two_terms(k.scatter[part * wide : (part + 1) * wide, :])
            for part in range(locals_, parts)
        ]
        to_owner = join([dot(back, coarse) + dot(back, fine) for coarse, fine in halo_sums])
        to_owner = to_owner.astype(BF16)
        for way in range(4):
            k.gives[layer, way] = to_owner[:, way * halo : (way + 1) * halo]
        start_exchange(exchange(k.gives, k.backs, k.back_send, k.back_recv, layer))

    def sender_weights(layer):
        sender = jnp.zeros((wide, wide), F32)
        for part in range(parts):
            if part < locals_:
                rows = k.xs[layer, :wide, part * high : (part + 1) * high]
            else:
                first = (part - locals_) * WAYS
                rows = join([k.halos[layer, first + way] for way in range(WAYS)])
            coarse, fine = two_terms(k.scatter[part * wide : (part + 1) * wide, :])
            sender = sender + dot_nt(coarse, rows) + dot_nt(fine, rows)
        k.acc_64[layer, 0] = sender

    def share_weights(layer):
        k.sums[layer, EB1] = fold(k.first_sum[...])
        first_sum = k.first_sum[...].astype(BF16)
        receiver = dot_nt(first_sum, k.xs[layer, :wide, :])
        sender = k.acc_64[layer, 0]
        lines = exact_dot(
            jnp.ones((8, 128), F32), k.sums[layer].reshape(6 * wide, 128), ((1,), (1,))
        )
        row = lax.broadcasted_iota(jnp.int32, (8, wide), 0)
        vectors = jnp.zeros((8, wide), F32)
        for which in range(6):
            vectors = jnp.where(
                row == which, lines[:, which * wide : (which + 1) * wide], vectors
            )
        vectors = jnp.concatenate([vectors, jnp.zeros((wide - 8, wide), F32)], axis=0)
        blocks = (
            join([sender, receiver]),
            join([k.acc_64[layer, 1], k.acc_64[layer, 2]]),
            k.acc_128[layer],
            join([k.acc_64[layer, 3], vectors]),
        )
        rows = k.share.shape[2]
        for at, block in enumerate(blocks):
            for piece in range(wide // rows):
                k.share[layer, at * (wide // rows) + piece] = block[
                    piece * rows : (piece + 1) * rows, :
                ].astype(WIRE)

    def own_rows(layer):
        back = k.small[layer, SENDER_B]
        first_sum = k.first_sum[...].astype(BF16)
        for part in range(locals_):
            place = slice(part * high, (part + 1) * high)
            coarse, fine = two_terms(k.scatter[part * wide : (part + 1) * wide, :])
            into(layer)[:, place] += (
                dot(back, coarse)
                + dot(back, fine)
                + dot(k.small[layer, RECEIVER_B], first_sum[:, place])
            )

    def take_back(layer):
        finish_exchange(exchange(k.gives, k.backs, k.back_send, k.back_recv, layer))
        returned = join([k.backs[layer, way] for way in range(4)])
        into(layer)[:, :LISTED] += dot_nt(returned, k.owner[...])

    def spread_copy(layer, slot, other):
        return pltpu.make_async_remote_copy(
            src_ref=k.share.at[layer, other],
            dst_ref=k.spread.at[layer, slot],
            send_sem=k.rs_send.at[layer, other],
            recv_sem=k.rs_recv.at[layer, slot],
            device_id=member_a(other),
            device_id_type=MESH,
        )

    def swap_copy(layer, slot, other):
        return pltpu.make_async_remote_copy(
            src_ref=k.swap.at[layer, at_b],
            dst_ref=k.swap.at[layer, slot],
            send_sem=k.sw_send.at[layer, other],
            recv_sem=k.sw_recv.at[layer, slot],
            device_id=member_b(other),
            device_id_type=MESH,
        )

    def gather_copy(layer, slot, other):
        return pltpu.make_async_remote_copy(
            src_ref=k.whole.at[layer, at_a],
            dst_ref=k.whole.at[layer, slot],
            send_sem=k.ag_send.at[layer, other],
            recv_sem=k.ag_recv.at[layer, slot],
            device_id=member_a(other),
            device_id_type=MESH,
        )

    def added(blocks):
        return jnp.sum(blocks.astype(F32), axis=0).astype(WIRE)

    def spread_start(layer):
        over(size_a, at_a, lambda other: spread_copy(layer, at_a, other).start())
        k.spread[layer, at_a] = k.share[layer, at_a]

    def swap_start(layer):
        over(size_a, at_a, lambda other: spread_copy(layer, other, other).wait())
        k.swap[layer, at_b] = added(k.spread[layer])
        over(size_b, at_b, lambda other: swap_copy(layer, at_b, other).start())

    def gather_start(layer):
        over(size_b, at_b, lambda other: swap_copy(layer, other, other).wait())
        k.whole[layer, at_a] = added(k.swap[layer])
        over(size_a, at_a, lambda other: gather_copy(layer, at_a, other).start())

    def gather_end(layer):
        over(size_a, at_a, lambda other: gather_copy(layer, other, other).wait())

    fetch["lists"].wait()
    owners()
    fetch["state"].wait()
    k.xs[0, :wide, :] = k.state[...]
    pick_halos(0)
    for name in FETCHED[2:-2]:
        fetch[name].wait()
    tables()
    pl.semaphore_wait(barrier, greeted)
    send_halos(0)
    k.sums[...] = jnp.zeros_like(k.sums)
    k.acc_64[...] = jnp.zeros_like(k.acc_64)
    k.acc_128[...] = jnp.zeros_like(k.acc_128)
    k.scatter[...] = jnp.zeros_like(k.scatter)
    project(0)
    edges_early(0)
    project_halos(0)
    edges_forward(0)
    fetch["latent"].wait()
    nodes_forward(0, 0, LISTED)
    pick_halos(1)
    send_halos(1)
    nodes_forward(0, LISTED, nodes)
    project(1)
    edges_early(1)
    project_halos(1)
    edges_forward(1)
    fetch["out_grad"].wait()
    nodes_forward(1, 0, nodes)
    stores[0].start()
    nodes_backward(1, 0, nodes)
    edges_backward(1)
    give_back(1)
    edge_weights(1)
    sender_weights(1)
    share_weights(1)
    spread_start(1)
    own_rows(1)
    nodes_backward(0, LISTED, nodes)
    take_back(1)
    stores[1].start()
    nodes_backward(0, 0, LISTED)
    edges_backward(0)
    edge_weights(0)
    share_weights(0)
    spread_start(0)
    swap_start(1)
    k.scatter[...] = jnp.zeros_like(k.scatter)
    scatter_pass(0, lambda: swap_start(0))
    give_back(0)
    gather_start(0)
    gather_start(1)
    own_rows(0)
    take_back(0)
    stores[2].start()
    gather_end(1)
    gather_end(0)
    stores[3].start()
    for store in stores:
        store.wait()


def finish(names, *refs):
    k = types.SimpleNamespace(**dict(zip(names, refs)))
    wide = k.g_ew2.shape[1]
    k.mesh_out[...] = k.mesh_in[...]
    k.grad_state[...] = k.state_in[...]
    k.grad_latent[...] = k.latent_in[...]
    for layer in range(2):
        rows = k.reduced.shape[2]
        pieces = wide // rows
        blocks = []
        for at in range(4):
            block = [k.reduced[layer, at * pieces + piece].astype(F32) for piece in range(pieces)]
            blocks.append(block[0] if pieces == 1 else jnp.concatenate(block, axis=0))
        k.g_ew1t[layer, :, : 2 * wide] = blocks[0]
        k.g_ew1t[layer, :, 2 * wide :] = blocks[1][:, :wide]
        k.g_ew2[layer] = blocks[1][:, wide:]
        k.g_nw1t[layer] = blocks[2]
        k.g_nw2[layer] = blocks[3][:, :wide]
        for which, out in enumerate(
            (k.g_eb1, k.g_egain, k.g_eshift, k.g_nb1, k.g_ngain, k.g_nshift)
        ):
            out[layer : layer + 1, :] = blocks[3][which : which + 1, wide:]


FETCHED = (
    "lists", "state", "nbr", "cmask", "ew1t", "eb1", "ew2", "egain", "eshift", "nw1t", "nb1",
    "nw2", "ngain", "nshift", "latent", "out_grad",
)
INPUTS = tuple(
    name if name == "count" else name + "_in"
    for name in (
        "state", "latent", "attr", "nbr", "lists", "count", "cmask", "ew1t", "eb1", "ew2",
        "egain", "eshift", "nw1t", "nb1", "nw2", "ngain", "nshift", "out_grad",
    )
)
OUTPUTS = (
    "mesh_out", "grad_state", "grad_latent", "g_ew1t", "g_eb1", "g_ew2", "g_egain",
    "g_eshift", "g_nw1t", "g_nb1", "g_nw2", "g_ngain", "g_nshift",
)


FIRST_OUTPUTS = ("mesh_to", "state_to", "latent_to", "reduced")
FINISH_INPUTS = ("mesh_in", "state_in", "latent_in", "reduced")
VMEM_BYTES = 60 * 2**20
WIRE = F32


def shards(bands, lons, *args):
    (
        node_state, latent, edge_attr, neighbours, halo_lists, valid_counts, channel_mask,
        edge_w1, edge_b1, edge_w2, edge_gain, edge_shift,
        node_w1, node_b1, node_w2, node_gain, node_shift, out_grad,
    ) = args
    nodes, wide = node_state.shape
    degree = neighbours.shape[2]
    halo = halo_lists.shape[1]
    high = WAYS * halo
    parts = nodes // high + 4 // WAYS
    size_a = lons * (2 if bands % 2 == 0 else 1)
    size_b = bands * lons // size_a
    rows = 4 * wide // size_a
    arrays = (
        node_state.T,
        latent.T,
        edge_attr.transpose(0, 2, 3, 1),
        neighbours.transpose(0, 2, 1),
        halo_lists,
        valid_counts,
        channel_mask,
        edge_w1.transpose(0, 2, 1),
        edge_b1,
        edge_w2,
        edge_gain,
        edge_shift,
        node_w1.transpose(0, 2, 1),
        node_b1,
        node_w2,
        node_gain,
        node_shift,
        out_grad.T,
    )
    shape = jax.ShapeDtypeStruct
    outs = (
        shape((wide, nodes), BF16),
        shape((wide, nodes), F32),
        shape((wide, nodes), F32),
        shape((2, wide, 3 * wide), F32),
        shape((2, wide), F32),
        shape((2, wide, wide), F32),
        shape((2, wide), F32),
        shape((2, wide), F32),
        shape((2, wide, 2 * wide), F32),
        shape((2, wide), F32),
        shape((2, wide, wide), F32),
        shape((2, wide), F32),
        shape((2, wide), F32),
    )
    sem = pltpu.SemaphoreType.DMA
    scratch = dict(
        halos=pltpu.VMEM((2, 4, wide, halo), BF16),
        backs=pltpu.VMEM((2, 4, wide, halo), BF16),
        sends=pltpu.VMEM((2, 4, wide, halo), BF16),
        gives=pltpu.VMEM((2, 4, wide, halo), BF16),
        share=pltpu.VMEM((2, size_a, rows, 128), WIRE),
        spread=pltpu.VMEM((2, size_a, rows, 128), WIRE),
        swap=pltpu.VMEM((2, size_b, rows, 128), WIRE),
        whole=pltpu.VMEM((2, size_a, rows, 128), WIRE),
        vrows=pltpu.VMEM((16, wide), F32),
        cols=pltpu.VMEM((wide, 16), F32),
        owner=pltpu.VMEM((LISTED, 4 * halo), BF16),
        small=pltpu.VMEM((2, 9, wide, wide), BF16),
        wide_w=pltpu.VMEM((2, wide, 2 * wide), BF16),
        tall_w=pltpu.VMEM((2, 2 * wide, wide), BF16),
        xs=pltpu.VMEM((2, 2 * wide, nodes), BF16),
        attr=pltpu.VMEM((2, degree, wide, nodes), BF16),
        mesh_out=pltpu.VMEM((wide, nodes), BF16),
        grad_latent=pltpu.VMEM((wide, nodes), F32),
        grad_state=pltpu.VMEM((wide, nodes), F32),
        load_sem=sem((len(FETCHED) + 2,)),
        store_sem=sem((4,)),
        pre=pltpu.VMEM((degree, wide, nodes), F32),
        senders=pltpu.VMEM((degree, wide, nodes), BF16),
        first=pltpu.VMEM((degree, wide, nodes), BF16),
        second=pltpu.VMEM((degree, wide, nodes), BF16),
        table=pltpu.VMEM((nodes // high * wide, high), BF16),
        far=pltpu.VMEM((wide, 4 * halo), F32),
        base=pltpu.VMEM((wide, nodes), F32),
        early=pltpu.VMEM((EARLY, wide, nodes), F32),
        act=pltpu.VMEM((2, degree, wide, nodes), BF16),
        slope=pltpu.VMEM((2, degree, wide, nodes), BF16),
        unit=pltpu.VMEM((2, degree, wide, nodes), BF16),
        rate_e=pltpu.VMEM((2, degree, nodes), F32),
        total=pltpu.VMEM((2, wide, nodes), F32),
        kept=pltpu.VMEM((2, 1, nodes), F32),
        act_n=pltpu.VMEM((2, wide, nodes), BF16),
        slope_n=pltpu.VMEM((2, wide, nodes), BF16),
        rate_n=pltpu.VMEM((2, 1, nodes), F32),
        unit_n=pltpu.VMEM((2, wide, nodes), F32),
        middle=pltpu.VMEM((wide, nodes), F32),
        scaled=pltpu.VMEM((wide, nodes), F32),
        center=pltpu.VMEM((wide, nodes), F32),
        first_sum=pltpu.VMEM((wide, nodes), F32),
        scatter=pltpu.VMEM((parts * wide, high), F32),
        sums=pltpu.VMEM((2, 6, wide, 128), F32),
        acc_64=pltpu.VMEM((2, 4, wide, wide), F32),
        acc_128=pltpu.VMEM((2, wide, 2 * wide), F32),
        halo_send=sem((2, 4)),
        halo_recv=sem((2, 4)),
        back_send=sem((2, 4)),
        back_recv=sem((2, 4)),
        rs_send=sem((2, size_a)),
        rs_recv=sem((2, size_a)),
        sw_send=sem((2, size_b)),
        sw_recv=sem((2, size_b)),
        ag_send=sem((2, size_a)),
        ag_recv=sem((2, size_a)),
    )
    fetched = dict(zip(INPUTS, arrays))
    for name in FETCHED:
        array = fetched[name + "_in"]
        scratch[name] = pltpu.VMEM(array.shape, array.dtype)
    vmem = pl.BlockSpec(memory_space=pltpu.VMEM)
    anywhere = pl.BlockSpec(memory_space=pl.ANY)
    specs = [anywhere] * len(INPUTS)
    specs[INPUTS.index("count")] = pl.BlockSpec(memory_space=pltpu.SMEM)
    first_outs = outs[:3] + (shape((2, size_a, rows, 128), WIRE),)
    mids = pl.pallas_call(
        functools.partial(kernel, INPUTS + FIRST_OUTPUTS + tuple(scratch), bands, lons),
        out_shape=first_outs,
        in_specs=specs,
        out_specs=(anywhere,) * 4,
        scratch_shapes=list(scratch.values()),
        compiler_params=pltpu.CompilerParams(
            collective_id=0, has_side_effects=True, vmem_limit_bytes=VMEM_BYTES
        ),
        name="layers",
    )(*arrays)
    result = pl.pallas_call(
        functools.partial(finish, FINISH_INPUTS + OUTPUTS),
        out_shape=outs,
        in_specs=(vmem,) * 4,
        out_specs=(vmem,) * 13,
        compiler_params=pltpu.CompilerParams(vmem_limit_bytes=VMEM_BYTES),
        name="finish",
    )(*mids)
    result = list(result)
    for at in range(3):
        result[at] = result[at].T
    for at in (3, 8):
        result[at] = result[at].transpose(0, 2, 1)
    return tuple(result)


def solution(mesh):
    nodes = P(("band", "lon"), None)
    whole = P()
    in_specs = (
        nodes,
        nodes,
        P(None, ("band", "lon"), None, None),
        P(None, ("band", "lon"), None),
        nodes,
        P(("band", "lon")),
    ) + (whole,) * 11 + (nodes,)
    return jax.shard_map(
        functools.partial(shards, mesh.shape["band"], mesh.shape["lon"]),
        mesh=mesh,
        in_specs=in_specs,
        out_specs=(nodes,) * 3 + (whole,) * 10,
        check_vma=False,
    )
```

```python
import functools
import types

import jax
import jax.numpy as jnp
from jax import lax
from jax.experimental import pallas as pl
from jax.experimental.pallas import tpu as pltpu
from jax.sharding import PartitionSpec as P

F32 = jnp.float32
BF16 = jnp.bfloat16
MESH = pl.DeviceIdType.MESH
LISTED = 1024
TILE_B, TILE_S = 2048, 1024
GROUP_F, GROUP_B, GROUP_S = 2, 2, 4
LOOP_P, LOOP_W = 2, 2
EARLY = 2
WAYS = 4
CHUNK = 256
EB1, EGAIN, ESHIFT, NB1, NGAIN, NSHIFT, CMASK = range(7)


def dot(left, right):
    return jnp.dot(left, right, preferred_element_type=F32)


def dot_nt(left, right):
    return lax.dot_general(left, right, (((1,), (1,)), ((), ())), preferred_element_type=F32)


def exact_dot(left, right, dims):
    return lax.dot_general(
        left, right, (dims, ((), ())), precision=lax.Precision.HIGHEST, preferred_element_type=F32
    )


def eye(size, kind):
    row = lax.broadcasted_iota(jnp.int32, (size, size), 0)
    col = lax.broadcasted_iota(jnp.int32, (size, size), 1)
    return (row == col).astype(F32).astype(kind)


def turned(matrix):
    return dot_nt(eye(matrix.shape[1], BF16), matrix).astype(BF16)


def one_hot(row, total):
    width = row.shape[1]
    index = lax.broadcasted_iota(jnp.int16, (total, width), 0)
    return jnp.where(
        index == jnp.broadcast_to(row.astype(jnp.int16), (total, width)), BF16(1), BF16(0)
    )


def join(parts):
    return parts[0] if len(parts) == 1 else jnp.concatenate(parts, axis=1)


def mean0(values):
    return jnp.mean(values, axis=0, keepdims=True)


def gate(half):
    bend = jnp.tanh(half)
    act = half + half * bend
    return act, (1.0 + bend) + act * (1.0 - bend)


def fold(values):
    total = values[:, :128]
    for at in range(128, values.shape[1], 128):
        total = total + values[:, at : at + 128]
    return total


def kernel(names, bands, lons, *refs):
    k = types.SimpleNamespace(**dict(zip(names, refs)))
    band, lon = lax.axis_index("band"), lax.axis_index("lon")
    wide, nodes = k.state.shape
    degree = k.nbr.shape[1]
    halo = k.lists.shape[1]
    high = WAYS * halo
    shift = high.bit_length() - 1
    locals_ = nodes // high
    parts = locals_ + 4 // WAYS
    count = k.count[0]
    fetch = {
        name: pltpu.make_async_copy(getattr(k, name + "_in"), getattr(k, name), k.load_sem.at[at])
        for at, name in enumerate(FETCHED)
    }
    for layer in range(2):
        fetch["attr", layer] = pltpu.make_async_copy(
            k.attr_in.at[layer], k.attr.at[layer], k.load_sem.at[len(FETCHED) + layer]
        )
    stores = [
        pltpu.make_async_copy(source, target, k.store_sem.at[at])
        for at, (source, target) in enumerate(
            (
                (k.mesh_out, k.mesh_to),
                (k.grad_latent, k.latent_to),
                (k.grad_state, k.state_to),
                (k.whole, k.reduced),
            )
        )
    ]
    west, east = lax.rem(lon + lons - 1, lons), lax.rem(lon + 1, lons)
    has_low, has_high = band > 0, band < bands - 1

    near = 2 if bands % 2 == 0 else 1
    size_a, size_b = near * lons, bands // near
    at_a = lax.rem(band, near) * lons + lon
    at_b = band // near

    def member_a(at):
        return (at_b * near + at // lons, lax.rem(at, lons))

    def member_b(at):
        return (at * near + lax.rem(band, near), lon)

    def over(size, here, act):
        def step(at, carry):
            act(lax.rem(here + at, size))
            return carry

        lax.fori_loop(1, size, step, 0)

    for use in range(2):
        for way in range(2):
            k.halos[use, way] = jnp.zeros((wide, halo), BF16)
            k.backs[use, way] = jnp.zeros((wide, halo), BF16)
    barrier = pltpu.get_barrier_semaphore()

    def greet(device):
        pl.semaphore_signal(barrier, inc=1, device_id=device, device_id_type=MESH)

    pl.when(has_low)(lambda: greet((band - 1, lon)))
    pl.when(has_high)(lambda: greet((band + 1, lon)))
    over(size_a, at_a, lambda at: greet(member_a(at)))
    over(size_b, at_b, lambda at: greet(member_b(at)))
    greeted = size_a + size_b - 2 + has_low.astype(jnp.int32) + has_high.astype(jnp.int32)
    for name in FETCHED[:2]:
        fetch[name].start()
    fetch["attr", 0].start()
    for name in FETCHED[2:]:
        fetch[name].start()
    fetch["attr", 1].start()

    def exchange(source, target, sends, recvs, use):
        def copy(block, landing, device):
            return pltpu.make_async_remote_copy(
                src_ref=source.at[use, block],
                dst_ref=target.at[use, landing],
                send_sem=sends.at[use, block],
                recv_sem=recvs.at[use, landing],
                device_id=device,
                device_id_type=MESH,
            )

        return copy

    turn = (1, 0, 3, 2)

    def targets():
        return ((band - 1, lon), (band + 1, lon), (band, west), (band, east))

    def start_exchange(copy):
        peers = targets()
        for block in range(4):
            go = copy(block, turn[block], peers[block]).start
            if block == 0:
                pl.when(has_low)(go)
            elif block == 1:
                pl.when(has_high)(go)
            else:
                go()

    def finish_exchange(copy):
        peers = targets()
        for block in range(4):
            def end(block=block):
                copy(block, block, peers[block]).wait()

            if block == 0:
                pl.when(has_low)(end)
            elif block == 1:
                pl.when(has_high)(end)
            else:
                end()

    SENDER, RECEIVER, ATTR, SECOND, NODE_TWO, SENDER_B, RECEIVER_B, SECOND_B, NODE_TWO_B = range(9)

    def col(layer, which):
        at = 2 * which + layer
        return k.cols[:, at : at + 1]

    def tables():
        for at, rows in enumerate((k.eb1, k.egain, k.eshift, k.nb1, k.ngain, k.nshift)):
            k.vrows[2 * at : 2 * at + 2, :] = rows[...]
        k.vrows[12:14, :] = k.cmask[...].astype(F32)
        k.vrows[14:16, :] = jnp.zeros((2, wide), F32)
        k.cols[...] = exact_dot(eye(wide, F32), k.vrows[...], ((1,), (1,)))

        weights = []
        for layer in range(2):
            w1t = k.ew1t[layer]
            n1t = k.nw1t[layer]
            w2 = k.ew2[layer]
            n2 = k.nw2[layer]
            half = BF16(0.5)
            weights.append(
                dict(
                    sender=w1t[:, :wide] * half,
                    receiver=w1t[:, wide : 2 * wide] * half,
                    attr=w1t[:, 2 * wide :] * half,
                    second=turned(w2),
                    node_one=n1t * half,
                    node_two=turned(n2),
                    sender_back=turned(w1t[:, :wide]),
                    receiver_back=turned(w1t[:, wide : 2 * wide]),
                    second_back=w2 * half,
                    node_one_back=turned(n1t),
                    node_two_back=n2 * half,
                )
            )
        for layer in range(2):
            for at, name in enumerate(
                (
                    "sender", "receiver", "attr", "second", "node_two",
                    "sender_back", "receiver_back", "second_back", "node_two_back",
                )
            ):
                k.small[layer, at] = weights[layer][name]
            k.wide_w[layer] = weights[layer]["node_one"]
            k.tall_w[layer] = weights[layer]["node_one_back"]

    def owners():
        for way in range(4):
            k.owner[:, way * halo : (way + 1) * halo] = one_hot(k.lists[way : way + 1, :], LISTED)

    def split_index(layer, lanes):
        index = k.nbr[layer, :, lanes]
        return index, index >> shift, index & (high - 1)

    def live_lanes(start, width):
        return lax.broadcasted_iota(jnp.int32, (1, width), 1) + start < count

    def over_nodes(first, last, act):
        for start in range(first, last, CHUNK):
            act(pl.ds(start, CHUNK))

    def pick_halos(layer):
        picked = dot(k.xs[layer, :wide, :LISTED], k.owner[...]).astype(BF16)
        for way in range(4):
            k.sends[layer, way] = picked[:, way * halo : (way + 1) * halo]

    def send_halos(layer):
        start_exchange(exchange(k.sends, k.halos, k.halo_send, k.halo_recv, layer))

    def as_sent(layer, rows):
        return rows if layer == 0 else dot(k.small[layer, SENDER], rows).astype(BF16)

    def project(layer):
        low = k.xs[layer, :wide, :]
        own = as_sent(layer, low)
        for part in range(locals_):
            k.table[part * wide : (part + 1) * wide, :] = own[:, part * high : (part + 1) * high]
        base = dot(k.small[layer, RECEIVER], low) + 0.5 * col(layer, EB1)
        fetch["attr", layer].wait()
        k.base[...] = base

        def attributes(at, carry):
            for inner in range(degree // LOOP_P):
                j = at * (degree // LOOP_P) + inner
                k.pre[j] = dot(k.small[layer, ATTR], k.attr[layer, j]) + k.base[...]
            return carry

        lax.fori_loop(0, LOOP_P, attributes, 0)

    def project_halos(layer):
        finish_exchange(exchange(k.sends, k.halos, k.halo_send, k.halo_recv, layer))
        rows = join([k.halos[layer, way] for way in range(4)])
        k.far[...] = rows.astype(F32) if layer == 0 else dot(k.small[layer, SENDER], rows)

    def own_senders(layer, first):
        slots = range(first, first + GROUP_F)
        index, sub, hi = split_index(layer, slice(None))
        found = dot(k.table[...], join([one_hot(hi[j : j + 1], high) for j in slots]))
        rows = []
        for place, j in enumerate(slots):
            piece = found[:, place * nodes : (place + 1) * nodes]
            piece = piece.reshape(locals_, wide // 8, 8, nodes)
            which = jnp.broadcast_to(sub[j : j + 1], (8, nodes))
            chosen = piece[0]
            for part in range(1, locals_):
                chosen = jnp.where((which == part)[None], piece[part], chosen)
            rows.append(chosen.reshape(wide, nodes))
        return rows

    def with_halos(layer, j, own):
        blocks = []
        for start in range(0, nodes, 128):
            index = jnp.broadcast_to(k.nbr[layer, j : j + 1, start : start + 128], (8, 128))
            lane, way = index & (halo - 1), (index - nodes) >> (halo.bit_length() - 1)
            rows = []
            for top in range(0, wide, 8):
                picked = own[top : top + 8, start : start + 128]
                for at in range(4):
                    block = k.far[top : top + 8, at * halo : (at + 1) * halo]
                    block = jnp.take_along_axis(block, lane, axis=1, mode="promise_in_bounds")
                    picked = jnp.where(way == at, block, picked)
                rows.append(picked)
            blocks.append(jnp.concatenate(rows, axis=0))
        return join(blocks)

    def edges_early(layer):
        for first in range(0, EARLY, GROUP_F):
            for place, rows in enumerate(own_senders(layer, first)):
                k.early[first + place] = rows

    def edges_forward(layer):
        index = k.nbr[layer]
        sender_ok = jnp.where(
            index < nodes,
            (index < count).astype(F32),
            jnp.where(
                index < nodes + halo,
                has_low.astype(F32),
                jnp.where(index < nodes + 2 * halo, has_high.astype(F32), 1.0),
            ),
        )
        edge_ok = sender_ok * live_lanes(0, nodes).astype(F32)
        total = jnp.zeros((wide, nodes), F32)
        for first in range(0, degree, GROUP_F):
            slots = range(first, first + GROUP_F)
            own = [k.early[j] for j in slots] if first < EARLY else own_senders(layer, first)
            for j, rows in zip(slots, own):
                chosen = with_halos(layer, j, rows)
                if layer == 0:
                    chosen = chosen.astype(BF16)
                    k.senders[j] = chosen
                    chosen = dot(k.small[layer, SENDER], chosen)
                act, slope = gate(chosen + k.pre[j])
                act = act.astype(BF16)
                k.act[layer, j] = act
                k.slope[layer, j] = slope.astype(BF16)
                second = dot(k.small[layer, SECOND], act)
                center = second - mean0(second)
                rate = lax.rsqrt(mean0(center * center) + 1e-05) * edge_ok[j : j + 1]
                k.rate_e[layer, j : j + 1, :] = rate
                unit = center * rate
                k.unit[layer, j] = unit.astype(BF16)
                total = total + unit
        k.total[layer] = total
        k.kept[layer] = jnp.sum(edge_ok, axis=0, keepdims=True)

    def nodes_forward(layer, first, last):
        def act_on(lanes):
            mask = col(layer, CMASK)
            summed = (mask * col(layer, EGAIN)) * k.total[layer, :, lanes] + (
                mask * col(layer, ESHIFT)
            ) * k.kept[layer, :, lanes]
            k.xs[layer, wide:, lanes] = summed.astype(BF16)
            half = dot(k.wide_w[layer], k.xs[layer, :, lanes]) + 0.5 * col(layer, NB1)
            act, slope = gate(half)
            act = act.astype(BF16)
            k.act_n[layer, :, lanes] = act
            k.slope_n[layer, :, lanes] = slope.astype(BF16)
            fourth = dot(k.small[layer, NODE_TWO], act)
            center = fourth - mean0(fourth)
            rate = lax.rsqrt(mean0(center * center) + 1e-05)
            unit = center * rate
            k.rate_n[layer, :, lanes] = rate
            k.unit_n[layer, :, lanes] = unit
            valid = live_lanes(lanes.start, CHUNK).astype(F32)
            change = valid * (unit * col(layer, NGAIN) + col(layer, NSHIFT))
            if layer == 0:
                middle = k.state[:, lanes].astype(F32) + change + k.latent[:, lanes].astype(F32)
                k.middle[:, lanes] = middle
                k.xs[1, :wide, lanes] = middle.astype(BF16)
            else:
                k.mesh_out[:, lanes] = (k.middle[:, lanes] + change).astype(BF16)

        over_nodes(first, last, act_on)

    def into(layer):
        return k.grad_latent if layer == 1 else k.grad_state

    def nodes_backward(layer, first, last):
        def act_on(lanes):
            valid = live_lanes(lanes.start, CHUNK).astype(F32)
            if layer == 1:
                grad = k.out_grad[:, lanes].astype(F32)
            else:
                grad = k.grad_latent[:, lanes]
            unit = k.unit_n[layer, :, lanes]
            grad_ok = valid * grad
            k.sums[layer, NGAIN] += fold(grad_ok * unit)
            k.sums[layer, NSHIFT] += fold(grad_ok)
            scaled = grad_ok * col(layer, NGAIN)
            fourth = k.rate_n[layer, :, lanes] * (
                scaled - mean0(scaled) - unit * mean0(scaled * unit)
            )
            fourth = fourth.astype(BF16)
            k.acc_64[layer, 3] += dot_nt(k.act_n[layer, :, lanes], fourth)
            third = dot(k.small[layer, NODE_TWO_B], fourth) * k.slope_n[layer, :, lanes].astype(F32)
            k.sums[layer, NB1] += fold(third)
            third = third.astype(BF16)
            k.acc_128[layer] += dot_nt(third, k.xs[layer, :, lanes])
            both = dot(k.tall_w[layer], third)
            into(layer)[:, lanes] = grad + both[:wide]
            masked = both[wide:] * col(layer, CMASK)
            k.sums[layer, EGAIN] += fold(masked * k.total[layer, :, lanes])
            k.sums[layer, ESHIFT] += fold(masked * k.kept[layer, :, lanes])
            scaled = masked * col(layer, EGAIN)
            k.scaled[:, lanes] = scaled
            k.center[:, lanes] = scaled - mean0(scaled)

        over_nodes(first, last, act_on)

    def scatter_slots(lanes, sub, hi, firsts, slots):
        spreads, hots = [], []
        for j, grad in zip(slots, firsts):
            width = grad.shape[1]
            which = jnp.broadcast_to(sub[j : j + 1].astype(jnp.int16), (16, width))
            rows = grad.reshape(wide // 16, 16, width)
            spreads.append(
                jnp.concatenate(
                    [
                        jnp.where((which == part)[None], rows, BF16(0)).reshape(wide, width)
                        for part in range(parts)
                    ],
                    axis=0,
                )
            )
            hots.append(one_hot(hi[j : j + 1], high))
        k.scatter[...] += dot_nt(join(spreads), join(hots))

    def scatter_pass(layer, between):
        def body(at, carry):
            lanes = pl.ds(pl.multiple_of(at * TILE_S, TILE_S), TILE_S)
            index, sub, hi = split_index(layer, lanes)
            for start in range(0, degree, GROUP_S):
                slots = range(start, start + GROUP_S)
                scatter_slots(lanes, sub, hi, [k.first[j, :, lanes] for j in slots], slots)
            pl.when(at == 0)(between)
            return carry

        lax.fori_loop(0, nodes // TILE_S, body, 0)

    def edges_backward(layer):
        def body(at, carry):
            lanes = pl.ds(pl.multiple_of(at * TILE_B, TILE_B), TILE_B)
            index, sub, hi = split_index(layer, lanes)
            scaled, center = k.scaled[:, lanes], k.center[:, lanes]
            first_sum = jnp.zeros((wide, TILE_B), F32)
            for start in range(0, degree, GROUP_B):
                slots = range(start, start + GROUP_B)
                firsts = []
                for j in slots:
                    unit = k.unit[layer, j, :, lanes].astype(F32)
                    second = (center - unit * mean0(scaled * unit)) * k.rate_e[
                        layer, j : j + 1, lanes
                    ]
                    second = second.astype(BF16)
                    grad_one = dot(k.small[layer, SECOND_B], second) * k.slope[
                        layer, j, :, lanes
                    ].astype(F32)
                    first_sum = first_sum + grad_one
                    grad_one = grad_one.astype(BF16)
                    k.first[j, :, lanes] = grad_one
                    k.second[j, :, lanes] = second
                    firsts.append(grad_one)
                if layer == 1:
                    scatter_slots(lanes, sub, hi, firsts, slots)
            k.first_sum[:, lanes] = first_sum
            return carry

        lax.fori_loop(0, nodes // TILE_B, body, 0)

    def edge_weights(layer):
        loops = LOOP_W if layer == 1 else 1

        def body(at, carry):
            grad_two = jnp.zeros((wide, wide), F32)
            grad_attr = jnp.zeros((wide, wide), F32)
            grad_both = jnp.zeros((wide, 2 * wide), F32)
            for inner in range(degree // loops):
                j = at * (degree // loops) + inner
                grad_two = grad_two + dot_nt(k.act[layer, j], k.second[j])
                if layer == 0:
                    both = jnp.concatenate([k.senders[j], k.attr[layer, j]], axis=0)
                    grad_both = grad_both + dot_nt(k.first[j], both)
                else:
                    grad_attr = grad_attr + dot_nt(k.first[j], k.attr[layer, j])
            k.acc_64[layer, 2] += grad_two
            if layer == 0:
                k.acc_64[layer, 0] += grad_both[:, :wide]
                k.acc_64[layer, 1] += grad_both[:, wide:]
            else:
                k.acc_64[layer, 1] += grad_attr
            return carry

        lax.fori_loop(0, loops, body, 0)

    def two_terms(values):
        coarse = values.astype(BF16)
        return coarse, (values - coarse.astype(F32)).astype(BF16)

    def give_back(layer):
        back = k.small[layer, SENDER_B]
        halo_sums = [
            two_terms(k.scatter[part * wide : (part + 1) * wide, :])
            for part in range(locals_, parts)
        ]
        to_owner = join([dot(back, coarse) + dot(back, fine) for coarse, fine in halo_sums])
        to_owner = to_owner.astype(BF16)
        for way in range(4):
            k.gives[layer, way] = to_owner[:, way * halo : (way + 1) * halo]
        start_exchange(exchange(k.gives, k.backs, k.back_send, k.back_recv, layer))

    def sender_weights(layer):
        sender = jnp.zeros((wide, wide), F32)
        for part in range(parts):
            if part < locals_:
                rows = k.xs[layer, :wide, part * high : (part + 1) * high]
            else:
                first = (part - locals_) * WAYS
                rows = join([k.halos[layer, first + way] for way in range(WAYS)])
            coarse, fine = two_terms(k.scatter[part * wide : (part + 1) * wide, :])
            sender = sender + dot_nt(coarse, rows) + dot_nt(fine, rows)
        k.acc_64[layer, 0] = sender

    def share_weights(layer):
        k.sums[layer, EB1] = fold(k.first_sum[...])
        first_sum = k.first_sum[...].astype(BF16)
        receiver = dot_nt(first_sum, k.xs[layer, :wide, :])
        sender = k.acc_64[layer, 0]
        lines = exact_dot(
            jnp.ones((8, 128), F32), k.sums[layer].reshape(6 * wide, 128), ((1,), (1,))
        )
        row = lax.broadcasted_iota(jnp.int32, (8, wide), 0)
        vectors = jnp.zeros((8, wide), F32)
        for which in range(6):
            vectors = jnp.where(
                row == which, lines[:, which * wide : (which + 1) * wide], vectors
            )
        vectors = jnp.concatenate([vectors, jnp.zeros((wide - 8, wide), F32)], axis=0)
        blocks = (
            join([sender, receiver]),
            join([k.acc_64[layer, 1], k.acc_64[layer, 2]]),
            k.acc_128[layer],
            join([k.acc_64[layer, 3], vectors]),
        )
        rows = k.share.shape[2]
        for at, block in enumerate(blocks):
            for piece in range(wide // rows):
                k.share[at * (wide // rows) + piece, layer] = block[
                    piece * rows : (piece + 1) * rows, :
                ].astype(WIRE)

    def own_rows(layer):
        back = k.small[layer, SENDER_B]
        first_sum = k.first_sum[...].astype(BF16)
        for part in range(locals_):
            place = slice(part * high, (part + 1) * high)
            coarse, fine = two_terms(k.scatter[part * wide : (part + 1) * wide, :])
            into(layer)[:, place] += (
                dot(back, coarse)
                + dot(back, fine)
                + dot(k.small[layer, RECEIVER_B], first_sum[:, place])
            )

    def take_back(layer):
        finish_exchange(exchange(k.gives, k.backs, k.back_send, k.back_recv, layer))
        returned = join([k.backs[layer, way] for way in range(4)])
        into(layer)[:, :LISTED] += dot_nt(returned, k.owner[...])

    def group_copy(source, piece, target, slot, sends, recvs, other, device):
        return pltpu.make_async_remote_copy(
            src_ref=source.at[piece],
            dst_ref=target.at[slot],
            send_sem=sends.at[other],
            recv_sem=recvs.at[slot],
            device_id=device,
            device_id_type=MESH,
        )

    def spread_copy(slot, other):
        return group_copy(
            k.share, other, k.spread, slot, k.rs_send, k.rs_recv, other, member_a(other)
        )

    def swap_copy(slot, other):
        return group_copy(k.swap, at_b, k.swap, slot, k.sw_send, k.sw_recv, other, member_b(other))

    def gather_copy(slot, other):
        return group_copy(
            k.whole, at_a, k.whole, slot, k.ag_send, k.ag_recv, other, member_a(other)
        )

    def added(blocks):
        return jnp.sum(blocks.astype(F32), axis=0).astype(WIRE)

    def spread_start():
        over(size_a, at_a, lambda other: spread_copy(at_a, other).start())
        k.spread[at_a] = k.share[at_a]

    def swap_start():
        over(size_a, at_a, lambda other: spread_copy(other, other).wait())
        k.swap[at_b] = added(k.spread[...])
        over(size_b, at_b, lambda other: swap_copy(at_b, other).start())

    def gather_start():
        over(size_b, at_b, lambda other: swap_copy(other, other).wait())
        k.whole[at_a] = added(k.swap[...])
        over(size_a, at_a, lambda other: gather_copy(at_a, other).start())

    def gather_end():
        over(size_a, at_a, lambda other: gather_copy(other, other).wait())

    fetch["lists"].wait()
    owners()
    fetch["state"].wait()
    k.xs[0, :wide, :] = k.state[...]
    pick_halos(0)
    for name in FETCHED[2:-2]:
        fetch[name].wait()
    tables()
    pl.semaphore_wait(barrier, greeted)
    send_halos(0)
    k.sums[...] = jnp.zeros_like(k.sums)
    k.acc_64[...] = jnp.zeros_like(k.acc_64)
    k.acc_128[...] = jnp.zeros_like(k.acc_128)
    k.scatter[...] = jnp.zeros_like(k.scatter)
    project(0)
    edges_early(0)
    project_halos(0)
    edges_forward(0)
    fetch["latent"].wait()
    nodes_forward(0, 0, LISTED)
    pick_halos(1)
    send_halos(1)
    nodes_forward(0, LISTED, nodes)
    project(1)
    edges_early(1)
    project_halos(1)
    edges_forward(1)
    fetch["out_grad"].wait()
    nodes_forward(1, 0, nodes)
    stores[0].start()
    nodes_backward(1, 0, nodes)
    edges_backward(1)
    give_back(1)
    edge_weights(1)
    sender_weights(1)
    share_weights(1)
    own_rows(1)
    nodes_backward(0, LISTED, nodes)
    take_back(1)
    stores[1].start()
    nodes_backward(0, 0, LISTED)
    edges_backward(0)
    edge_weights(0)
    share_weights(0)
    spread_start()
    k.scatter[...] = jnp.zeros_like(k.scatter)
    scatter_pass(0, lambda: swap_start())
    give_back(0)
    gather_start()
    own_rows(0)
    take_back(0)
    stores[2].start()
    gather_end()
    stores[3].start()
    for store in stores:
        store.wait()


def finish(names, *refs):
    k = types.SimpleNamespace(**dict(zip(names, refs)))
    wide = k.g_ew2.shape[1]
    k.mesh_out[...] = k.mesh_in[...]
    k.grad_state[...] = k.state_in[...]
    k.grad_latent[...] = k.latent_in[...]
    for layer in range(2):
        rows = k.reduced.shape[2]
        pieces = wide // rows
        blocks = []
        for at in range(4):
            block = [k.reduced[at * pieces + piece, layer].astype(F32) for piece in range(pieces)]
            blocks.append(block[0] if pieces == 1 else jnp.concatenate(block, axis=0))
        k.g_ew1t[layer, :, : 2 * wide] = blocks[0]
        k.g_ew1t[layer, :, 2 * wide :] = blocks[1][:, :wide]
        k.g_ew2[layer] = blocks[1][:, wide:]
        k.g_nw1t[layer] = blocks[2]
        k.g_nw2[layer] = blocks[3][:, :wide]
        for which, out in enumerate(
            (k.g_eb1, k.g_egain, k.g_eshift, k.g_nb1, k.g_ngain, k.g_nshift)
        ):
            out[layer : layer + 1, :] = blocks[3][which : which + 1, wide:]


FETCHED = (
    "lists", "state", "nbr", "cmask", "ew1t", "eb1", "ew2", "egain", "eshift", "nw1t", "nb1",
    "nw2", "ngain", "nshift", "latent", "out_grad",
)
INPUTS = tuple(
    name if name == "count" else name + "_in"
    for name in (
        "state", "latent", "attr", "nbr", "lists", "count", "cmask", "ew1t", "eb1", "ew2",
        "egain", "eshift", "nw1t", "nb1", "nw2", "ngain", "nshift", "out_grad",
    )
)
OUTPUTS = (
    "mesh_out", "grad_state", "grad_latent", "g_ew1t", "g_eb1", "g_ew2", "g_egain",
    "g_eshift", "g_nw1t", "g_nb1", "g_nw2", "g_ngain", "g_nshift",
)


FIRST_OUTPUTS = ("mesh_to", "state_to", "latent_to", "reduced")
FINISH_INPUTS = ("mesh_in", "state_in", "latent_in", "reduced")
VMEM_BYTES = 60 * 2**20
WIRE = BF16


def shards(bands, lons, *args):
    (
        node_state, latent, edge_attr, neighbours, halo_lists, valid_counts, channel_mask,
        edge_w1, edge_b1, edge_w2, edge_gain, edge_shift,
        node_w1, node_b1, node_w2, node_gain, node_shift, out_grad,
    ) = args
    nodes, wide = node_state.shape
    degree = neighbours.shape[2]
    halo = halo_lists.shape[1]
    high = WAYS * halo
    parts = nodes // high + 4 // WAYS
    size_a = lons * (2 if bands % 2 == 0 else 1)
    size_b = bands * lons // size_a
    rows = 4 * wide // size_a
    arrays = (
        node_state.T,
        latent.T,
        edge_attr.transpose(0, 2, 3, 1),
        neighbours.transpose(0, 2, 1),
        halo_lists,
        valid_counts,
        channel_mask,
        edge_w1.transpose(0, 2, 1),
        edge_b1,
        edge_w2,
        edge_gain,
        edge_shift,
        node_w1.transpose(0, 2, 1),
        node_b1,
        node_w2,
        node_gain,
        node_shift,
        out_grad.T,
    )
    shape = jax.ShapeDtypeStruct
    outs = (
        shape((wide, nodes), BF16),
        shape((wide, nodes), F32),
        shape((wide, nodes), F32),
        shape((2, wide, 3 * wide), F32),
        shape((2, wide), F32),
        shape((2, wide, wide), F32),
        shape((2, wide), F32),
        shape((2, wide), F32),
        shape((2, wide, 2 * wide), F32),
        shape((2, wide), F32),
        shape((2, wide, wide), F32),
        shape((2, wide), F32),
        shape((2, wide), F32),
    )
    sem = pltpu.SemaphoreType.DMA
    scratch = dict(
        halos=pltpu.VMEM((2, 4, wide, halo), BF16),
        backs=pltpu.VMEM((2, 4, wide, halo), BF16),
        sends=pltpu.VMEM((2, 4, wide, halo), BF16),
        gives=pltpu.VMEM((2, 4, wide, halo), BF16),
        share=pltpu.VMEM((size_a, 2, rows, 128), WIRE),
        spread=pltpu.VMEM((size_a, 2, rows, 128), WIRE),
        swap=pltpu.VMEM((size_b, 2, rows, 128), WIRE),
        whole=pltpu.VMEM((size_a, 2, rows, 128), WIRE),
        vrows=pltpu.VMEM((16, wide), F32),
        cols=pltpu.VMEM((wide, 16), F32),
        owner=pltpu.VMEM((LISTED, 4 * halo), BF16),
        small=pltpu.VMEM((2, 9, wide, wide), BF16),
        wide_w=pltpu.VMEM((2, wide, 2 * wide), BF16),
        tall_w=pltpu.VMEM((2, 2 * wide, wide), BF16),
        xs=pltpu.VMEM((2, 2 * wide, nodes), BF16),
        attr=pltpu.VMEM((2, degree, wide, nodes), BF16),
        mesh_out=pltpu.VMEM((wide, nodes), BF16),
        grad_latent=pltpu.VMEM((wide, nodes), F32),
        grad_state=pltpu.VMEM((wide, nodes), F32),
        load_sem=sem((len(FETCHED) + 2,)),
        store_sem=sem((4,)),
        pre=pltpu.VMEM((degree, wide, nodes), F32),
        senders=pltpu.VMEM((degree, wide, nodes), BF16),
        first=pltpu.VMEM((degree, wide, nodes), BF16),
        second=pltpu.VMEM((degree, wide, nodes), BF16),
        table=pltpu.VMEM((nodes // high * wide, high), BF16),
        far=pltpu.VMEM((wide, 4 * halo), F32),
        base=pltpu.VMEM((wide, nodes), F32),
        early=pltpu.VMEM((EARLY, wide, nodes), F32),
        act=pltpu.VMEM((2, degree, wide, nodes), BF16),
        slope=pltpu.VMEM((2, degree, wide, nodes), BF16),
        unit=pltpu.VMEM((2, degree, wide, nodes), BF16),
        rate_e=pltpu.VMEM((2, degree, nodes), F32),
        total=pltpu.VMEM((2, wide, nodes), F32),
        kept=pltpu.VMEM((2, 1, nodes), F32),
        act_n=pltpu.VMEM((2, wide, nodes), BF16),
        slope_n=pltpu.VMEM((2, wide, nodes), BF16),
        rate_n=pltpu.VMEM((2, 1, nodes), F32),
        unit_n=pltpu.VMEM((2, wide, nodes), F32),
        middle=pltpu.VMEM((wide, nodes), F32),
        scaled=pltpu.VMEM((wide, nodes), F32),
        center=pltpu.VMEM((wide, nodes), F32),
        first_sum=pltpu.VMEM((wide, nodes), F32),
        scatter=pltpu.VMEM((parts * wide, high), F32),
        sums=pltpu.VMEM((2, 6, wide, 128), F32),
        acc_64=pltpu.VMEM((2, 4, wide, wide), F32),
        acc_128=pltpu.VMEM((2, wide, 2 * wide), F32),
        halo_send=sem((2, 4)),
        halo_recv=sem((2, 4)),
        back_send=sem((2, 4)),
        back_recv=sem((2, 4)),
        rs_send=sem((size_a,)),
        rs_recv=sem((size_a,)),
        sw_send=sem((size_b,)),
        sw_recv=sem((size_b,)),
        ag_send=sem((size_a,)),
        ag_recv=sem((size_a,)),
    )
    fetched = dict(zip(INPUTS, arrays))
    for name in FETCHED:
        array = fetched[name + "_in"]
        scratch[name] = pltpu.VMEM(array.shape, array.dtype)
    vmem = pl.BlockSpec(memory_space=pltpu.VMEM)
    anywhere = pl.BlockSpec(memory_space=pl.ANY)
    specs = [anywhere] * len(INPUTS)
    specs[INPUTS.index("count")] = pl.BlockSpec(memory_space=pltpu.SMEM)
    first_outs = outs[:3] + (shape((size_a, 2, rows, 128), WIRE),)
    mids = pl.pallas_call(
        functools.partial(kernel, INPUTS + FIRST_OUTPUTS + tuple(scratch), bands, lons),
        out_shape=first_outs,
        in_specs=specs,
        out_specs=(anywhere,) * 4,
        scratch_shapes=list(scratch.values()),
        compiler_params=pltpu.CompilerParams(
            collective_id=0, has_side_effects=True, vmem_limit_bytes=VMEM_BYTES
        ),
        name="layers",
    )(*arrays)
    result = pl.pallas_call(
        functools.partial(finish, FINISH_INPUTS + OUTPUTS),
        out_shape=outs,
        in_specs=(vmem,) * 4,
        out_specs=(vmem,) * 13,
        compiler_params=pltpu.CompilerParams(vmem_limit_bytes=VMEM_BYTES),
        name="finish",
    )(*mids)
    result = list(result)
    for at in range(3):
        result[at] = result[at].T
    for at in (3, 8):
        result[at] = result[at].transpose(0, 2, 1)
    return tuple(result)


def solution(mesh):
    nodes = P(("band", "lon"), None)
    whole = P()
    in_specs = (
        nodes,
        nodes,
        P(None, ("band", "lon"), None, None),
        P(None, ("band", "lon"), None),
        nodes,
        P(("band", "lon")),
    ) + (whole,) * 11 + (nodes,)
    return jax.shard_map(
        functools.partial(shards, mesh.shape["band"], mesh.shape["lon"]),
        mesh=mesh,
        in_specs=in_specs,
        out_specs=(nodes,) * 3 + (whole,) * 10,
        check_vma=False,
    )
```
